32 devices in a mesh: runs: 2 (over x), blocks: 16 (over z, y, core).
Axes of the slice: x: 2, y: 2, z: 4, core: 2. Of those that a mesh axis runs over, the one named last changes fastest.
Arguments:
- centroid: float32 [3, 32768], P(None, ('runs', 'blocks')), parts along dimension 1, may hold values from -1 to 4
- angles: float32 [2, 32768], P(None, ('runs', 'blocks')), parts along dimension 1, may hold values from -1 to 2
- size: float32 [32768], P(('runs', 'blocks')), parts along dimension 0, may hold values from 0.001 to 0.004
- slip_rate: float32 [32768], P(('runs', 'blocks')), parts along dimension 0, may hold values from -1 to 3
- live_count: int32 [32], P(('runs', 'blocks')), parts along dimension 0, may hold values from 1 to 1024, 12288 in all
- near: int32 [32, 16], P(('runs', 'blocks')), parts along dimension 0, may hold values from 0 to 1, as said below
Outputs:
- shear_rate: float32 [32768], P(('runs', 'blocks')), parts along dimension 0
- normal_rate: float32 [32768], P(('runs', 'blocks')), parts along dimension 0
The draws below stay inside these ranges and needn't reach their ends.
There are 2 independent parts, one for each index of `runs`. The reference program is written for one: setup_inputs(seed, part) draws one part's arguments, and reference() takes and returns one part's arrays. A program takes and returns all parts, laid end to end along the dimension named above; each array names one. Nothing has to cross between parts.
Inputs may be any that keep to these rules, and one draw needn't show every extreme that they name: `live_count`: the blocks' counts sum to 12288; some block is full. `near`: Symmetric, with ones on the diagonal; an entry off the diagonal is 1 only where the two blocks' numbers, taken modulo half of 16, differ by at most one.
All inputs are finite; a program needn't handle non-finite values.
Results may differ from the reference program's by a relative error of at most 0.0003.
Values sent between devices are 32-bit elements; how exact they have to be, the bound alone decides.
No kernel may reach another device: no remote copies, remote signals or barrier semaphores. Data moves between devices by JAX's collectives and lax.ppermute only.
A program may use at most 64 MiB of HBM per device.

```python
import math
import jax
import jax.numpy as jnp
import numpy as np
from jax import lax

E_DEV = 1024
FAULT_BLOCKS = 16
ELEMS = 16384
LIVE_TOTAL = 12288


slot_area = 4e-06


depth_extent = 0.016


strand_gap = 0.03


def block_frames(key):
    strands = FAULT_BLOCKS // 2
    length = E_DEV * slot_area / depth_extent
    strand_turn = jax.random.uniform(jax.random.fold_in(key, 101), (strands,), jnp.float32, -0.1, 0.1)
    bend = jax.random.uniform(jax.random.fold_in(key, 102), (2, strands), jnp.float32, -0.08, 0.08)
    strike = strand_turn[None, :] + bend
    dip_angle = jax.random.uniform(jax.random.fold_in(key, 103), (2, strands), jnp.float32, 1.1, 1.5707964)
    shift_x = jax.random.uniform(jax.random.fold_in(key, 104), (strands,), jnp.float32, 0.0, 0.25) * length
    jitter_y = jax.random.uniform(jax.random.fold_in(key, 105), (strands,), jnp.float32, -0.2, 0.2)
    shift_y = (jnp.arange(strands, dtype=jnp.float32) + jitter_y) * strand_gap
    zeros = jnp.zeros((strands,), jnp.float32)
    first_anchor = jnp.stack([shift_x, shift_y, zeros])
    heading = jnp.stack([jnp.cos(strike[0]), jnp.sin(strike[0]), zeros])
    second_anchor = first_anchor + length * heading
    anchor = jnp.stack([first_anchor, second_anchor], axis=1)
    return (anchor.reshape(3, FAULT_BLOCKS), strike.reshape(FAULT_BLOCKS), dip_angle.reshape(FAULT_BLOCKS), length)


def draw_centroid(key, part):
    anchor, strike, dip_angle, length = block_frames(key)
    along_strike = jax.random.uniform(jax.random.fold_in(key, 106), (FAULT_BLOCKS, E_DEV), jnp.float32, 0.0, 1.0) * length
    down_dip = jax.random.uniform(jax.random.fold_in(key, 107), (FAULT_BLOCKS, E_DEV), jnp.float32, 0.0, 1.0) * depth_extent
    slip_x = jnp.cos(strike)[:, None]
    slip_y = jnp.sin(strike)[:, None]
    dip_x = (-jnp.sin(strike) * jnp.cos(dip_angle))[:, None]
    dip_y = (jnp.cos(strike) * jnp.cos(dip_angle))[:, None]
    dip_z = (-jnp.sin(dip_angle))[:, None]
    coord_x = anchor[0][:, None] + along_strike * slip_x + down_dip * dip_x
    coord_y = anchor[1][:, None] + along_strike * slip_y + down_dip * dip_y
    coord_z = anchor[2][:, None] + down_dip * dip_z
    return jnp.stack([coord_x, coord_y, coord_z]).reshape(3, ELEMS).astype(jnp.float32)


def draw_angles(key, part):
    anchor, strike, dip_angle, length = block_frames(key)
    strike_rough = jax.random.uniform(jax.random.fold_in(key, 108), (FAULT_BLOCKS, E_DEV), jnp.float32, -0.25, 0.25)
    dip_rough = jax.random.uniform(jax.random.fold_in(key, 109), (FAULT_BLOCKS, E_DEV), jnp.float32, -0.25, 0.25)
    element_strike = strike[:, None] + strike_rough
    element_dip = dip_angle[:, None] + dip_rough
    return jnp.stack([element_strike, element_dip]).reshape(2, ELEMS).astype(jnp.float32)


def draw_slip_rate(key, part):
    variation = jax.random.normal(jax.random.fold_in(key, 112), (FAULT_BLOCKS, E_DEV), jnp.float32)
    values = jnp.clip(1.0 + 0.5 * variation, -1.0, 3.0)
    return values.reshape(ELEMS).astype(jnp.float32)


def draw_near(key, part):
    strands = FAULT_BLOCKS // 2
    row_index = lax.broadcasted_iota(jnp.int32, (FAULT_BLOCKS, FAULT_BLOCKS), 0)
    col_index = lax.broadcasted_iota(jnp.int32, (FAULT_BLOCKS, FAULT_BLOCKS), 1)
    strand_diff = jnp.abs(row_index % strands - col_index % strands)
    beside = strand_diff <= 1
    coin_flips = jax.random.randint(jax.random.fold_in(key, 113), (FAULT_BLOCKS, FAULT_BLOCKS), 0, 2)
    linked = jnp.where(row_index < col_index, coin_flips, coin_flips.T)
    flags = jnp.where(beside, linked, 0)
    return jnp.where(row_index == col_index, 1, flags).astype(jnp.int32)


def level_of(stream_key, extent, shards, smallest, top_value):
    level, own = 1.0, jax.random.fold_in(stream_key, 6)
    for axis_at, blocks in shards:
        heights = jnp.exp(jax.random.uniform(jax.random.fold_in(own, axis_at), (blocks,), jnp.float32, smallest / len(shards), top_value / len(shards)))
        level = level * jnp.repeat(heights, extent[axis_at] // blocks).reshape([-1 if axis == axis_at else 1 for axis in range(len(extent))])
    return level


def length_profile(number_of, total, reach, slope):
    weights = [(1 << 20) // math.isqrt(rank ** slope) + 1 for rank in range(2, number_of + 1)]
    spare, counts = total - reach - (number_of - 1), [1] * (number_of - 1)
    while spare > 0:
        movable = [i for i in range(number_of - 1) if counts[i] < reach]
        pool, remaining = sum([weights[i] for i in movable]), spare
        for i in movable:
            extra = min(reach - counts[i], max(1, remaining * weights[i] // pool), spare)
            counts[i] = counts[i] + extra
            spare = spare - extra
    return np.array([reach] + counts)


def uneven(rng, number_of, total, most, skew):
    if number_of == 2:
        one = jax.random.randint(rng, (), max(1, total - most), min(most, total - 1) + 1)
        return jnp.stack([one, total - one])
    lengths = jnp.asarray(length_profile(number_of, total, most, skew), jnp.int32)
    twos = (number_of - 1) // 2
    source_of, taker = lengths[1:1 + 2 * twos:2], lengths[2:2 + 2 * twos:2]
    room = jnp.minimum(source_of - 1, most - taker)
    shifted = jax.random.randint(jax.random.fold_in(rng, 1), (twos,), 0, 1 << 20) % (room + 1)
    lengths = lengths.at[1:1 + 2 * twos:2].set(source_of - shifted).at[2:2 + 2 * twos:2].set(taker + shifted)
    return lengths[jax.random.permutation(jax.random.fold_in(rng, 2), number_of)]


def setup_inputs(seed: int = 0, part: int = 0) -> dict:
    seeds = jax.random.split(jax.random.key(seed), 7)
    part_splits = jax.random.split(jax.random.fold_in(seeds[6], part), 7)
    centroid = draw_centroid(jax.random.fold_in(jax.random.fold_in(seeds[6], part), 71), part)
    angles = draw_angles(jax.random.fold_in(jax.random.fold_in(seeds[6], part), 71), part)
    size = jnp.clip(jnp.exp(math.log(0.004) - 1.3862944 * jax.random.uniform(part_splits[2], (ELEMS,), jnp.float32) ** level_of(part_splits[2], (ELEMS,), ((0, 16),), -0.2, 0.2)), 0.001, 0.004)
    slip_rate = draw_slip_rate(jax.random.fold_in(jax.random.fold_in(seeds[6], part), 71), part)
    live_count = uneven(part_splits[4], FAULT_BLOCKS, LIVE_TOTAL, E_DEV, 2).astype(jnp.int32)
    near = draw_near(jax.random.fold_in(jax.random.fold_in(seeds[6], part), 71), part)
    return dict(centroid=centroid, angles=angles, size=size, slip_rate=slip_rate, live_count=live_count, near=near)


coupling = 0.002

def frame(centroid, angles, size, weight):
    strike = angles[0]
    dip_angle = angles[1]
    squared = size * size
    rows = [centroid[0], centroid[1], centroid[2], jnp.cos(strike), jnp.sin(strike), -jnp.sin(dip_angle) * jnp.sin(strike), jnp.sin(dip_angle) * jnp.cos(strike), jnp.cos(dip_angle), squared, weight * squared]
    return jnp.stack(rows)

def pair_terms(target, source, flags):
    sep_x = target[0][:, None] - source[0][None, :]
    sep_y = target[1][:, None] - source[1][None, :]
    sep_z = target[2][:, None] - source[2][None, :]
    dist_sq = sep_x * sep_x + sep_y * sep_y + sep_z * sep_z + target[8][:, None] + source[8][None, :]
    inverse = 1.0 / dist_sq
    inv_cube = inverse * jnp.sqrt(inverse)
    inv_five = inv_cube * inverse
    along_target = target[3][:, None] * sep_x + target[4][:, None] * sep_y
    along_source = source[3][None, :] * sep_x + source[4][None, :] * sep_y
    normal_target = target[5][:, None] * sep_x + target[6][:, None] * sep_y + target[7][:, None] * sep_z
    slip_dot = target[3][:, None] * source[3][None, :] + target[4][:, None] * source[4][None, :]
    cross_dot = target[5][:, None] * source[3][None, :] + target[6][:, None] * source[4][None, :]
    shear = inv_cube * slip_dot - 3.0 * inv_five * along_target * along_source
    normal = flags * (inv_cube * cross_dot - 3.0 * inv_five * normal_target * along_source)
    return (shear, normal)

def reference(centroid, angles, size, slip_rate, live_count, near):
    index = jnp.arange(ELEMS, dtype=jnp.int32)
    owner = index // E_DEV
    live = (index - owner * E_DEV < live_count[owner]).astype(jnp.float32)
    geometry = frame(centroid, angles, size, slip_rate * live)

    def one_block(block):
        target = lax.dynamic_slice_in_dim(geometry, (block * E_DEV).astype(jnp.int32), E_DEV, 1)
        flags = jnp.repeat(near[block], E_DEV).astype(jnp.float32)[None, :]
        shear, normal = pair_terms(target, geometry, flags)
        return (jnp.dot(shear, geometry[9], precision=lax.Precision.HIGHEST), jnp.dot(normal, geometry[9], precision=lax.Precision.HIGHEST))
    shear_rows, normal_rows = lax.map(one_block, jnp.arange(FAULT_BLOCKS, dtype=jnp.int32))
    shear_rate = coupling * live * shear_rows.reshape(ELEMS)
    normal_rate = coupling * live * normal_rows.reshape(ELEMS)
    return (shear_rate, normal_rate)
```

```python
import functools

import jax
import jax.numpy as jnp
from jax import lax
from jax.experimental import pallas as pl
from jax.experimental.pallas import tpu as pltpu
from jax.sharding import PartitionSpec as P

coupling = 0.002
LANES = 128
ROWS = 32
UNROLL = 8
FIELDS = 6


def prep_kernel(live_ref, centroid, angles, size, slip_rate, source_ref, target_ref):
    per_block = centroid.shape[1]
    count = live_ref[0]
    strike = angles[0:1, :]
    dip_angle = angles[1:2, :]
    cos_p, sin_p = jnp.cos(strike), jnp.sin(strike)
    cos_q, sin_q = jnp.cos(dip_angle), jnp.sin(dip_angle)
    live = (lax.broadcasted_iota(jnp.int32, (1, per_block), 1) < count).astype(jnp.float32)
    squared = size[...] * size[...]
    weight = slip_rate[...] * live * squared
    source_ref[0:3, :] = centroid[...]
    source_ref[3:4, :] = squared
    source_ref[4:5, :] = weight * cos_p
    source_ref[5:6, :] = weight * sin_p
    source_ref[6:7, :] = jnp.full((1, per_block), count, jnp.int32).astype(jnp.float32)
    source_ref[7:8, :] = jnp.zeros((1, per_block), jnp.float32)
    target_ref[0:3, :] = centroid[...]
    target_ref[3:4, :] = squared
    target_ref[4:5, :] = cos_p
    target_ref[5:6, :] = sin_p
    target_ref[6:7, :] = -sin_q * sin_p
    target_ref[7:8, :] = sin_q * cos_p
    target_ref[8:9, :] = cos_q
    target_ref[9:10, :] = live * coupling
    target_ref[10:16, :] = jnp.zeros((6, per_block), jnp.float32)


def pair_sums(columns, field, totals):
    x, y, z, s2 = columns
    rx = x - field(0)
    ry = y - field(1)
    rz = z - field(2)
    d2 = (rx * rx + ry * ry) + (rz * rz + (s2 + field(3)))
    root = lax.rsqrt(d2)
    inverse = root * root
    cube = inverse * root
    ux, uy = field(4), field(5)
    bent = (cube * inverse) * (ux * rx + uy * ry)
    ax, ay, bx, by, bz = totals
    return (ax + cube * ux, ay + cube * uy, bx + bent * rx, by + bent * ry, bz + bent * rz)


def main_kernel(live_ref, near_ref, piece, target, shear_ref, normal_ref,
                spread, columns, chunks, shear_part, normal_part):
    count_blocks = near_ref.shape[1]
    per_block = target.shape[1]
    per_chunks = per_block // LANES
    total_chunks = count_blocks * per_chunks

    for block in range(count_blocks):
        for at in range(per_chunks):
            lo = block * per_block + at * LANES
            for row in range(FIELDS):
                spread[block * per_chunks + at, row * 8:row * 8 + 8, :] = jnp.broadcast_to(
                    piece[row:row + 1, lo:lo + LANES], (8, LANES))
    for row in range(FIELDS):
        fill = 0.0 if row != 3 else 1.0
        spread[total_chunks, row * 8:row * 8 + 8, :] = jnp.full((8, LANES), fill, jnp.float32)
    columns[...] = target[...].T

    def list_blocks(wanted, start):
        position = start
        for block in range(count_blocks):
            held = piece[6:7, block * per_block:block * per_block + 1][0, 0].astype(jnp.int32)
            here = jnp.where(near_ref[0, block] == wanted, (held + LANES - 1) // LANES, 0)

            def put(at, carry, block=block, position=position):
                chunks[position + at] = block * per_chunks + at
                return carry

            lax.fori_loop(0, here, put, 0)
            position = position + here
        rest = lax.rem(UNROLL - lax.rem(position, UNROLL), UNROLL)

        def pad(at, carry):
            chunks[position + at] = total_chunks
            return carry

        lax.fori_loop(0, rest, pad, 0)
        return position + rest

    linked_end = list_blocks(1, 0)
    all_end = list_blocks(0, linked_end)
    linked_steps = linked_end // UNROLL
    all_steps = all_end // UNROLL

    shear_part[...] = jnp.zeros_like(shear_part)
    normal_part[...] = jnp.zeros_like(normal_part)

    def group(number, carry):
        lo = pl.multiple_of(number * ROWS, ROWS)
        held = columns[pl.ds(lo, ROWS), :]

        def column(row):
            return [jnp.broadcast_to(held[8 * k:8 * k + 8, row:row + 1], (8, LANES))
                    for k in range(ROWS // 8)]

        places = list(zip(column(0), column(1), column(2), column(3)))
        zero = jnp.zeros((8, LANES), jnp.float32)

        def step(at, totals):
            totals = list(totals)
            for k in range(UNROLL):
                chunk = chunks[at * UNROLL + k]

                def field(row):
                    return spread[chunk, row * 8:row * 8 + 8, :]

                for sub in range(ROWS // 8):
                    totals[sub] = pair_sums(places[sub], field, totals[sub])
            return tuple(totals)

        start = tuple((zero,) * 5 for _ in range(ROWS // 8))
        linked = lax.fori_loop(0, linked_steps, step, start)
        nx, ny, nz = column(6), column(7), column(8)
        for sub in range(ROWS // 8):
            ax, ay, bx, by, bz = linked[sub]
            normal_part[pl.ds(lo + 8 * sub, 8), :] = (
                nx[sub] * (ax - 3.0 * bx) + ny[sub] * (ay - 3.0 * by) - nz[sub] * (3.0 * bz))
        totals = lax.fori_loop(linked_steps, all_steps, step, linked)
        tx, ty = column(4), column(5)
        for sub in range(ROWS // 8):
            ax, ay, bx, by, bz = totals[sub]
            shear_part[pl.ds(lo + 8 * sub, 8), :] = (
                tx[sub] * (ax - 3.0 * bx) + ty[sub] * (ay - 3.0 * by))
        return carry

    lax.fori_loop(0, (live_ref[0] + ROWS - 1) // ROWS, group, 0)
    ones = jnp.ones((8, LANES), jnp.float32)
    dims = (((1,), (1,)), ((), ()))
    for part, out in ((shear_part, shear_ref), (normal_part, normal_ref)):
        summed = lax.dot_general(ones, part[...], dims, precision=lax.Precision.HIGHEST,
                                 preferred_element_type=jnp.float32)
        out[...] = summed[0:1, :] * target[9:10, :]


def body(centroid, angles, size, slip_rate, live_count, near):
    per_block = centroid.shape[1]
    count_blocks = near.shape[1]
    smem = pl.BlockSpec(memory_space=pltpu.SMEM)
    vmem = pl.BlockSpec(memory_space=pltpu.VMEM)
    source, target = pl.pallas_call(
        prep_kernel,
        out_shape=(jax.ShapeDtypeStruct((8, per_block), jnp.float32),
                   jax.ShapeDtypeStruct((16, per_block), jnp.float32)),
        in_specs=[smem] + [vmem] * 4,
        out_specs=(vmem, vmem),
    )(live_count, centroid, angles, size.reshape(1, per_block), slip_rate.reshape(1, per_block))
    piece = lax.all_gather(source, "blocks", axis=1, tiled=True)
    total_chunks = count_blocks * per_block // LANES
    shear, normal = pl.pallas_call(
        main_kernel,
        out_shape=(jax.ShapeDtypeStruct((1, per_block), jnp.float32),) * 2,
        in_specs=[smem, smem, vmem, vmem],
        out_specs=(vmem, vmem),
        scratch_shapes=[
            pltpu.VMEM((total_chunks + 1, 8 * FIELDS, LANES), jnp.float32),
            pltpu.VMEM((per_block, 16), jnp.float32),
            pltpu.SMEM((total_chunks + 2 * UNROLL,), jnp.int32),
            pltpu.VMEM((per_block, LANES), jnp.float32),
            pltpu.VMEM((per_block, LANES), jnp.float32),
        ],
        compiler_params=pltpu.CompilerParams(vmem_limit_bytes=48 * 1024 * 1024),
    )(live_count, near, piece, target)
    return shear.reshape(per_block), normal.reshape(per_block)


def solution(mesh):
    in_specs = (
        P(None, ("runs", "blocks")),
        P(None, ("runs", "blocks")),
        P(("runs", "blocks")),
        P(("runs", "blocks")),
        P(("runs", "blocks")),
        P(("runs", "blocks"), None),
    )
    out_specs = (P(("runs", "blocks")), P(("runs", "blocks")))
    return jax.shard_map(body, mesh=mesh, in_specs=in_specs, out_specs=out_specs, check_vma=False)
```

```python
import functools
import math

import jax
import jax.numpy as jnp
from jax import lax
from jax.experimental import pallas as pl
from jax.experimental.pallas import tpu as pltpu
from jax.sharding import PartitionSpec as P

coupling = 0.002
LANES = 128
ROWS = 32
UNROLL = 8
FIELDS = 6
WIDE = 4
TURNS = 64
COUNT_LANE = 127
BIG = 1e30
SMALLEST = 2e-6
SPREAD_LIMIT = 800.0
FEATURES = 16
SOURCE_PIECES = (0, 0, 1, 0, 2, 1)
TARGET_PIECES = (0, 1, 0, 2, 0, 1)
DEPTH = FEATURES * len(SOURCE_PIECES)


def prep_kernel(live_ref, centroid, angles, size, slip_rate, source_ref, target_ref):
    per_block = centroid.shape[1]
    count = live_ref[0]
    strike = angles[0:1, :]
    dip_angle = angles[1:2, :]
    cos_p, sin_p = jnp.cos(strike), jnp.sin(strike)
    cos_q, sin_q = jnp.cos(dip_angle), jnp.sin(dip_angle)
    is_live = lax.broadcasted_iota(jnp.int32, (1, per_block), 1) < count
    live = is_live.astype(jnp.float32)
    squared = size[...] * size[...]
    weight = slip_rate[...] * live * squared
    place = [jnp.where(is_live, centroid[k:k + 1, :], centroid[k:k + 1, 0:1]) for k in range(3)]
    for k in range(3):
        source_ref[k:k + 1, :] = place[k]
        target_ref[k:k + 1, :] = place[k]
    source_ref[3:4, :] = squared
    source_ref[4:5, :] = weight * cos_p
    source_ref[5:6, :] = weight * sin_p
    target_ref[3:4, :] = squared
    target_ref[4:5, :] = cos_p
    target_ref[5:6, :] = sin_p
    target_ref[6:7, :] = -sin_q * sin_p
    target_ref[7:8, :] = sin_q * cos_p
    target_ref[8:9, :] = cos_q
    target_ref[9:10, :] = live * coupling
    target_ref[10:16, :] = jnp.zeros((6, per_block), jnp.float32)
    turn = lax.broadcasted_iota(jnp.int32, (TURNS, 1), 0).astype(jnp.float32) * (math.pi / TURNS)
    along = jnp.cos(turn) * place[0] + jnp.sin(turn) * place[1]
    row = lax.broadcasted_iota(jnp.int32, (TURNS + 8, LANES), 0)
    lane = lax.broadcasted_iota(jnp.int32, (TURNS + 8, LANES), 1)
    all_rows = jnp.concatenate([along, jnp.broadcast_to(place[2], (8, per_block))], axis=0)
    for at, ends in ((6, jnp.min(all_rows, axis=1, keepdims=True)),
                     (7, jnp.max(all_rows, axis=1, keepdims=True))):
        line = jnp.sum(jnp.where(row == lane, ends, 0.0), axis=0, keepdims=True)
        line = jnp.where(lane[0:1, :] == COUNT_LANE, count.astype(jnp.float32), line)
        source_ref[at:at + 1, 0:LANES] = line
        source_ref[at:at + 1, LANES:] = jnp.zeros((1, per_block - LANES), jnp.float32)


def pair_sums(columns, field, totals):
    x, y, z, s2 = columns
    rx = x - field(0)
    ry = y - field(1)
    rz = z - field(2)
    d2 = (rx * rx + ry * ry) + (rz * rz + (s2 + field(3)))
    root = lax.rsqrt(d2)
    inverse = root * root
    cube = inverse * root
    ux, uy = field(4), field(5)
    bent = (cube * inverse) * (ux * rx + uy * ry)
    ax, ay, bx, by, bz = totals
    return (ax + cube * ux, ay + cube * uy, bx + bent * rx, by + bent * ry, bz + bent * rz)


def three_pieces(value):
    first = value.astype(jnp.bfloat16)
    rest = value - first.astype(jnp.float32)
    second = rest.astype(jnp.bfloat16)
    third = (rest - second.astype(jnp.float32)).astype(jnp.bfloat16)
    return first, second, third


def source_features(held, middle):
    x, y, z = (held[k:k + 1, :] - middle[k] for k in range(3))
    ux, uy = held[4:5, :], held[5:6, :]
    s = x * x + y * y + z * z + held[3:4, :]
    uxx, uxy, uxz, uyx, uyy, uyz = ux * x, ux * y, ux * z, uy * x, uy * y, uy * z
    along = uxx + uyy
    along3 = 3.0 * along
    return jnp.concatenate([
        jnp.ones_like(x), s, x, y, z, ux, uy, uxx, uxy, uxz, uyx, uyy, uyz,
        s * ux - along3 * x, s * uy - along3 * y, z * along], axis=0)


def target_features(held, middle, direction):
    x, y, z = (held[k:k + 1, :] - middle[k] for k in range(3))
    r = x * x + y * y + z * z + held[3:4, :]
    zero, one = jnp.zeros_like(x), jnp.ones_like(x)
    if direction is None:
        return jnp.concatenate([r, one, -2.0 * x, -2.0 * y, -2.0 * z] + [zero] * 11, axis=0)
    a, b, c = direction
    t3 = 3.0 * (a * x + b * y + c * z)
    return jnp.concatenate([
        zero, zero, zero, zero, zero, r * a - t3 * x, r * b - t3 * y,
        a * x + t3, 3.0 * b * x - 2.0 * a * y, 3.0 * c * x - 2.0 * a * z,
        3.0 * a * y - 2.0 * b * x, b * y + t3, 3.0 * c * y - 2.0 * b * z,
        a, b, -3.0 * c], axis=0)


def block_at(position, me, count_blocks):
    flipped, bit, other = 0, 1, count_blocks // 2
    while other:
        if position & bit:
            flipped |= other
        bit, other = bit * 2, other // 2
    return me ^ flipped


def main_kernel(me_ref, near_ref, piece, target, shear_ref, normal_ref,
                spread, columns, near_chunks, far_chunks, shear_part, normal_part,
                weights, factors):
    count_blocks = near_ref.shape[1]
    per_block = target.shape[1]
    per_chunks = per_block // LANES
    total_chunks = count_blocks * per_chunks
    me = me_ref[0]

    low = jnp.concatenate([piece[p, 6:7, 0:LANES] for p in range(count_blocks)], axis=0)
    high = jnp.concatenate([piece[p, 7:8, 0:LANES] for p in range(count_blocks)], axis=0)
    lane = lax.broadcasted_iota(jnp.int32, (1, LANES), 1)
    own_low, own_high = low[0:1, :], high[0:1, :]
    center = 0.5 * (own_low + own_high)
    is_axis = (lane == 0) | (lane == TURNS // 2) | (lane == TURNS)
    gap = jnp.max(jnp.where(lane <= TURNS, jnp.maximum(low - own_high, own_low - high), 0.0),
                  axis=1, keepdims=True)
    gap = jnp.maximum(gap, 0.0)
    out = jnp.maximum(jnp.abs(low - center), jnp.abs(high - center))
    reach = jnp.sqrt(jnp.sum(jnp.where(is_axis, out * out, 0.0), axis=1, keepdims=True))
    both = reach + reach[0:1, :]
    is_near = (gap * gap + SMALLEST) * SPREAD_LIMIT < both * both
    marks = jnp.where(is_near, 1, 0)
    held_count = low[:, COUNT_LANE:COUNT_LANE + 1].astype(jnp.int32)
    middle = [center[0:1, k:k + 1] for k in (0, TURNS // 2, TURNS)]

    def list_blocks(chunks, near, linked, start, unit):
        position = start
        for p in range(count_blocks):
            wanted = (marks[p, 0] == near) & (near_ref[0, block_at(p, me, count_blocks)] == linked)
            here = jnp.where(wanted, (held_count[p, 0] + LANES - 1) // LANES, 0)

            def put(at, carry, p=p, position=position):
                chunks[position + at] = p * per_chunks + at
                return carry

            lax.fori_loop(0, here, put, 0)
            position = position + here
        rest = lax.rem(unit - lax.rem(position, unit), unit)

        def pad(at, carry):
            chunks[position + at] = total_chunks
            return carry

        lax.fori_loop(0, rest, pad, 0)
        return position + rest

    near_linked = list_blocks(near_chunks, 1, 1, 0, UNROLL)
    near_all = list_blocks(near_chunks, 1, 0, near_linked, UNROLL)
    far_linked = list_blocks(far_chunks, 0, 1, 0, WIDE)
    far_all = list_blocks(far_chunks, 0, 0, far_linked, WIDE)

    def chunk_of(chunk):
        real = jnp.minimum(chunk, total_chunks - 1)
        lo = pl.multiple_of(lax.rem(real, per_chunks) * LANES, LANES)
        held = piece[real // per_chunks, :, pl.ds(lo, LANES)]
        row = lax.broadcasted_iota(jnp.int32, (8, LANES), 0)
        blank = jnp.where(row == 3, 1.0, 0.0)
        return jnp.where((row >= 3) & (chunk == total_chunks), blank, held)

    def place_near(at, carry):
        for k in range(UNROLL):
            number = at * UNROLL + k
            held = chunk_of(near_chunks[number])
            for row in range(FIELDS):
                spread[number, row * 8:row * 8 + 8, :] = jnp.broadcast_to(
                    held[row:row + 1, :], (8, LANES))
        return carry

    lax.fori_loop(0, near_all // UNROLL, place_near, 0)

    def place_far(at, carry):
        for k in range(WIDE):
            number = at * WIDE + k
            pieces = three_pieces(source_features(chunk_of(far_chunks[number]), middle))
            lo = pl.multiple_of(number * LANES, LANES)
            for slot, which in enumerate(SOURCE_PIECES):
                weights[slot * FEATURES:(slot + 1) * FEATURES, pl.ds(lo, LANES)] = pieces[which]
        return carry

    lax.fori_loop(0, far_all // WIDE, place_far, 0)

    columns[...] = target[...].T
    own = target[...]
    zero_row = jnp.zeros((1, per_block), jnp.float32)
    ways = (None, (own[4:5], own[5:6], zero_row), (own[6:7], own[7:8], own[8:9]))
    for which, way in enumerate(ways):
        pieces = three_pieces(target_features(own, middle, way))
        stacked = jnp.concatenate(
            [pieces[k].astype(jnp.float32) for k in TARGET_PIECES]
            + [jnp.zeros((LANES - DEPTH, per_block), jnp.float32)], axis=0)
        factors[which, :, :] = stacked.T.astype(jnp.bfloat16)

    def group(number, carry):
        lo = pl.multiple_of(number * ROWS, ROWS)
        held = columns[pl.ds(lo, ROWS), :]

        def column(row):
            return [jnp.broadcast_to(held[8 * k:8 * k + 8, row:row + 1], (8, LANES))
                    for k in range(ROWS // 8)]

        places = list(zip(column(0), column(1), column(2), column(3)))
        zero = jnp.zeros((8, LANES), jnp.float32)

        def step(at, totals):
            totals = list(totals)
            for k in range(UNROLL):
                def field(row):
                    return spread[at * UNROLL + k, row * 8:row * 8 + 8, :]

                for sub in range(ROWS // 8):
                    totals[sub] = pair_sums(places[sub], field, totals[sub])
            return tuple(totals)

        start = tuple((zero,) * 5 for _ in range(ROWS // 8))
        linked = lax.fori_loop(0, near_linked // UNROLL, step, start)
        nx, ny, nz = column(6), column(7), column(8)
        for sub in range(ROWS // 8):
            ax, ay, bx, by, bz = linked[sub]
            normal_part[pl.ds(lo + 8 * sub, 8), :] = (
                nx[sub] * (ax - 3.0 * bx) + ny[sub] * (ay - 3.0 * by) - nz[sub] * (3.0 * bz))
        totals = lax.fori_loop(near_linked // UNROLL, near_all // UNROLL, step, linked)
        tx, ty = column(4), column(5)
        for sub in range(ROWS // 8):
            ax, ay, bx, by, bz = totals[sub]
            shear_part[pl.ds(lo + 8 * sub, 8), :] = (
                tx[sub] * (ax - 3.0 * bx) + ty[sub] * (ay - 3.0 * by))
        return carry

    lax.fori_loop(0, per_block // ROWS, group, 0)

    def far_step(with_normal, at, carry):
        lo = pl.multiple_of(at * WIDE * LANES, WIDE * LANES)
        sources = weights[:, pl.ds(lo, WIDE * LANES)]

        def product(which):
            return jnp.dot(factors[which, :, 0:DEPTH], sources,
                           preferred_element_type=jnp.float32)

        def add(part, terms):
            total = terms[:, 0:LANES]
            for k in range(1, WIDE):
                total = total + terms[:, k * LANES:(k + 1) * LANES]
            part[...] += total

        root = lax.rsqrt(product(0))
        inverse = root * root
        fourth = inverse * inverse
        add(shear_part, (product(1) * root) * fourth)
        if with_normal:
            add(normal_part, (product(2) * root) * fourth)
        return carry

    lax.fori_loop(0, far_linked // WIDE, functools.partial(far_step, True), 0)
    lax.fori_loop(far_linked // WIDE, far_all // WIDE, functools.partial(far_step, False), 0)

    ones = jnp.ones((8, LANES), jnp.float32)
    dims = (((1,), (1,)), ((), ()))
    for part, result in ((shear_part, shear_ref), (normal_part, normal_ref)):
        summed = lax.dot_general(ones, part[...], dims, precision=lax.Precision.HIGHEST,
                                 preferred_element_type=jnp.float32)
        result[...] = summed[0:1, :] * own[9:10, :]


def body(centroid, angles, size, slip_rate, live_count, near):
    per_block = centroid.shape[1]
    count_blocks = near.shape[1]
    smem = pl.BlockSpec(memory_space=pltpu.SMEM)
    vmem = pl.BlockSpec(memory_space=pltpu.VMEM)
    source, target = pl.pallas_call(
        prep_kernel,
        out_shape=(jax.ShapeDtypeStruct((8, per_block), jnp.float32),
                   jax.ShapeDtypeStruct((16, per_block), jnp.float32)),
        in_specs=[smem] + [vmem] * 4,
        out_specs=(vmem, vmem),
    )(live_count, centroid, angles, size.reshape(1, per_block), slip_rate.reshape(1, per_block))
    piece = source[None]
    bit = count_blocks // 2
    while bit:
        swap = [(at, at ^ bit) for at in range(count_blocks)]
        piece = jnp.concatenate([piece, lax.ppermute(piece, "blocks", swap)], axis=0)
        bit //= 2
    total_chunks = count_blocks * per_block // LANES
    me = lax.axis_index("blocks").astype(jnp.int32).reshape(1)
    shear, normal = pl.pallas_call(
        main_kernel,
        out_shape=(jax.ShapeDtypeStruct((1, per_block), jnp.float32),) * 2,
        in_specs=[smem, smem, vmem, vmem],
        out_specs=(vmem, vmem),
        scratch_shapes=[
            pltpu.VMEM((total_chunks + 2 * UNROLL, 8 * FIELDS, LANES), jnp.float32),
            pltpu.VMEM((per_block, 16), jnp.float32),
            pltpu.SMEM((total_chunks + 2 * UNROLL,), jnp.int32),
            pltpu.SMEM((total_chunks + 2 * WIDE,), jnp.int32),
            pltpu.VMEM((per_block, LANES), jnp.float32),
            pltpu.VMEM((per_block, LANES), jnp.float32),
            pltpu.VMEM((DEPTH, (total_chunks + 2 * WIDE) * LANES), jnp.bfloat16),
            pltpu.VMEM((3, per_block, LANES), jnp.bfloat16),
        ],
        compiler_params=pltpu.CompilerParams(vmem_limit_bytes=56 * 1024 * 1024),
    )(me, near, piece, target)
    return shear.reshape(per_block), normal.reshape(per_block)


def solution(mesh):
    in_specs = (
        P(None, ("runs", "blocks")),
        P(None, ("runs", "blocks")),
        P(("runs", "blocks")),
        P(("runs", "blocks")),
        P(("runs", "blocks")),
        P(("runs", "blocks"), None),
    )
    out_specs = (P(("runs", "blocks")), P(("runs", "blocks")))
    return jax.shard_map(body, mesh=mesh, in_specs=in_specs, out_specs=out_specs, check_vma=False)
```

```python
import functools
import math

import jax
import jax.numpy as jnp
from jax import lax
from jax.experimental import pallas as pl
from jax.experimental.pallas import tpu as pltpu
from jax.sharding import PartitionSpec as P

coupling = 0.002
LANES = 128
ROWS = 128
UNROLL = 2
FIELDS = 6
WIDE = 4
TURNS = 64
COUNT_LANE = 127
BIG = 1e30
SMALLEST = 2e-6
SPREAD_LIMIT = 800.0
FEATURES = 16
SOURCE_PIECES = (0, 0, 1, 0, 2, 1)
TARGET_PIECES = (0, 1, 0, 2, 0, 1)
DEPTH = FEATURES * len(SOURCE_PIECES)


def prep_kernel(live_ref, centroid, angles, size, slip_rate, source_ref, target_ref):
    per_block = centroid.shape[1]
    count = live_ref[0]
    strike = angles[0:1, :]
    dip_angle = angles[1:2, :]
    cos_p, sin_p = jnp.cos(strike), jnp.sin(strike)
    cos_q, sin_q = jnp.cos(dip_angle), jnp.sin(dip_angle)
    is_live = lax.broadcasted_iota(jnp.int32, (1, per_block), 1) < count
    live = is_live.astype(jnp.float32)
    squared = size[...] * size[...]
    weight = slip_rate[...] * live * squared
    place = [jnp.where(is_live, centroid[k:k + 1, :], centroid[k:k + 1, 0:1]) for k in range(3)]
    for k in range(3):
        source_ref[k:k + 1, :] = place[k]
        target_ref[k:k + 1, :] = place[k]
    source_ref[3:4, :] = squared
    source_ref[4:5, :] = weight * cos_p
    source_ref[5:6, :] = weight * sin_p
    target_ref[3:4, :] = squared
    target_ref[4:5, :] = cos_p
    target_ref[5:6, :] = sin_p
    target_ref[6:7, :] = -sin_q * sin_p
    target_ref[7:8, :] = sin_q * cos_p
    target_ref[8:9, :] = cos_q
    target_ref[9:10, :] = live * coupling
    target_ref[10:16, :] = jnp.zeros((6, per_block), jnp.float32)
    turn = lax.broadcasted_iota(jnp.int32, (TURNS, 1), 0).astype(jnp.float32) * (math.pi / TURNS)
    along = jnp.cos(turn) * place[0] + jnp.sin(turn) * place[1]
    row = lax.broadcasted_iota(jnp.int32, (TURNS + 8, LANES), 0)
    lane = lax.broadcasted_iota(jnp.int32, (TURNS + 8, LANES), 1)
    all_rows = jnp.concatenate([along, jnp.broadcast_to(place[2], (8, per_block))], axis=0)
    for at, ends in ((6, jnp.min(all_rows, axis=1, keepdims=True)),
                     (7, jnp.max(all_rows, axis=1, keepdims=True))):
        line = jnp.sum(jnp.where(row == lane, ends, 0.0), axis=0, keepdims=True)
        line = jnp.where(lane[0:1, :] == COUNT_LANE, count.astype(jnp.float32), line)
        source_ref[at:at + 1, 0:LANES] = line
        source_ref[at:at + 1, LANES:] = jnp.zeros((1, per_block - LANES), jnp.float32)


def pair_sums(columns, field, totals):
    x, y, z, s2 = columns
    rx = x - field(0)
    ry = y - field(1)
    rz = z - field(2)
    d2 = (rx * rx + ry * ry) + (rz * rz + (s2 + field(3)))
    root = lax.rsqrt(d2)
    inverse = root * root
    cube = inverse * root
    ux, uy = field(4), field(5)
    bent = (cube * inverse) * (ux * rx + uy * ry)
    ax, ay, bx, by, bz = totals
    return (ax + cube * ux, ay + cube * uy, bx + bent * rx, by + bent * ry, bz + bent * rz)


def three_pieces(value):
    first = value.astype(jnp.bfloat16)
    rest = value - first.astype(jnp.float32)
    second = rest.astype(jnp.bfloat16)
    third = (rest - second.astype(jnp.float32)).astype(jnp.bfloat16)
    return first, second, third


def source_features(held, middle):
    x, y, z = (held[k:k + 1, :] - middle[k] for k in range(3))
    ux, uy = held[4:5, :], held[5:6, :]
    s = x * x + y * y + z * z + held[3:4, :]
    uxx, uxy, uxz, uyx, uyy, uyz = ux * x, ux * y, ux * z, uy * x, uy * y, uy * z
    along = uxx + uyy
    along3 = 3.0 * along
    return jnp.concatenate([
        jnp.ones_like(x), s, x, y, z, ux, uy, uxx, uxy, uxz, uyx, uyy, uyz,
        s * ux - along3 * x, s * uy - along3 * y, z * along], axis=0)


def target_features(held, middle, direction):
    x, y, z = (held[k:k + 1, :] - middle[k] for k in range(3))
    r = x * x + y * y + z * z + held[3:4, :]
    zero, one = jnp.zeros_like(x), jnp.ones_like(x)
    if direction is None:
        return jnp.concatenate([r, one, -2.0 * x, -2.0 * y, -2.0 * z] + [zero] * 11, axis=0)
    a, b, c = direction
    t3 = 3.0 * (a * x + b * y + c * z)
    return jnp.concatenate([
        zero, zero, zero, zero, zero, r * a - t3 * x, r * b - t3 * y,
        a * x + t3, 3.0 * b * x - 2.0 * a * y, 3.0 * c * x - 2.0 * a * z,
        3.0 * a * y - 2.0 * b * x, b * y + t3, 3.0 * c * y - 2.0 * b * z,
        a, b, -3.0 * c], axis=0)


def block_at(position, me, count_blocks):
    flipped, bit, other = 0, 1, count_blocks // 2
    while other:
        if position & bit:
            flipped |= other
        bit, other = bit * 2, other // 2
    return me ^ flipped


def stage_kernel(first, last, me_ref, near_ref, source, piece, target, *rest):
    (spread, columns, near_chunks, far_chunks, shear_part, normal_part,
     weights, factors) = rest[-8:]
    if last:
        earlier, (shear_ref, normal_ref) = rest[:-10], rest[-10:-8]
    else:
        earlier, sums_ref = (), rest[-9]
    count_blocks = near_ref.shape[1]
    held_blocks = piece.shape[0]
    per_block = target.shape[1]
    per_chunks = per_block // LANES
    total_chunks = held_blocks * per_chunks
    me = me_ref[0]

    low = jnp.concatenate([piece[p, 6:7, 0:LANES] for p in range(held_blocks)], axis=0)
    high = jnp.concatenate([piece[p, 7:8, 0:LANES] for p in range(held_blocks)], axis=0)
    lane = lax.broadcasted_iota(jnp.int32, (1, LANES), 1)
    own_low, own_high = source[6:7, 0:LANES], source[7:8, 0:LANES]
    center = 0.5 * (own_low + own_high)
    is_axis = (lane == 0) | (lane == TURNS // 2) | (lane == TURNS)
    gap = jnp.max(jnp.where(lane <= TURNS, jnp.maximum(low - own_high, own_low - high), 0.0),
                  axis=1, keepdims=True)
    gap = jnp.maximum(gap, 0.0)

    def reach(low, high):
        out = jnp.maximum(jnp.abs(low - center), jnp.abs(high - center))
        return jnp.sqrt(jnp.sum(jnp.where(is_axis, out * out, 0.0), axis=1, keepdims=True))

    both = reach(low, high) + reach(own_low, own_high)
    is_near = (gap * gap + SMALLEST) * SPREAD_LIMIT < both * both
    nears = jnp.where(is_near, 1, 0)
    counts = low[:, COUNT_LANE:COUNT_LANE + 1].astype(jnp.int32)
    blocks = [(nears[p, 0], near_ref[0, block_at(first + p, me, count_blocks)],
               (counts[p, 0] + LANES - 1) // LANES) for p in range(held_blocks)]
    middle = [center[0:1, k:k + 1] for k in (0, TURNS // 2, TURNS)]

    def list_blocks(chunks, near, linked, start, unit):
        position = start
        for p, (is_near, is_linked, chunk_count) in enumerate(blocks):
            here = jnp.where((is_near == near) & (is_linked == linked), chunk_count, 0)

            def put(at, carry, p=p, position=position):
                chunks[position + at] = p * per_chunks + at
                return carry

            lax.fori_loop(0, here, put, 0)
            position = position + here
        rest = lax.rem(unit - lax.rem(position, unit), unit)

        def pad(at, carry):
            chunks[position + at] = total_chunks
            return carry

        lax.fori_loop(0, rest, pad, 0)
        return position + rest

    near_linked = list_blocks(near_chunks, 1, 1, 0, UNROLL)
    near_all = list_blocks(near_chunks, 1, 0, near_linked, UNROLL)
    far_linked = list_blocks(far_chunks, 0, 1, 0, WIDE)
    far_all = list_blocks(far_chunks, 0, 0, far_linked, WIDE)

    def chunk_of(chunk):
        real = jnp.minimum(chunk, total_chunks - 1)
        lo = pl.multiple_of(lax.rem(real, per_chunks) * LANES, LANES)
        held = piece[real // per_chunks, :, pl.ds(lo, LANES)]
        row = lax.broadcasted_iota(jnp.int32, (8, LANES), 0)
        blank = jnp.where(row == 3, 1.0, 0.0)
        return jnp.where((row >= 3) & (chunk == total_chunks), blank, held)

    def place_near(at, carry):
        for k in range(UNROLL):
            number = at * UNROLL + k
            held = chunk_of(near_chunks[number])
            for row in range(FIELDS):
                spread[number, row * 8:row * 8 + 8, :] = jnp.broadcast_to(
                    held[row:row + 1, :], (8, LANES))
        return carry

    lax.fori_loop(0, near_all // UNROLL, place_near, 0)

    def place_far(at, carry):
        for k in range(WIDE):
            number = at * WIDE + k
            pieces = three_pieces(source_features(chunk_of(far_chunks[number]), middle))
            lo = pl.multiple_of(number * LANES, LANES)
            for slot, which in enumerate(SOURCE_PIECES):
                weights[slot * FEATURES:(slot + 1) * FEATURES, pl.ds(lo, LANES)] = pieces[which]
        return carry

    lax.fori_loop(0, far_all // WIDE, place_far, 0)

    columns[...] = target[...].T
    own = target[...]
    zero_row = jnp.zeros((1, per_block), jnp.float32)
    ways = (None, (own[4:5], own[5:6], zero_row), (own[6:7], own[7:8], own[8:9]))
    for which, way in enumerate(ways):
        pieces = three_pieces(target_features(own, middle, way))
        stacked = jnp.concatenate(
            [pieces[k].astype(jnp.float32) for k in TARGET_PIECES]
            + [jnp.zeros((LANES - DEPTH, per_block), jnp.float32)], axis=0)
        factors[which, :, :] = stacked.T.astype(jnp.bfloat16)

    def group(number, carry):
        lo = pl.multiple_of(number * ROWS, ROWS)
        held = columns[pl.ds(lo, ROWS), :]

        def column(row):
            return [jnp.broadcast_to(held[8 * k:8 * k + 8, row:row + 1], (8, LANES))
                    for k in range(ROWS // 8)]

        places = list(zip(column(0), column(1), column(2), column(3)))
        zero = jnp.zeros((8, LANES), jnp.float32)

        def step(at, totals):
            totals = list(totals)
            for k in range(UNROLL):
                def field(row):
                    return spread[at * UNROLL + k, row * 8:row * 8 + 8, :]

                for sub in range(ROWS // 8):
                    totals[sub] = pair_sums(places[sub], field, totals[sub])
            return tuple(totals)

        start = tuple((zero,) * 5 for _ in range(ROWS // 8))
        linked = lax.fori_loop(0, near_linked // UNROLL, step, start)
        nx, ny, nz = column(6), column(7), column(8)
        for sub in range(ROWS // 8):
            ax, ay, bx, by, bz = linked[sub]
            normal_part[pl.ds(lo + 8 * sub, 8), :] = (
                nx[sub] * (ax - 3.0 * bx) + ny[sub] * (ay - 3.0 * by) - nz[sub] * (3.0 * bz))
        totals = lax.fori_loop(near_linked // UNROLL, near_all // UNROLL, step, linked)
        tx, ty = column(4), column(5)
        for sub in range(ROWS // 8):
            ax, ay, bx, by, bz = totals[sub]
            shear_part[pl.ds(lo + 8 * sub, 8), :] = (
                tx[sub] * (ax - 3.0 * bx) + ty[sub] * (ay - 3.0 * by))
        return carry

    lax.fori_loop(0, per_block // ROWS, group, 0)

    def far_step(with_normal, at, carry):
        lo = pl.multiple_of(at * WIDE * LANES, WIDE * LANES)
        sources = weights[:, pl.ds(lo, WIDE * LANES)]

        def product(which):
            return jnp.dot(factors[which, :, 0:DEPTH], sources,
                           preferred_element_type=jnp.float32)

        def add(part, terms):
            total = terms[:, 0:LANES]
            for k in range(1, WIDE):
                total = total + terms[:, k * LANES:(k + 1) * LANES]
            part[...] += total

        root = lax.rsqrt(product(0))
        inverse = root * root
        fourth = inverse * inverse
        add(shear_part, (product(1) * root) * fourth)
        if with_normal:
            add(normal_part, (product(2) * root) * fourth)
        return carry

    lax.fori_loop(0, far_linked // WIDE, functools.partial(far_step, True), 0)
    lax.fori_loop(far_linked // WIDE, far_all // WIDE, functools.partial(far_step, False), 0)

    ones = jnp.ones((8, LANES), jnp.float32)
    dims = (((1,), (1,)), ((), ()))
    for at, part in enumerate((shear_part, normal_part)):
        summed = lax.dot_general(ones, part[...], dims, precision=lax.Precision.HIGHEST,
                                 preferred_element_type=jnp.float32)[0:1, :]
        if last:
            for other in earlier:
                summed = summed + other[at:at + 1, :]
            (shear_ref, normal_ref)[at][...] = summed * own[9:10, :]
        else:
            sums_ref[at:at + 1, :] = summed


def body(centroid, angles, size, slip_rate, live_count, near):
    per_block = centroid.shape[1]
    count_blocks = near.shape[1]
    smem = pl.BlockSpec(memory_space=pltpu.SMEM)
    vmem = pl.BlockSpec(memory_space=pltpu.VMEM)
    source, target = pl.pallas_call(
        prep_kernel,
        out_shape=(jax.ShapeDtypeStruct((8, per_block), jnp.float32),
                   jax.ShapeDtypeStruct((16, per_block), jnp.float32)),
        in_specs=[smem] + [vmem] * 4,
        out_specs=(vmem, vmem),
    )(live_count, centroid, angles, size.reshape(1, per_block), slip_rate.reshape(1, per_block))
    me = lax.axis_index("blocks").astype(jnp.int32).reshape(1)

    def stage(piece, first, earlier, last):
        held_blocks = piece.shape[0]
        total_chunks = held_blocks * per_block // LANES
        row = jax.ShapeDtypeStruct((1, per_block), jnp.float32)
        pairs = per_block * per_block * held_blocks
        return pl.pallas_call(
            functools.partial(stage_kernel, first, last),
            out_shape=(row, row) if last else jax.ShapeDtypeStruct((8, per_block), jnp.float32),
            in_specs=[smem, smem] + [vmem] * (3 + len(earlier)),
            out_specs=(vmem, vmem) if last else vmem,
            scratch_shapes=[
                pltpu.VMEM((total_chunks + 2 * UNROLL, 8 * FIELDS, LANES), jnp.float32),
                pltpu.VMEM((per_block, 16), jnp.float32),
                pltpu.SMEM((total_chunks + 2 * UNROLL,), jnp.int32),
                pltpu.SMEM((total_chunks + 2 * WIDE,), jnp.int32),
                pltpu.VMEM((per_block, LANES), jnp.float32),
                pltpu.VMEM((per_block, LANES), jnp.float32),
                pltpu.VMEM((DEPTH, (total_chunks + 2 * WIDE) * LANES), jnp.bfloat16),
                pltpu.VMEM((3, per_block, LANES), jnp.bfloat16),
            ],
            compiler_params=pltpu.CompilerParams(vmem_limit_bytes=56 * 1024 * 1024),
            cost_estimate=pl.CostEstimate(flops=pairs * 2 * DEPTH * 4, bytes_accessed=pairs,
                                          transcendentals=pairs),
        )(me, near, source, piece, target, *earlier)

    held = source[None]
    fresh, first, sums = held, 0, []
    bit = count_blocks // 2
    while bit:
        swap = [(at, at ^ bit) for at in range(count_blocks)]
        coming = lax.ppermute(held, "blocks", swap)
        sums.append(stage(fresh, first, (), False))
        first = held.shape[0]
        held = jnp.concatenate([held, coming], axis=0) if bit > 1 else None
        fresh = coming
        bit //= 2
    shear, normal = stage(fresh, first, sums, True)
    return shear.reshape(per_block), normal.reshape(per_block)


def solution(mesh):
    in_specs = (
        P(None, ("runs", "blocks")),
        P(None, ("runs", "blocks")),
        P(("runs", "blocks")),
        P(("runs", "blocks")),
        P(("runs", "blocks")),
        P(("runs", "blocks"), None),
    )
    out_specs = (P(("runs", "blocks")), P(("runs", "blocks")))
    return jax.shard_map(body, mesh=mesh, in_specs=in_specs, out_specs=out_specs, check_vma=False)
```

```python
import functools
import math

import jax
import jax.numpy as jnp
from jax import lax
from jax.experimental import pallas as pl
from jax.experimental.pallas import tpu as pltpu
from jax.sharding import PartitionSpec as P

coupling = 0.002
LANES = 128
ROWS = 128
UNROLL = 2
FIELDS = 6
WIDE = 4
TALL = 128
TURNS = 64
COUNT_LANE = 127
BIG = 1e30
SMALLEST = 2e-6
SPREAD_LIMIT = 800.0
FEATURES = 16
SOURCE_PIECES = (0, 0, 1, 0, 2, 1)
TARGET_PIECES = (0, 1, 0, 2, 0, 1)
DEPTH = FEATURES * len(SOURCE_PIECES)


def prep_kernel(live_ref, centroid, angles, size, slip_rate, source_ref, target_ref):
    per_block = centroid.shape[1]
    count = live_ref[0]
    strike = angles[0:1, :]
    dip_angle = angles[1:2, :]
    cos_p, sin_p = jnp.cos(strike), jnp.sin(strike)
    cos_q, sin_q = jnp.cos(dip_angle), jnp.sin(dip_angle)
    is_live = lax.broadcasted_iota(jnp.int32, (1, per_block), 1) < count
    live = is_live.astype(jnp.float32)
    squared = size[...] * size[...]
    weight = slip_rate[...] * live * squared
    place = [jnp.where(is_live, centroid[k:k + 1, :], centroid[k:k + 1, 0:1]) for k in range(3)]
    for k in range(3):
        source_ref[k:k + 1, :] = place[k]
        target_ref[k:k + 1, :] = place[k]
    source_ref[3:4, :] = squared
    source_ref[4:5, :] = weight * cos_p
    source_ref[5:6, :] = weight * sin_p
    target_ref[3:4, :] = squared
    target_ref[4:5, :] = cos_p
    target_ref[5:6, :] = sin_p
    target_ref[6:7, :] = -sin_q * sin_p
    target_ref[7:8, :] = sin_q * cos_p
    target_ref[8:9, :] = cos_q
    target_ref[9:10, :] = live * coupling
    target_ref[10:16, :] = jnp.zeros((6, per_block), jnp.float32)
    turn = lax.broadcasted_iota(jnp.int32, (TURNS, 1), 0).astype(jnp.float32) * (math.pi / TURNS)
    along = jnp.cos(turn) * place[0] + jnp.sin(turn) * place[1]
    row = lax.broadcasted_iota(jnp.int32, (TURNS + 8, LANES), 0)
    lane = lax.broadcasted_iota(jnp.int32, (TURNS + 8, LANES), 1)
    all_rows = jnp.concatenate([along, jnp.broadcast_to(place[2], (8, per_block))], axis=0)
    for at, ends in ((6, jnp.min(all_rows, axis=1, keepdims=True)),
                     (7, jnp.max(all_rows, axis=1, keepdims=True))):
        line = jnp.sum(jnp.where(row == lane, ends, 0.0), axis=0, keepdims=True)
        line = jnp.where(lane[0:1, :] == COUNT_LANE, count.astype(jnp.float32), line)
        source_ref[at:at + 1, 0:LANES] = line
        source_ref[at:at + 1, LANES:] = jnp.zeros((1, per_block - LANES), jnp.float32)


def pair_sums(columns, field, totals):
    x, y, z, s2 = columns
    rx = x - field(0)
    ry = y - field(1)
    rz = z - field(2)
    d2 = (rx * rx + ry * ry) + (rz * rz + (s2 + field(3)))
    root = lax.rsqrt(d2)
    inverse = root * root
    cube = inverse * root
    ux, uy = field(4), field(5)
    bent = (cube * inverse) * (ux * rx + uy * ry)
    ax, ay, bx, by, bz = totals
    return (ax + cube * ux, ay + cube * uy, bx + bent * rx, by + bent * ry, bz + bent * rz)


def three_pieces(value):
    first = value.astype(jnp.bfloat16)
    rest = value - first.astype(jnp.float32)
    second = rest.astype(jnp.bfloat16)
    third = (rest - second.astype(jnp.float32)).astype(jnp.bfloat16)
    return first, second, third


def source_features(held, middle):
    x, y, z = (held[k:k + 1, :] - middle[k] for k in range(3))
    ux, uy = held[4:5, :], held[5:6, :]
    s = x * x + y * y + z * z + held[3:4, :]
    uxx, uxy, uxz, uyx, uyy, uyz = ux * x, ux * y, ux * z, uy * x, uy * y, uy * z
    along = uxx + uyy
    along3 = 3.0 * along
    return jnp.concatenate([
        jnp.ones_like(x), s, x, y, z, ux, uy, uxx, uxy, uxz, uyx, uyy, uyz,
        s * ux - along3 * x, s * uy - along3 * y, z * along], axis=0)


def target_features(held, middle, direction):
    x, y, z = (held[k:k + 1, :] - middle[k] for k in range(3))
    r = x * x + y * y + z * z + held[3:4, :]
    zero, one = jnp.zeros_like(x), jnp.ones_like(x)
    if direction is None:
        return jnp.concatenate([r, one, -2.0 * x, -2.0 * y, -2.0 * z] + [zero] * 11, axis=0)
    a, b, c = direction
    t3 = 3.0 * (a * x + b * y + c * z)
    return jnp.concatenate([
        zero, zero, zero, zero, zero, r * a - t3 * x, r * b - t3 * y,
        a * x + t3, 3.0 * b * x - 2.0 * a * y, 3.0 * c * x - 2.0 * a * z,
        3.0 * a * y - 2.0 * b * x, b * y + t3, 3.0 * c * y - 2.0 * b * z,
        a, b, -3.0 * c], axis=0)


def exchanges(count_blocks):
    bits = [1 << at for at in range(count_blocks.bit_length() - 1)]
    return bits[:1] + bits[:0:-1]


def block_at(position, me, count_blocks):
    flipped = 0
    for at, bit in enumerate(exchanges(count_blocks)):
        if position >> at & 1:
            flipped |= bit
    return me ^ flipped


def stage_kernel(first, last, me_ref, near_ref, source, piece, target, *rest):
    (spread, columns, near_chunks, far_chunks, shear_part, normal_part,
     weights, factors) = rest[-8:]
    if last:
        earlier, (shear_ref, normal_ref) = rest[:-10], rest[-10:-8]
    else:
        earlier, sums_ref = (), rest[-9]
    count_blocks = near_ref.shape[1]
    held_blocks = piece.shape[0]
    per_block = target.shape[1]
    per_chunks = per_block // LANES
    total_chunks = held_blocks * per_chunks
    me = me_ref[0]

    low = jnp.concatenate([piece[p, 6:7, 0:LANES] for p in range(held_blocks)], axis=0)
    high = jnp.concatenate([piece[p, 7:8, 0:LANES] for p in range(held_blocks)], axis=0)
    lane = lax.broadcasted_iota(jnp.int32, (1, LANES), 1)
    own_low, own_high = source[6:7, 0:LANES], source[7:8, 0:LANES]
    center = 0.5 * (own_low + own_high)
    is_axis = (lane == 0) | (lane == TURNS // 2) | (lane == TURNS)
    gap = jnp.max(jnp.where(lane <= TURNS, jnp.maximum(low - own_high, own_low - high), 0.0),
                  axis=1, keepdims=True)
    gap = jnp.maximum(gap, 0.0)

    def reach(low, high):
        out = jnp.maximum(jnp.abs(low - center), jnp.abs(high - center))
        return jnp.sqrt(jnp.sum(jnp.where(is_axis, out * out, 0.0), axis=1, keepdims=True))

    both = reach(low, high) + reach(own_low, own_high)
    is_near = (gap * gap + SMALLEST) * SPREAD_LIMIT < both * both
    nears = jnp.where(is_near, 1, 0)
    counts = low[:, COUNT_LANE:COUNT_LANE + 1].astype(jnp.int32)
    blocks = [(nears[p, 0], near_ref[0, block_at(first + p, me, count_blocks)],
               (counts[p, 0] + LANES - 1) // LANES) for p in range(held_blocks)]
    middle = [center[0:1, k:k + 1] for k in (0, TURNS // 2, TURNS)]

    def list_blocks(chunks, near, linked, start, unit):
        position = start
        for p, (is_near, is_linked, chunk_count) in enumerate(blocks):
            here = jnp.where((is_near == near) & (is_linked == linked), chunk_count, 0)

            def put(at, carry, p=p, position=position):
                chunks[position + at] = p * per_chunks + at
                return carry

            lax.fori_loop(0, here, put, 0)
            position = position + here
        rest = lax.rem(unit - lax.rem(position, unit), unit)

        def pad(at, carry):
            chunks[position + at] = total_chunks
            return carry

        lax.fori_loop(0, rest, pad, 0)
        return position + rest

    near_linked = list_blocks(near_chunks, 1, 1, 0, UNROLL)
    near_all = list_blocks(near_chunks, 1, 0, near_linked, UNROLL)
    far_linked = list_blocks(far_chunks, 0, 1, 0, WIDE)
    far_all = list_blocks(far_chunks, 0, 0, far_linked, WIDE)

    def chunk_of(chunk):
        real = jnp.minimum(chunk, total_chunks - 1)
        lo = pl.multiple_of(lax.rem(real, per_chunks) * LANES, LANES)
        held = piece[real // per_chunks, :, pl.ds(lo, LANES)]
        row = lax.broadcasted_iota(jnp.int32, (8, LANES), 0)
        blank = jnp.where(row == 3, 1.0, 0.0)
        return jnp.where((row >= 3) & (chunk == total_chunks), blank, held)

    def place_near(at, carry):
        for k in range(UNROLL):
            number = at * UNROLL + k
            held = chunk_of(near_chunks[number])
            for row in range(FIELDS):
                spread[number, row * 8:row * 8 + 8, :] = jnp.broadcast_to(
                    held[row:row + 1, :], (8, LANES))
        return carry

    lax.fori_loop(0, near_all // UNROLL, place_near, 0)

    def place_far(at, carry):
        for k in range(WIDE):
            number = at * WIDE + k
            pieces = three_pieces(source_features(chunk_of(far_chunks[number]), middle))
            lo = pl.multiple_of(number * LANES, LANES)
            for slot, which in enumerate(SOURCE_PIECES):
                weights[slot * FEATURES:(slot + 1) * FEATURES, pl.ds(lo, LANES)] = pieces[which]
        return carry

    lax.fori_loop(0, far_all // WIDE, place_far, 0)

    columns[...] = target[...].T
    own = target[...]
    zero_row = jnp.zeros((1, per_block), jnp.float32)
    ways = (None, (own[4:5], own[5:6], zero_row), (own[6:7], own[7:8], own[8:9]))
    for which, way in enumerate(ways):
        pieces = three_pieces(target_features(own, middle, way))
        stacked = jnp.concatenate(
            [pieces[k].astype(jnp.float32) for k in TARGET_PIECES]
            + [jnp.zeros((LANES - DEPTH, per_block), jnp.float32)], axis=0)
        factors[which, :, :] = stacked.T.astype(jnp.bfloat16)

    def group(number, carry):
        lo = pl.multiple_of(number * ROWS, ROWS)
        held = columns[pl.ds(lo, ROWS), :]

        def column(row):
            return [jnp.broadcast_to(held[8 * k:8 * k + 8, row:row + 1], (8, LANES))
                    for k in range(ROWS // 8)]

        places = list(zip(column(0), column(1), column(2), column(3)))
        zero = jnp.zeros((8, LANES), jnp.float32)

        def step(at, totals):
            totals = list(totals)
            for k in range(UNROLL):
                def field(row):
                    return spread[at * UNROLL + k, row * 8:row * 8 + 8, :]

                for sub in range(ROWS // 8):
                    totals[sub] = pair_sums(places[sub], field, totals[sub])
            return tuple(totals)

        start = tuple((zero,) * 5 for _ in range(ROWS // 8))
        linked = lax.fori_loop(0, near_linked // UNROLL, step, start)
        nx, ny, nz = column(6), column(7), column(8)
        for sub in range(ROWS // 8):
            ax, ay, bx, by, bz = linked[sub]
            normal_part[pl.ds(lo + 8 * sub, 8), :] = (
                nx[sub] * (ax - 3.0 * bx) + ny[sub] * (ay - 3.0 * by) - nz[sub] * (3.0 * bz))
        totals = lax.fori_loop(near_linked // UNROLL, near_all // UNROLL, step, linked)
        tx, ty = column(4), column(5)
        for sub in range(ROWS // 8):
            ax, ay, bx, by, bz = totals[sub]
            shear_part[pl.ds(lo + 8 * sub, 8), :] = (
                tx[sub] * (ax - 3.0 * bx) + ty[sub] * (ay - 3.0 * by))
        return carry

    @pl.when(near_all > 0)
    def near_blocks():
        lax.fori_loop(0, per_block // ROWS, group, 0)

    @pl.when(near_all == 0)
    def no_near_blocks():
        shear_part[...] = jnp.zeros_like(shear_part)
        normal_part[...] = jnp.zeros_like(normal_part)

    def far_step(with_normal, at, carry):
        lo = pl.multiple_of(at * WIDE * LANES, WIDE * LANES)
        sources = weights[:, pl.ds(lo, WIDE * LANES)]

        for top in range(0, per_block, TALL):
            def product(which):
                return jnp.dot(factors[which, top:top + TALL, 0:DEPTH], sources,
                               preferred_element_type=jnp.float32)

            def add(part, terms):
                total = terms[:, 0:LANES]
                for k in range(1, WIDE):
                    total = total + terms[:, k * LANES:(k + 1) * LANES]
                part[top:top + TALL, :] += total

            root = lax.rsqrt(product(0))
            inverse = root * root
            fourth = inverse * inverse
            add(shear_part, (product(1) * root) * fourth)
            if with_normal:
                add(normal_part, (product(2) * root) * fourth)
        return carry

    lax.fori_loop(0, far_linked // WIDE, functools.partial(far_step, True), 0)
    lax.fori_loop(far_linked // WIDE, far_all // WIDE, functools.partial(far_step, False), 0)

    ones = jnp.ones((8, LANES), jnp.bfloat16)
    dims = (((1,), (1,)), ((), ()))
    for at, part in enumerate((shear_part, normal_part)):
        first_sum, second_sum, third_sum = (
            lax.dot_general(ones, piece_of, dims, preferred_element_type=jnp.float32)[0:1, :]
            for piece_of in three_pieces(part[...]))
        summed = first_sum + (second_sum + third_sum)
        if last:
            for other in earlier:
                summed = summed + other[at:at + 1, :]
            (shear_ref, normal_ref)[at][...] = summed * own[9:10, :]
        else:
            sums_ref[at:at + 1, :] = summed


def body(centroid, angles, size, slip_rate, live_count, near):
    per_block = centroid.shape[1]
    count_blocks = near.shape[1]
    smem = pl.BlockSpec(memory_space=pltpu.SMEM)
    vmem = pl.BlockSpec(memory_space=pltpu.VMEM)
    source, target = pl.pallas_call(
        prep_kernel,
        out_shape=(jax.ShapeDtypeStruct((8, per_block), jnp.float32),
                   jax.ShapeDtypeStruct((16, per_block), jnp.float32)),
        in_specs=[smem] + [vmem] * 4,
        out_specs=(vmem, vmem),
    )(live_count, centroid, angles, size.reshape(1, per_block), slip_rate.reshape(1, per_block))
    me = lax.axis_index("blocks").astype(jnp.int32).reshape(1)

    def stage(piece, first, earlier, last):
        held_blocks = piece.shape[0]
        total_chunks = held_blocks * per_block // LANES
        row = jax.ShapeDtypeStruct((1, per_block), jnp.float32)
        pairs = per_block * per_block * held_blocks
        return pl.pallas_call(
            functools.partial(stage_kernel, first, last),
            out_shape=(row, row) if last else jax.ShapeDtypeStruct((8, per_block), jnp.float32),
            in_specs=[smem, smem] + [vmem] * (3 + len(earlier)),
            out_specs=(vmem, vmem) if last else vmem,
            scratch_shapes=[
                pltpu.VMEM((total_chunks + 2 * UNROLL, 8 * FIELDS, LANES), jnp.float32),
                pltpu.VMEM((per_block, 16), jnp.float32),
                pltpu.SMEM((total_chunks + 2 * UNROLL,), jnp.int32),
                pltpu.SMEM((total_chunks + 2 * WIDE,), jnp.int32),
                pltpu.VMEM((per_block, LANES), jnp.float32),
                pltpu.VMEM((per_block, LANES), jnp.float32),
                pltpu.VMEM((DEPTH, (total_chunks + 2 * WIDE) * LANES), jnp.bfloat16),
                pltpu.VMEM((3, per_block, LANES), jnp.bfloat16),
            ],
            compiler_params=pltpu.CompilerParams(vmem_limit_bytes=56 * 1024 * 1024),
            cost_estimate=pl.CostEstimate(flops=pairs * 2 * DEPTH * 4, bytes_accessed=pairs,
                                          transcendentals=pairs),
        )(me, near, source, piece, target, *earlier)

    bits = exchanges(count_blocks)
    held, fresh, first, sums = source[None], None, 0, []
    for at, bit in enumerate(bits):
        swap = [(one, one ^ bit) for one in range(count_blocks)]
        coming = lax.ppermute(held, "blocks", swap)
        if at:
            sums.append(stage(fresh, first, (), False))
            first = held.shape[0]
        if at < len(bits) - 1:
            held = jnp.concatenate([held, coming], axis=0)
        fresh = coming if at else held
    shear, normal = stage(fresh, first, sums, True)
    return shear.reshape(per_block), normal.reshape(per_block)


def solution(mesh):
    in_specs = (
        P(None, ("runs", "blocks")),
        P(None, ("runs", "blocks")),
        P(("runs", "blocks")),
        P(("runs", "blocks")),
        P(("runs", "blocks")),
        P(("runs", "blocks"), None),
    )
    out_specs = (P(("runs", "blocks")), P(("runs", "blocks")))
    return jax.shard_map(body, mesh=mesh, in_specs=in_specs, out_specs=out_specs, check_vma=False)
```

```python
import functools
import math

import jax
import jax.numpy as jnp
from jax import lax
from jax.experimental import pallas as pl
from jax.experimental.pallas import tpu as pltpu
from jax.sharding import PartitionSpec as P

coupling = 0.002
LANES = 128
FIELDS = 6
FRAME = 9
WIDE = 4
TALL = 128
TURNS = 64
COUNT_LANE = 127
BIG = 1e15
SMALLEST = 2e-6
SPREAD_LIMIT = 800.0
FEATURES = 16
SOURCE_PIECES = (0, 0, 1, 0, 2, 1)
TARGET_PIECES = (0, 1, 0, 2, 0, 1)
DEPTH = FEATURES * len(SOURCE_PIECES)


def three_pieces(value):
    first = value.astype(jnp.bfloat16)
    rest = value - first.astype(jnp.float32)
    second = rest.astype(jnp.bfloat16)
    third = (rest - second.astype(jnp.float32)).astype(jnp.bfloat16)
    return first, second, third


def ranks(key_row):
    per_block = key_row.shape[1]
    key_column = jnp.broadcast_to(key_row, (8, per_block)).T[:, 0:1]
    slot = lax.broadcasted_iota(jnp.int32, (LANES, per_block), 1)
    total = jnp.zeros((1, per_block), jnp.float32)
    for top in range(0, per_block, LANES):
        other = key_column[top:top + LANES, :]
        earlier = lax.broadcasted_iota(jnp.int32, (LANES, per_block), 0) + top < slot
        before = (other < key_row) | ((other == key_row) & earlier)
        total = total + jnp.sum(jnp.where(before, 1.0, 0.0), axis=0, keepdims=True)
    return total


def prep_kernel(live_ref, centroid, angles, size, slip_rate, source_ref, target_ref):
    per_block = centroid.shape[1]
    count = live_ref[0]
    strike = angles[0:1, :]
    dip_angle = angles[1:2, :]
    cos_p, sin_p = jnp.cos(strike), jnp.sin(strike)
    cos_q, sin_q = jnp.cos(dip_angle), jnp.sin(dip_angle)
    lane = lax.broadcasted_iota(jnp.int32, (1, per_block), 1)
    live = lane < count
    squared = size[...] * size[...]
    weight = slip_rate[...] * squared
    place = [centroid[k:k + 1, :] for k in range(3)]

    extent = [jnp.max(jnp.where(live, row, -BIG), axis=1, keepdims=True)
              - jnp.min(jnp.where(live, row, BIG), axis=1, keepdims=True) for row in place]
    key = jnp.where((extent[0] >= extent[1]) & (extent[0] >= extent[2]), place[0],
                    jnp.where(extent[1] >= extent[2], place[1], place[2]))
    rank = ranks(jnp.where(live, key, BIG))
    rank_column = jnp.broadcast_to(rank, (8, per_block)).T[:, 0:1]

    zero = jnp.zeros((5, per_block), jnp.float32)
    rows = jnp.concatenate(place + [squared, weight * cos_p, weight * sin_p, cos_p, sin_p,
                                    -sin_q * sin_p, sin_q * cos_p, cos_q, zero], axis=0)
    pieces = jnp.concatenate(three_pieces(rows), axis=0)
    step = math.gcd(per_block, 256)
    parts = []
    for at in range(0, per_block, step):
        wanted = jnp.minimum(lax.broadcasted_iota(jnp.int32, (1, step), 1) + at, count - 1)
        pick = jnp.where(rank_column == wanted.astype(jnp.float32), 1.0, 0.0).astype(jnp.bfloat16)
        three = jnp.dot(pieces, pick, preferred_element_type=jnp.float32)
        parts.append(three[0:16, :] + (three[16:32, :] + three[32:48, :]))
    ordered = jnp.concatenate(parts, axis=1)

    source_ref[0:4, :] = ordered[0:4, :]
    source_ref[4:6, :] = jnp.where(live, ordered[4:6, :], 0.0)
    target_ref[0:4, :] = ordered[0:4, :]
    target_ref[4:9, :] = ordered[6:11, :]
    target_ref[9:10, :] = jnp.where(live, coupling, 0.0)
    target_ref[10:11, :] = rank
    target_ref[11:16, :] = zero

    turn = lax.broadcasted_iota(jnp.int32, (TURNS, 1), 0).astype(jnp.float32) * (math.pi / TURNS)
    along = jnp.cos(turn) * ordered[0:1, :] + jnp.sin(turn) * ordered[1:2, :]
    all_rows = jnp.concatenate([along, jnp.broadcast_to(ordered[2:3, :], (8, per_block))], axis=0)
    row = lax.broadcasted_iota(jnp.int32, (TURNS + 8, LANES), 0)
    column = lax.broadcasted_iota(jnp.int32, (TURNS + 8, LANES), 1)
    for lo in range(0, per_block, LANES):
        here = all_rows[:, lo:lo + LANES]
        used = live[:, lo:lo + LANES]
        for at, ends in ((6, jnp.min(jnp.where(used, here, BIG), axis=1, keepdims=True)),
                         (7, jnp.max(jnp.where(used, here, -BIG), axis=1, keepdims=True))):
            line = jnp.sum(jnp.where(row == column, ends, 0.0), axis=0, keepdims=True)
            line = jnp.where(column[0:1, :] == COUNT_LANE, count.astype(jnp.float32), line)
            source_ref[at:at + 1, lo:lo + LANES] = line


def pair_sums(columns, field):
    x, y, z, s2 = columns
    rx = x - field(0)
    ry = y - field(1)
    rz = z - field(2)
    d2 = (rx * rx + ry * ry) + (rz * rz + (s2 + field(3)))
    root = lax.rsqrt(d2)
    inverse = root * root
    cube = inverse * root
    ux, uy = field(4), field(5)
    bent = (cube * inverse) * (ux * rx + uy * ry)
    bent = 3.0 * bent
    return cube * ux - bent * rx, cube * uy - bent * ry, -bent * rz


def source_features(held, middle):
    x, y, z = (held[k:k + 1, :] - middle[k] for k in range(3))
    ux, uy = held[4:5, :], held[5:6, :]
    s = x * x + y * y + z * z + held[3:4, :]
    uxx, uxy, uxz, uyx, uyy, uyz = ux * x, ux * y, ux * z, uy * x, uy * y, uy * z
    along = uxx + uyy
    along3 = 3.0 * along
    return jnp.concatenate([
        jnp.ones_like(x), s, x, y, z, ux, uy, uxx, uxy, uxz, uyx, uyy, uyz,
        s * ux - along3 * x, s * uy - along3 * y, z * along], axis=0)


def target_features(held, middle, direction):
    x, y, z = (held[k:k + 1, :] - middle[k] for k in range(3))
    r = x * x + y * y + z * z + held[3:4, :]
    zero, one = jnp.zeros_like(x), jnp.ones_like(x)
    if direction is None:
        return jnp.concatenate([r, one, -2.0 * x, -2.0 * y, -2.0 * z] + [zero] * 11, axis=0)
    a, b, c = direction
    t3 = 3.0 * (a * x + b * y + c * z)
    return jnp.concatenate([
        zero, zero, zero, zero, zero, r * a - t3 * x, r * b - t3 * y,
        a * x + t3, 3.0 * b * x - 2.0 * a * y, 3.0 * c * x - 2.0 * a * z,
        3.0 * a * y - 2.0 * b * x, b * y + t3, 3.0 * c * y - 2.0 * b * z,
        a, b, -3.0 * c], axis=0)


def exchanges(count_blocks):
    bits = [1 << at for at in range(count_blocks.bit_length() - 1)]
    return bits[:1] + bits[:0:-1]


def block_at(position, me, count_blocks):
    flipped = 0
    for at, bit in enumerate(exchanges(count_blocks)):
        if position >> at & 1:
            flipped |= bit
    return me ^ flipped


def stage_kernel(first, last, me_ref, near_ref, source, piece, target, *rest):
    (columns, near_list, far_chunks, far_marks, counters, shear_part, normal_part,
     weights, factors) = rest[-9:]
    if last:
        earlier, (shear_ref, normal_ref) = rest[:-11], rest[-11:-9]
    else:
        earlier, sums_ref = (), rest[-10]
    count_blocks = near_ref.shape[1]
    held_blocks = piece.shape[0]
    per_block = target.shape[1]
    per_chunks = per_block // LANES
    total_chunks = held_blocks * per_chunks
    me = me_ref[0]

    def runs(ref, at):
        return jnp.concatenate([ref[at:at + 1, t * LANES:(t + 1) * LANES]
                                for t in range(per_chunks)], axis=0)

    low = jnp.concatenate([runs(piece.at[p], 6) for p in range(held_blocks)], axis=0)
    high = jnp.concatenate([runs(piece.at[p], 7) for p in range(held_blocks)], axis=0)
    own_low, own_high = runs(source, 6), runs(source, 7)
    lane = lax.broadcasted_iota(jnp.int32, (1, LANES), 1)
    center = 0.5 * (jnp.min(own_low, axis=0, keepdims=True)
                    + jnp.max(own_high, axis=0, keepdims=True))
    is_axis = (lane == 0) | (lane == TURNS // 2) | (lane == TURNS)

    def reach(low, high):
        out = jnp.maximum(jnp.abs(low - center), jnp.abs(high - center))
        return jnp.sqrt(jnp.sum(jnp.where(is_axis, out * out, 0.0), axis=1, keepdims=True))

    source_reach, own_reach = reach(low, high), reach(own_low, own_high)
    marks = jnp.zeros((total_chunks, 1), jnp.int32)
    for t in range(per_chunks):
        apart = jnp.maximum(low - own_high[t:t + 1, :], own_low[t:t + 1, :] - high)
        gap = jnp.max(jnp.where(lane <= TURNS, apart, 0.0), axis=1, keepdims=True)
        gap = jnp.maximum(gap, 0.0)
        both = source_reach + own_reach[t:t + 1, :]
        is_near = (gap * gap + SMALLEST) * SPREAD_LIMIT < both * both
        marks = marks + jnp.where(is_near, 1 << t, 0)
    middle = [center[0:1, k:k + 1] for k in (0, TURNS // 2, TURNS)]
    blocks = []
    for p in range(held_blocks):
        top = p * per_chunks
        held = marks[top:top + per_chunks, :]
        count = low[top, COUNT_LANE].astype(jnp.int32)
        blocks.append((held, jnp.max(held), (count + LANES - 1) // LANES,
                       near_ref[0, block_at(first + p, me, count_blocks)]))

    def pad(chunks, position):
        rest = lax.rem(WIDE - lax.rem(position, WIDE), WIDE)

        def put(at, carry):
            chunks[position + at] = total_chunks
            far_marks[position + at] = 0
            return carry

        lax.fori_loop(0, rest, put, 0)
        return position + rest

    counters[0] = 0
    counters[1] = 0
    for p, (held, any_near, chunk_count, linked) in enumerate(blocks):
        @pl.when(any_near > 0)
        def near_block(p=p, held=held, chunk_count=chunk_count, linked=linked):
            pairs, position = counters[0], counters[1]
            for t in range(per_chunks):
                chunk = p * per_chunks + t
                mark = jnp.where(t < chunk_count, held[t, 0], 0)
                far_chunks[position + t] = chunk
                far_marks[position + t] = mark * 2 + linked
                for run in range(per_chunks):
                    near_list[pairs] = (chunk * per_chunks + run) * 2 + linked
                    pairs = pairs + (lax.shift_right_logical(mark, run) & 1)
            counters[0] = pairs
            counters[1] = position + chunk_count

    near_pairs = counters[0]
    mixed_end = pad(far_chunks, counters[1])

    def list_blocks(wanted, start):
        position = start
        for p, (_, any_near, chunk_count, linked) in enumerate(blocks):
            here = jnp.where((any_near == 0) & (linked == wanted), chunk_count, 0)

            def put(at, carry, p=p, position=position):
                far_chunks[position + at] = p * per_chunks + at
                return carry

            lax.fori_loop(0, here, put, 0)
            position = position + here
        return pad(far_chunks, position)

    far_linked = list_blocks(1, mixed_end)
    far_all = list_blocks(0, far_linked)

    def chunk_of(chunk):
        real = jnp.minimum(chunk, total_chunks - 1)
        lo = pl.multiple_of(lax.rem(real, per_chunks) * LANES, LANES)
        held = piece[real // per_chunks, :, pl.ds(lo, LANES)]
        row = lax.broadcasted_iota(jnp.int32, (8, LANES), 0)
        blank = jnp.where(row == 3, 1.0, 0.0)
        return jnp.where((row >= 3) & (chunk == total_chunks), blank, held)

    def place_far(at, carry):
        for k in range(WIDE):
            number = at * WIDE + k
            pieces = three_pieces(source_features(chunk_of(far_chunks[number]), middle))
            lo = pl.multiple_of(number * LANES, LANES)
            for slot, which in enumerate(SOURCE_PIECES):
                weights[slot * FEATURES:(slot + 1) * FEATURES, pl.ds(lo, LANES)] = pieces[which]
        return carry

    lax.fori_loop(0, far_all // WIDE, place_far, 0)

    own = target[...]
    zero_row = jnp.zeros((1, per_block), jnp.float32)
    ways = (None, (own[4:5], own[5:6], zero_row), (own[6:7], own[7:8], own[8:9]))
    for which, way in enumerate(ways):
        pieces = three_pieces(target_features(own, middle, way))
        stacked = jnp.concatenate(
            [pieces[k].astype(jnp.float32) for k in TARGET_PIECES]
            + [jnp.zeros((LANES - DEPTH, per_block), jnp.float32)], axis=0)
        factors[which, :, :] = stacked.T.astype(jnp.bfloat16)

    shear_part[...] = jnp.zeros_like(shear_part)
    normal_part[...] = jnp.zeros_like(normal_part)

    @pl.when(near_pairs > 0)
    def spread_columns():
        turned = own.T
        for row in range(FRAME):
            columns[row, :, :] = jnp.broadcast_to(turned[:, row:row + 1], (per_block, LANES))

    def near_step(at, carry):
        code = near_list[at]
        linked = (code & 1) == 1
        run = lax.shift_right_logical(code, 1) & (per_chunks - 1)
        chunk = lax.shift_right_logical(code, 1) // per_chunks
        held = piece[chunk // per_chunks, :,
                     pl.ds(pl.multiple_of(lax.rem(chunk, per_chunks) * LANES, LANES), LANES)]
        fields = [jnp.broadcast_to(held[row:row + 1, :], (8, LANES)) for row in range(FIELDS)]
        for sub in range(LANES // 8):
            rows = pl.ds(pl.multiple_of(run * LANES + 8 * sub, 8), 8)
            x, y, z, s2, tx, ty, nx, ny, nz = (columns[row, rows, :] for row in range(FRAME))
            fx, fy, fz = pair_sums((x, y, z, s2), fields.__getitem__)
            shear_part[rows, :] += tx * fx + ty * fy
            normal_part[rows, :] += jnp.where(linked, nx * fx + ny * fy + nz * fz, 0.0)
        return carry

    lax.fori_loop(0, near_pairs, near_step, 0)

    def far_step(with_normal, mixed, at, carry):
        lo = pl.multiple_of(at * WIDE * LANES, WIDE * LANES)
        sources = weights[:, pl.ds(lo, WIDE * LANES)]

        held_marks = [far_marks[at * WIDE + k] for k in range(WIDE)] if mixed else None
        for top in range(0, per_block, TALL):
            def product(which):
                return jnp.dot(factors[which, top:top + TALL, 0:DEPTH], sources,
                               preferred_element_type=jnp.float32)

            def add(part, terms, linked_only):
                total = None
                for k in range(WIDE):
                    term = terms[:, k * LANES:(k + 1) * LANES]
                    if mixed:
                        mark = held_marks[k]
                        keep = (lax.shift_right_logical(mark, top // TALL + 1) & 1) == 0
                        if linked_only:
                            keep = keep & ((mark & 1) == 1)
                        term = jnp.where(keep, term, 0.0)
                    total = term if total is None else total + term
                part[top:top + TALL, :] += total

            root = lax.rsqrt(product(0))
            inverse = root * root
            fourth = inverse * inverse
            add(shear_part, (product(1) * root) * fourth, False)
            if with_normal:
                add(normal_part, (product(2) * root) * fourth, True)
        return carry

    ends = (0, mixed_end // WIDE, far_linked // WIDE, far_all // WIDE)
    for kind, way in enumerate(((True, True), (True, False), (False, False))):
        lax.fori_loop(ends[kind], ends[kind + 1], functools.partial(far_step, *way), 0)

    ones = jnp.ones((8, LANES), jnp.bfloat16)
    dims = (((1,), (1,)), ((), ()))
    sums = []
    for at, part in enumerate((shear_part, normal_part)):
        first_sum, second_sum, third_sum = (
            lax.dot_general(ones, piece_of, dims, preferred_element_type=jnp.float32)[0:1, :]
            for piece_of in three_pieces(part[...]))
        summed = first_sum + (second_sum + third_sum)
        for other in earlier:
            summed = summed + other[at:at + 1, :]
        sums.append(summed)
    if not last:
        for at in range(2):
            sums_ref[at:at + 1, :] = sums[at]
        return
    both = jnp.concatenate([jnp.where(own[9:10, :] > 0.0, one * own[9:10, :], 0.0) for one in sums]
                           + [jnp.zeros((14, per_block), jnp.float32)], axis=0)
    pieces = jnp.concatenate(three_pieces(both), axis=0)
    step = math.gcd(per_block, 256)
    slot = lax.broadcasted_iota(jnp.int32, (per_block, 1), 0).astype(jnp.float32)
    for at in range(0, per_block, step):
        pick = jnp.where(slot == own[10:11, at:at + step], 1.0, 0.0).astype(jnp.bfloat16)
        three = jnp.dot(pieces, pick, preferred_element_type=jnp.float32)
        back = three[0:16, :] + (three[16:32, :] + three[32:48, :])
        shear_ref[:, at:at + step] = back[0:1, :]
        normal_ref[:, at:at + step] = back[1:2, :]


def body(centroid, angles, size, slip_rate, live_count, near):
    per_block = centroid.shape[1]
    count_blocks = near.shape[1]
    smem = pl.BlockSpec(memory_space=pltpu.SMEM)
    vmem = pl.BlockSpec(memory_space=pltpu.VMEM)
    source, target = pl.pallas_call(
        prep_kernel,
        out_shape=(jax.ShapeDtypeStruct((8, per_block), jnp.float32),
                   jax.ShapeDtypeStruct((16, per_block), jnp.float32)),
        in_specs=[smem] + [vmem] * 4,
        out_specs=(vmem, vmem),
    )(live_count, centroid, angles, size.reshape(1, per_block), slip_rate.reshape(1, per_block))
    me = lax.axis_index("blocks").astype(jnp.int32).reshape(1)

    def stage(piece, first, earlier, last):
        held_blocks = piece.shape[0]
        total_chunks = held_blocks * per_block // LANES
        row = jax.ShapeDtypeStruct((1, per_block), jnp.float32)
        pairs = per_block * per_block * held_blocks
        return pl.pallas_call(
            functools.partial(stage_kernel, first, last),
            out_shape=(row, row) if last else jax.ShapeDtypeStruct((8, per_block), jnp.float32),
            in_specs=[smem, smem] + [vmem] * (3 + len(earlier)),
            out_specs=(vmem, vmem) if last else vmem,
            scratch_shapes=[
                pltpu.VMEM((FRAME, per_block, LANES), jnp.float32),
                pltpu.SMEM((total_chunks * (per_block // LANES) + 8,), jnp.int32),
                pltpu.SMEM((total_chunks + per_block // LANES + 3 * WIDE,), jnp.int32),
                pltpu.SMEM((total_chunks + per_block // LANES + 3 * WIDE,), jnp.int32),
                pltpu.SMEM((2,), jnp.int32),
                pltpu.VMEM((per_block, LANES), jnp.float32),
                pltpu.VMEM((per_block, LANES), jnp.float32),
                pltpu.VMEM((DEPTH, (total_chunks + 3 * WIDE) * LANES), jnp.bfloat16),
                pltpu.VMEM((3, per_block, LANES), jnp.bfloat16),
            ],
            compiler_params=pltpu.CompilerParams(vmem_limit_bytes=56 * 1024 * 1024),
            cost_estimate=pl.CostEstimate(flops=pairs * 2 * DEPTH * 4, bytes_accessed=pairs,
                                          transcendentals=pairs),
        )(me, near, source, piece, target, *earlier)

    bits = exchanges(count_blocks)
    held, fresh, first, sums = source[None], None, 0, []
    for at, bit in enumerate(bits):
        swap = [(one, one ^ bit) for one in range(count_blocks)]
        coming = lax.ppermute(held, "blocks", swap)
        if at:
            sums.append(stage(fresh, first, (), False))
            first = held.shape[0]
        if at < len(bits) - 1:
            held = jnp.concatenate([held, coming], axis=0)
        fresh = coming if at else held
    shear, normal = stage(fresh, first, sums, True)
    return shear.reshape(per_block), normal.reshape(per_block)


def solution(mesh):
    in_specs = (
        P(None, ("runs", "blocks")),
        P(None, ("runs", "blocks")),
        P(("runs", "blocks")),
        P(("runs", "blocks")),
        P(("runs", "blocks")),
        P(("runs", "blocks"), None),
    )
    out_specs = (P(("runs", "blocks")), P(("runs", "blocks")))
    return jax.shard_map(body, mesh=mesh, in_specs=in_specs, out_specs=out_specs, check_vma=False)
```

```python
import functools
import math

import jax
import jax.numpy as jnp
from jax import lax
from jax.experimental import pallas as pl
from jax.experimental.pallas import tpu as pltpu
from jax.sharding import PartitionSpec as P

coupling = 0.002
LANES = 128
FIELDS = 6
FRAME = 9
WIDE = 4
PAIRS = 2
TALL = 128
TURNS = 64
COUNT_LANE = 127
BIG = 1e15
SMALLEST = 2e-6
SPREAD_LIMIT = 1500.0
FEATURES = 16
SOURCE_PIECES = (0, 0, 1, 0, 2, 1)
TARGET_PIECES = (0, 1, 0, 2, 0, 1)
DEPTH = FEATURES * len(SOURCE_PIECES)


def three_pieces(value):
    first = value.astype(jnp.bfloat16)
    rest = value - first.astype(jnp.float32)
    second = rest.astype(jnp.bfloat16)
    third = (rest - second.astype(jnp.float32)).astype(jnp.bfloat16)
    return first, second, third


def ranks(key_row):
    per_block = key_row.shape[1]
    key_column = jnp.broadcast_to(key_row, (8, per_block)).T[:, 0:1]
    slot = lax.broadcasted_iota(jnp.int32, (LANES, per_block), 1)
    total = jnp.zeros((1, per_block), jnp.float32)
    for top in range(0, per_block, LANES):
        other = key_column[top:top + LANES, :]
        earlier = lax.broadcasted_iota(jnp.int32, (LANES, per_block), 0) + top < slot
        before = (other < key_row) | ((other == key_row) & earlier)
        total = total + jnp.sum(jnp.where(before, 1.0, 0.0), axis=0, keepdims=True)
    return total


def prep_kernel(live_ref, centroid, angles, size, slip_rate, source_ref, target_ref):
    per_block = centroid.shape[1]
    count = live_ref[0]
    strike = angles[0:1, :]
    dip_angle = angles[1:2, :]
    cos_p, sin_p = jnp.cos(strike), jnp.sin(strike)
    cos_q, sin_q = jnp.cos(dip_angle), jnp.sin(dip_angle)
    lane = lax.broadcasted_iota(jnp.int32, (1, per_block), 1)
    live = lane < count
    squared = size[...] * size[...]
    weight = slip_rate[...] * squared
    place = [centroid[k:k + 1, :] for k in range(3)]

    extent = [jnp.max(jnp.where(live, row, -BIG), axis=1, keepdims=True)
              - jnp.min(jnp.where(live, row, BIG), axis=1, keepdims=True) for row in place]
    key = jnp.where((extent[0] >= extent[1]) & (extent[0] >= extent[2]), place[0],
                    jnp.where(extent[1] >= extent[2], place[1], place[2]))
    rank = ranks(jnp.where(live, key, BIG))
    rank_column = jnp.broadcast_to(rank, (8, per_block)).T[:, 0:1]

    zero = jnp.zeros((5, per_block), jnp.float32)
    rows = jnp.concatenate(place + [squared, weight * cos_p, weight * sin_p, cos_p, sin_p,
                                    -sin_q * sin_p, sin_q * cos_p, cos_q, zero], axis=0)
    pieces = jnp.concatenate(three_pieces(rows), axis=0)
    step = math.gcd(per_block, 256)
    parts = []
    for at in range(0, per_block, step):
        wanted = jnp.minimum(lax.broadcasted_iota(jnp.int32, (1, step), 1) + at, count - 1)
        pick = jnp.where(rank_column == wanted.astype(jnp.float32), 1.0, 0.0).astype(jnp.bfloat16)
        three = jnp.dot(pieces, pick, preferred_element_type=jnp.float32)
        parts.append(three[0:16, :] + (three[16:32, :] + three[32:48, :]))
    ordered = jnp.concatenate(parts, axis=1)

    source_ref[0:4, :] = ordered[0:4, :]
    source_ref[4:6, :] = jnp.where(live, ordered[4:6, :], 0.0)
    target_ref[0:4, :] = ordered[0:4, :]
    target_ref[4:9, :] = ordered[6:11, :]
    target_ref[9:10, :] = jnp.where(live, coupling, 0.0)
    target_ref[10:11, :] = rank
    target_ref[11:16, :] = zero

    turn = lax.broadcasted_iota(jnp.int32, (TURNS, 1), 0).astype(jnp.float32) * (math.pi / TURNS)
    along = jnp.cos(turn) * ordered[0:1, :] + jnp.sin(turn) * ordered[1:2, :]
    all_rows = jnp.concatenate([along, jnp.broadcast_to(ordered[2:3, :], (8, per_block))], axis=0)
    row = lax.broadcasted_iota(jnp.int32, (TURNS + 8, LANES), 0)
    column = lax.broadcasted_iota(jnp.int32, (TURNS + 8, LANES), 1)
    for lo in range(0, per_block, LANES):
        here = all_rows[:, lo:lo + LANES]
        used = live[:, lo:lo + LANES]
        for at, ends in ((6, jnp.min(jnp.where(used, here, BIG), axis=1, keepdims=True)),
                         (7, jnp.max(jnp.where(used, here, -BIG), axis=1, keepdims=True))):
            line = jnp.sum(jnp.where(row == column, ends, 0.0), axis=0, keepdims=True)
            line = jnp.where(column[0:1, :] == COUNT_LANE, count.astype(jnp.float32), line)
            source_ref[at:at + 1, lo:lo + LANES] = line


def pair_sums(columns, field):
    x, y, z, s2 = columns
    rx = x - field(0)
    ry = y - field(1)
    rz = z - field(2)
    d2 = (rx * rx + ry * ry) + (rz * rz + (s2 + field(3)))
    root = lax.rsqrt(d2)
    inverse = root * root
    cube = inverse * root
    ux, uy = field(4), field(5)
    bent = (cube * inverse) * (ux * rx + uy * ry)
    bent = 3.0 * bent
    return cube * ux - bent * rx, cube * uy - bent * ry, -bent * rz


def source_features(held, middle):
    x, y, z = (held[k:k + 1, :] - middle[k] for k in range(3))
    ux, uy = held[4:5, :], held[5:6, :]
    s = x * x + y * y + z * z + held[3:4, :]
    uxx, uxy, uxz, uyx, uyy, uyz = ux * x, ux * y, ux * z, uy * x, uy * y, uy * z
    along = uxx + uyy
    along3 = 3.0 * along
    return jnp.concatenate([
        jnp.ones_like(x), s, x, y, z, ux, uy, uxx, uxy, uxz, uyx, uyy, uyz,
        s * ux - along3 * x, s * uy - along3 * y, z * along], axis=0)


def target_features(held, middle, direction):
    x, y, z = (held[k:k + 1, :] - middle[k] for k in range(3))
    r = x * x + y * y + z * z + held[3:4, :]
    zero, one = jnp.zeros_like(x), jnp.ones_like(x)
    if direction is None:
        return jnp.concatenate([r, one, -2.0 * x, -2.0 * y, -2.0 * z] + [zero] * 11, axis=0)
    a, b, c = direction
    t3 = 3.0 * (a * x + b * y + c * z)
    return jnp.concatenate([
        zero, zero, zero, zero, zero, r * a - t3 * x, r * b - t3 * y,
        a * x + t3, 3.0 * b * x - 2.0 * a * y, 3.0 * c * x - 2.0 * a * z,
        3.0 * a * y - 2.0 * b * x, b * y + t3, 3.0 * c * y - 2.0 * b * z,
        a, b, -3.0 * c], axis=0)


def exchanges(count_blocks):
    bits = [1 << at for at in range(count_blocks.bit_length() - 1)]
    return bits[:1] + bits[:0:-1]


def block_at(position, me, count_blocks):
    flipped = 0
    for at, bit in enumerate(exchanges(count_blocks)):
        if position >> at & 1:
            flipped |= bit
    return me ^ flipped


def stage_kernel(first, last, me_ref, near_ref, source, piece, target, *rest):
    (columns, near_list, far_chunks, far_marks, counters, shear_part, normal_part,
     weights, factors) = rest[-9:]
    if last:
        earlier, (shear_ref, normal_ref) = rest[:-11], rest[-11:-9]
    else:
        earlier, sums_ref = (), rest[-10]
    count_blocks = near_ref.shape[1]
    held_blocks = piece.shape[0]
    per_block = target.shape[1]
    per_chunks = per_block // LANES
    total_chunks = held_blocks * per_chunks
    me = me_ref[0]

    def runs(ref, at):
        return jnp.concatenate([ref[at:at + 1, t * LANES:(t + 1) * LANES]
                                for t in range(per_chunks)], axis=0)

    low = jnp.concatenate([runs(piece.at[p], 6) for p in range(held_blocks)], axis=0)
    high = jnp.concatenate([runs(piece.at[p], 7) for p in range(held_blocks)], axis=0)
    own_low, own_high = runs(source, 6), runs(source, 7)
    lane = lax.broadcasted_iota(jnp.int32, (1, LANES), 1)
    center = 0.5 * (jnp.min(own_low, axis=0, keepdims=True)
                    + jnp.max(own_high, axis=0, keepdims=True))
    is_axis = (lane == 0) | (lane == TURNS // 2) | (lane == TURNS)

    def reach(low, high):
        out = jnp.maximum(jnp.abs(low - center), jnp.abs(high - center))
        return jnp.sqrt(jnp.sum(jnp.where(is_axis, out * out, 0.0), axis=1, keepdims=True))

    source_reach, own_reach = reach(low, high), reach(own_low, own_high)
    marks = jnp.zeros((total_chunks, 1), jnp.int32)
    for t in range(per_chunks):
        apart = jnp.maximum(low - own_high[t:t + 1, :], own_low[t:t + 1, :] - high)
        gap = jnp.max(jnp.where(lane <= TURNS, apart, 0.0), axis=1, keepdims=True)
        gap = jnp.maximum(gap, 0.0)
        both = source_reach + own_reach[t:t + 1, :]
        is_near = (gap * gap + SMALLEST) * SPREAD_LIMIT < both * both
        marks = marks + jnp.where(is_near, 1 << t, 0)
    middle = [center[0:1, k:k + 1] for k in (0, TURNS // 2, TURNS)]
    blocks = []
    for p in range(held_blocks):
        top = p * per_chunks
        held = marks[top:top + per_chunks, :]
        count = low[top, COUNT_LANE].astype(jnp.int32)
        blocks.append((held, jnp.max(held), (count + LANES - 1) // LANES,
                       near_ref[0, block_at(first + p, me, count_blocks)]))

    def pad(chunks, position):
        rest = lax.rem(WIDE - lax.rem(position, WIDE), WIDE)

        def put(at, carry):
            chunks[position + at] = total_chunks
            far_marks[position + at] = 0
            return carry

        lax.fori_loop(0, rest, put, 0)
        return position + rest

    counters[0] = 0
    counters[1] = 0
    for p, (held, any_near, chunk_count, linked) in enumerate(blocks):
        @pl.when(any_near > 0)
        def near_block(p=p, held=held, chunk_count=chunk_count, linked=linked):
            pairs, position = counters[0], counters[1]
            for t in range(per_chunks):
                chunk = p * per_chunks + t
                mark = jnp.where(t < chunk_count, held[t, 0], 0)
                far_chunks[position + t] = chunk
                far_marks[position + t] = mark * 2 + linked
                for run in range(per_chunks):
                    near_list[pairs] = (chunk * per_chunks + run) * 2 + linked
                    pairs = pairs + (lax.shift_right_logical(mark, run) & 1)
            counters[0] = pairs
            counters[1] = position + chunk_count

    near_pairs = counters[0]
    for spare in range(PAIRS - 1):
        near_list[near_pairs + spare] = total_chunks * per_chunks * 2
    near_steps = (near_pairs + PAIRS - 1) // PAIRS

    def list_blocks(wanted, start):
        position = start
        for p, (_, any_near, chunk_count, linked) in enumerate(blocks):
            here = jnp.where((any_near == 0) & (linked == wanted), chunk_count, 0)

            def put(at, carry, p=p, position=position):
                far_chunks[position + at] = p * per_chunks + at
                far_marks[position + at] = wanted
                return carry

            lax.fori_loop(0, here, put, 0)
            position = position + here
        return pad(far_chunks, position)

    far_mixed = list_blocks(1, counters[1])
    far_all = list_blocks(0, far_mixed)

    def chunk_of(chunk):
        real = jnp.minimum(chunk, total_chunks - 1)
        lo = pl.multiple_of(lax.rem(real, per_chunks) * LANES, LANES)
        held = piece[real // per_chunks, :, pl.ds(lo, LANES)]
        row = lax.broadcasted_iota(jnp.int32, (8, LANES), 0)
        blank = jnp.where(row == 3, 1.0, 0.0)
        return jnp.where((row >= 3) & (chunk == total_chunks), blank, held)

    def place_far(at, carry):
        for k in range(WIDE):
            number = at * WIDE + k
            pieces = three_pieces(source_features(chunk_of(far_chunks[number]), middle))
            lo = pl.multiple_of(number * LANES, LANES)
            for slot, which in enumerate(SOURCE_PIECES):
                weights[slot * FEATURES:(slot + 1) * FEATURES, pl.ds(lo, LANES)] = pieces[which]
        return carry

    lax.fori_loop(0, far_all // WIDE, place_far, 0)

    own = target[...]
    zero_row = jnp.zeros((1, per_block), jnp.float32)
    ways = (None, (own[4:5], own[5:6], zero_row), (own[6:7], own[7:8], own[8:9]))
    for which, way in enumerate(ways):
        pieces = three_pieces(target_features(own, middle, way))
        stacked = jnp.concatenate(
            [pieces[k].astype(jnp.float32) for k in TARGET_PIECES]
            + [jnp.zeros((LANES - DEPTH, per_block), jnp.float32)], axis=0)
        factors[which, :, :] = stacked.T.astype(jnp.bfloat16)

    shear_part[...] = jnp.zeros_like(shear_part)
    normal_part[...] = jnp.zeros_like(normal_part)

    @pl.when(near_pairs > 0)
    def spread_columns():
        turned = own.T
        for row in range(FRAME):
            columns[row, :, :] = jnp.broadcast_to(turned[:, row:row + 1], (per_block, LANES))

    def near_step(at, carry):
        work = []
        for k in range(PAIRS):
            code = near_list[at * PAIRS + k]
            chunk = lax.shift_right_logical(code, 1) // per_chunks
            held = chunk_of(chunk)
            fields = [jnp.broadcast_to(held[row:row + 1, :], (8, LANES)) for row in range(FIELDS)]
            run = lax.shift_right_logical(code, 1) & (per_chunks - 1)
            work.append(((code & 1) == 1, run, fields))
        for sub in range(LANES // 8):
            for linked, run, fields in work:
                rows = pl.ds(pl.multiple_of(run * LANES + 8 * sub, 8), 8)
                x, y, z, s2, tx, ty, nx, ny, nz = (columns[row, rows, :] for row in range(FRAME))
                fx, fy, fz = pair_sums((x, y, z, s2), fields.__getitem__)
                shear_part[rows, :] += tx * fx + ty * fy
                normal_part[rows, :] += jnp.where(linked, nx * fx + ny * fy + nz * fz, 0.0)
        return carry

    lax.fori_loop(0, near_steps, near_step, 0)

    def far_step(mixed, at, carry):
        lo = pl.multiple_of(at * WIDE * LANES, WIDE * LANES)
        sources = weights[:, pl.ds(lo, WIDE * LANES)]

        held_marks = [far_marks[at * WIDE + k] for k in range(WIDE)] if mixed else None
        for top in range(0, per_block, TALL):
            def product(which):
                return jnp.dot(factors[which, top:top + TALL, 0:DEPTH], sources,
                               preferred_element_type=jnp.float32)

            def add(part, terms, linked_only):
                total = None
                for k in range(WIDE):
                    term = terms[:, k * LANES:(k + 1) * LANES]
                    if mixed:
                        mark = held_marks[k]
                        keep = (lax.shift_right_logical(mark, top // TALL + 1) & 1) == 0
                        if linked_only:
                            keep = keep & ((mark & 1) == 1)
                        term = jnp.where(keep, term, 0.0)
                    total = term if total is None else total + term
                part[top:top + TALL, :] += total

            root = lax.rsqrt(product(0))
            inverse = root * root
            fourth = inverse * inverse
            add(shear_part, (product(1) * root) * fourth, False)
            if mixed:
                add(normal_part, (product(2) * root) * fourth, True)
        return carry

    mixed_steps, far_steps = far_mixed // WIDE, far_all // WIDE
    lax.fori_loop(0, mixed_steps, functools.partial(far_step, True), 0)
    lax.fori_loop(mixed_steps, far_steps, functools.partial(far_step, False), 0)

    ones = jnp.ones((8, LANES), jnp.bfloat16)
    dims = (((1,), (1,)), ((), ()))
    sums = []
    for at, part in enumerate((shear_part, normal_part)):
        first_sum, second_sum, third_sum = (
            lax.dot_general(ones, piece_of, dims, preferred_element_type=jnp.float32)[0:1, :]
            for piece_of in three_pieces(part[...]))
        summed = first_sum + (second_sum + third_sum)
        for other in earlier:
            summed = summed + other[at:at + 1, :]
        sums.append(summed)
    if not last:
        for at in range(2):
            sums_ref[at:at + 1, :] = sums[at]
        return
    both = jnp.concatenate([jnp.where(own[9:10, :] > 0.0, one * own[9:10, :], 0.0) for one in sums]
                           + [jnp.zeros((14, per_block), jnp.float32)], axis=0)
    pieces = jnp.concatenate(three_pieces(both), axis=0)
    step = math.gcd(per_block, 256)
    slot = lax.broadcasted_iota(jnp.int32, (per_block, 1), 0).astype(jnp.float32)
    for at in range(0, per_block, step):
        pick = jnp.where(slot == own[10:11, at:at + step], 1.0, 0.0).astype(jnp.bfloat16)
        three = jnp.dot(pieces, pick, preferred_element_type=jnp.float32)
        back = three[0:16, :] + (three[16:32, :] + three[32:48, :])
        shear_ref[:, at:at + step] = back[0:1, :]
        normal_ref[:, at:at + step] = back[1:2, :]


def body(centroid, angles, size, slip_rate, live_count, near):
    per_block = centroid.shape[1]
    count_blocks = near.shape[1]
    smem = pl.BlockSpec(memory_space=pltpu.SMEM)
    vmem = pl.BlockSpec(memory_space=pltpu.VMEM)
    source, target = pl.pallas_call(
        prep_kernel,
        out_shape=(jax.ShapeDtypeStruct((8, per_block), jnp.float32),
                   jax.ShapeDtypeStruct((16, per_block), jnp.float32)),
        in_specs=[smem] + [vmem] * 4,
        out_specs=(vmem, vmem),
    )(live_count, centroid, angles, size.reshape(1, per_block), slip_rate.reshape(1, per_block))
    me = lax.axis_index("blocks").astype(jnp.int32).reshape(1)

    def stage(piece, first, earlier, last):
        held_blocks = piece.shape[0]
        total_chunks = held_blocks * per_block // LANES
        row = jax.ShapeDtypeStruct((1, per_block), jnp.float32)
        pairs = per_block * per_block * held_blocks
        return pl.pallas_call(
            functools.partial(stage_kernel, first, last),
            out_shape=(row, row) if last else jax.ShapeDtypeStruct((8, per_block), jnp.float32),
            in_specs=[smem, smem] + [vmem] * (3 + len(earlier)),
            out_specs=(vmem, vmem) if last else vmem,
            scratch_shapes=[
                pltpu.VMEM((FRAME, per_block, LANES), jnp.float32),
                pltpu.SMEM((total_chunks * (per_block // LANES) + 8,), jnp.int32),
                pltpu.SMEM((total_chunks + per_block // LANES + 2 * WIDE,), jnp.int32),
                pltpu.SMEM((total_chunks + per_block // LANES + 2 * WIDE,), jnp.int32),
                pltpu.SMEM((2,), jnp.int32),
                pltpu.VMEM((per_block, LANES), jnp.float32),
                pltpu.VMEM((per_block, LANES), jnp.float32),
                pltpu.VMEM((DEPTH, (total_chunks + 2 * WIDE) * LANES), jnp.bfloat16),
                pltpu.VMEM((3, per_block, LANES), jnp.bfloat16),
            ],
            compiler_params=pltpu.CompilerParams(vmem_limit_bytes=20 * 1024 * 1024),
            cost_estimate=pl.CostEstimate(flops=pairs * 2 * DEPTH * 4, bytes_accessed=pairs,
                                          transcendentals=pairs),
        )(me, near, source, piece, target, *earlier)

    bits = exchanges(count_blocks)
    held, fresh, first, sums = source[None], None, 0, []
    for at, bit in enumerate(bits):
        swap = [(one, one ^ bit) for one in range(count_blocks)]
        coming = lax.ppermute(held, "blocks", swap)
        if at:
            sums.append(stage(fresh, first, (), False))
            first = held.shape[0]
        if at < len(bits) - 1:
            held = jnp.concatenate([held, coming], axis=0)
        fresh = coming if at else held
    shear, normal = stage(fresh, first, sums, True)
    return shear.reshape(per_block), normal.reshape(per_block)


def solution(mesh):
    in_specs = (
        P(None, ("runs", "blocks")),
        P(None, ("runs", "blocks")),
        P(("runs", "blocks")),
        P(("runs", "blocks")),
        P(("runs", "blocks")),
        P(("runs", "blocks"), None),
    )
    out_specs = (P(("runs", "blocks")), P(("runs", "blocks")))
    return jax.shard_map(body, mesh=mesh, in_specs=in_specs, out_specs=out_specs, check_vma=False)
```

```python
import functools
import math

import jax
import jax.numpy as jnp
from jax import lax
from jax.experimental import pallas as pl
from jax.experimental.pallas import tpu as pltpu
from jax.sharding import PartitionSpec as P

coupling = 0.002
LANES = 128
FIELDS = 6
FRAME = 9
WIDE = 4
PAIRS = 2
TALL = 128
TURNS = 64
COUNT_LANE = 127
BIG = 1e15
SMALLEST = 2e-6
SPREAD_LIMIT = 1500.0
FEATURES = 16
SOURCE_PIECES = (0, 0, 1, 0, 2, 1)
TARGET_PIECES = (0, 1, 0, 2, 0, 1)
DEPTH = FEATURES * len(SOURCE_PIECES)


def three_pieces(value):
    first = value.astype(jnp.bfloat16)
    rest = value - first.astype(jnp.float32)
    second = rest.astype(jnp.bfloat16)
    third = (rest - second.astype(jnp.float32)).astype(jnp.bfloat16)
    return first, second, third


def ranks(key_row):
    per_block = key_row.shape[1]
    key_column = jnp.broadcast_to(key_row, (8, per_block)).T[:, 0:1]
    tile = (LANES, LANES)
    earlier = lax.broadcasted_iota(jnp.int32, tile, 0) < lax.broadcasted_iota(jnp.int32, tile, 1)

    def counted(before):
        return jnp.sum(jnp.where(before, 1.0, 0.0), axis=0, keepdims=True)

    total = jnp.zeros((1, per_block), jnp.float32)
    for top in range(0, per_block, LANES):
        other = key_column[top:top + LANES, :]
        end = top + LANES
        same = key_row[:, top:end]
        parts = [counted((other < same) | ((other == same) & earlier))]
        if top:
            parts.insert(0, counted(other < key_row[:, :top]))
        if end < per_block:
            parts.append(counted(other <= key_row[:, end:]))
        total = total + jnp.concatenate(parts, axis=1)
    return total


def prep_kernel(live_ref, centroid, angles, size, slip_rate, source_ref, target_ref):
    per_block = centroid.shape[1]
    count = live_ref[0]
    strike = angles[0:1, :]
    dip_angle = angles[1:2, :]
    cos_p, sin_p = jnp.cos(strike), jnp.sin(strike)
    cos_q, sin_q = jnp.cos(dip_angle), jnp.sin(dip_angle)
    lane = lax.broadcasted_iota(jnp.int32, (1, per_block), 1)
    live = lane < count
    squared = size[...] * size[...]
    weight = slip_rate[...] * squared
    place = [centroid[k:k + 1, :] for k in range(3)]

    extent = [jnp.max(jnp.where(live, row, -BIG), axis=1, keepdims=True)
              - jnp.min(jnp.where(live, row, BIG), axis=1, keepdims=True) for row in place]
    key = jnp.where((extent[0] >= extent[1]) & (extent[0] >= extent[2]), place[0],
                    jnp.where(extent[1] >= extent[2], place[1], place[2]))
    rank = ranks(jnp.where(live, key, BIG))
    rank_column = jnp.broadcast_to(rank, (8, per_block)).T[:, 0:1]

    zero = jnp.zeros((5, per_block), jnp.float32)
    rows = jnp.concatenate(place + [squared, weight * cos_p, weight * sin_p, cos_p, sin_p,
                                    -sin_q * sin_p, sin_q * cos_p, cos_q, zero], axis=0)
    pieces = jnp.concatenate(three_pieces(rows), axis=0)
    step = math.gcd(per_block, 256)
    parts = []
    for at in range(0, per_block, step):
        wanted = jnp.minimum(lax.broadcasted_iota(jnp.int32, (1, step), 1) + at, count - 1)
        pick = jnp.where(rank_column == wanted.astype(jnp.float32), 1.0, 0.0).astype(jnp.bfloat16)
        three = jnp.dot(pieces, pick, preferred_element_type=jnp.float32)
        parts.append(three[0:16, :] + (three[16:32, :] + three[32:48, :]))
    ordered = jnp.concatenate(parts, axis=1)

    source_ref[0:4, :] = ordered[0:4, :]
    source_ref[4:6, :] = jnp.where(live, ordered[4:6, :], 0.0)
    target_ref[0:4, :] = ordered[0:4, :]
    target_ref[4:9, :] = ordered[6:11, :]
    target_ref[9:10, :] = jnp.where(live, coupling, 0.0)
    target_ref[10:11, :] = rank
    target_ref[11:16, :] = zero

    turn = lax.broadcasted_iota(jnp.int32, (TURNS, 1), 0).astype(jnp.float32) * (math.pi / TURNS)
    along = jnp.cos(turn) * ordered[0:1, :] + jnp.sin(turn) * ordered[1:2, :]
    all_rows = jnp.concatenate([along, jnp.broadcast_to(ordered[2:3, :], (8, per_block))], axis=0)
    row = lax.broadcasted_iota(jnp.int32, (TURNS + 8, LANES), 0)
    column = lax.broadcasted_iota(jnp.int32, (TURNS + 8, LANES), 1)
    for lo in range(0, per_block, LANES):
        here = all_rows[:, lo:lo + LANES]
        used = live[:, lo:lo + LANES]
        for at, ends in ((6, jnp.min(jnp.where(used, here, BIG), axis=1, keepdims=True)),
                         (7, jnp.max(jnp.where(used, here, -BIG), axis=1, keepdims=True))):
            line = jnp.sum(jnp.where(row == column, ends, 0.0), axis=0, keepdims=True)
            line = jnp.where(column[0:1, :] == COUNT_LANE, count.astype(jnp.float32), line)
            source_ref[at:at + 1, lo:lo + LANES] = line


def pair_sums(columns, field):
    x, y, z, s2 = columns
    rx = x - field(0)
    ry = y - field(1)
    rz = z - field(2)
    d2 = (rx * rx + ry * ry) + (rz * rz + (s2 + field(3)))
    root = lax.rsqrt(d2)
    inverse = root * root
    cube = inverse * root
    ux, uy = field(4), field(5)
    bent = (cube * inverse) * (ux * rx + uy * ry)
    bent = 3.0 * bent
    return cube * ux - bent * rx, cube * uy - bent * ry, -bent * rz


def source_features(held, middle):
    x, y, z = (held[k:k + 1, :] - middle[k] for k in range(3))
    ux, uy = held[4:5, :], held[5:6, :]
    s = x * x + y * y + z * z + held[3:4, :]
    uxx, uxy, uxz, uyx, uyy, uyz = ux * x, ux * y, ux * z, uy * x, uy * y, uy * z
    along = uxx + uyy
    along3 = 3.0 * along
    return jnp.concatenate([
        jnp.ones_like(x), s, x, y, z, ux, uy, uxx, uxy, uxz, uyx, uyy, uyz,
        s * ux - along3 * x, s * uy - along3 * y, z * along], axis=0)


def target_features(held, middle, direction):
    x, y, z = (held[k:k + 1, :] - middle[k] for k in range(3))
    r = x * x + y * y + z * z + held[3:4, :]
    zero, one = jnp.zeros_like(x), jnp.ones_like(x)
    if direction is None:
        return jnp.concatenate([r, one, -2.0 * x, -2.0 * y, -2.0 * z] + [zero] * 11, axis=0)
    a, b, c = direction
    t3 = 3.0 * (a * x + b * y + c * z)
    return jnp.concatenate([
        zero, zero, zero, zero, zero, r * a - t3 * x, r * b - t3 * y,
        a * x + t3, 3.0 * b * x - 2.0 * a * y, 3.0 * c * x - 2.0 * a * z,
        3.0 * a * y - 2.0 * b * x, b * y + t3, 3.0 * c * y - 2.0 * b * z,
        a, b, -3.0 * c], axis=0)


def exchanges(count_blocks):
    bits = [1 << at for at in range(count_blocks.bit_length() - 1)]
    return bits[:1] + bits[:0:-1]


def block_at(position, me, count_blocks):
    flipped = 0
    for at, bit in enumerate(exchanges(count_blocks)):
        if position >> at & 1:
            flipped |= bit
    return me ^ flipped


def stage_kernel(first, last, me_ref, near_ref, source, piece, target, *rest):
    (columns, near_list, far_chunks, far_marks, counters, shear_part, normal_part,
     weights, factors) = rest[-9:]
    if last:
        earlier, (shear_ref, normal_ref) = rest[:-11], rest[-11:-9]
    else:
        earlier, sums_ref = (), rest[-10]
    count_blocks = near_ref.shape[1]
    held_blocks = piece.shape[0]
    per_block = target.shape[1]
    per_chunks = per_block // LANES
    total_chunks = held_blocks * per_chunks
    me = me_ref[0]

    def runs(ref, at):
        return jnp.concatenate([ref[at:at + 1, t * LANES:(t + 1) * LANES]
                                for t in range(per_chunks)], axis=0)

    low = jnp.concatenate([runs(piece.at[p], 6) for p in range(held_blocks)], axis=0)
    high = jnp.concatenate([runs(piece.at[p], 7) for p in range(held_blocks)], axis=0)
    own_low, own_high = runs(source, 6), runs(source, 7)
    lane = lax.broadcasted_iota(jnp.int32, (1, LANES), 1)
    center = 0.5 * (jnp.min(own_low, axis=0, keepdims=True)
                    + jnp.max(own_high, axis=0, keepdims=True))
    is_axis = (lane == 0) | (lane == TURNS // 2) | (lane == TURNS)

    def reach(low, high):
        out = jnp.maximum(jnp.abs(low - center), jnp.abs(high - center))
        return jnp.sqrt(jnp.sum(jnp.where(is_axis, out * out, 0.0), axis=1, keepdims=True))

    source_reach, own_reach = reach(low, high), reach(own_low, own_high)
    marks = jnp.zeros((total_chunks, 1), jnp.int32)
    for t in range(per_chunks):
        apart = jnp.maximum(low - own_high[t:t + 1, :], own_low[t:t + 1, :] - high)
        gap = jnp.max(jnp.where(lane <= TURNS, apart, 0.0), axis=1, keepdims=True)
        gap = jnp.maximum(gap, 0.0)
        both = source_reach + own_reach[t:t + 1, :]
        is_near = (gap * gap + SMALLEST) * SPREAD_LIMIT < both * both
        marks = marks + jnp.where(is_near, 1 << t, 0)
    middle = [center[0:1, k:k + 1] for k in (0, TURNS // 2, TURNS)]
    blocks = []
    for p in range(held_blocks):
        top = p * per_chunks
        held = marks[top:top + per_chunks, :]
        count = low[top, COUNT_LANE].astype(jnp.int32)
        blocks.append((held, jnp.max(held), (count + LANES - 1) // LANES,
                       near_ref[0, block_at(first + p, me, count_blocks)]))

    def pad(chunks, position):
        rest = lax.rem(WIDE - lax.rem(position, WIDE), WIDE)

        def put(at, carry):
            chunks[position + at] = total_chunks
            far_marks[position + at] = 0
            return carry

        lax.fori_loop(0, rest, put, 0)
        return position + rest

    counters[0] = 0
    counters[1] = 0
    for p, (held, any_near, chunk_count, linked) in enumerate(blocks):
        @pl.when(any_near > 0)
        def near_block(p=p, held=held, chunk_count=chunk_count, linked=linked):
            pairs, position = counters[0], counters[1]
            for t in range(per_chunks):
                chunk = p * per_chunks + t
                mark = jnp.where(t < chunk_count, held[t, 0], 0)
                far_chunks[position + t] = chunk
                far_marks[position + t] = mark * 2 + linked
                for run in range(per_chunks):
                    near_list[pairs] = (chunk * per_chunks + run) * 2 + linked
                    pairs = pairs + (lax.shift_right_logical(mark, run) & 1)
            counters[0] = pairs
            counters[1] = position + chunk_count

    near_pairs = counters[0]
    for spare in range(PAIRS - 1):
        near_list[near_pairs + spare] = total_chunks * per_chunks * 2
    near_steps = (near_pairs + PAIRS - 1) // PAIRS

    def list_blocks(wanted, start):
        position = start
        for p, (_, any_near, chunk_count, linked) in enumerate(blocks):
            here = jnp.where((any_near == 0) & (linked == wanted), chunk_count, 0)

            def put(at, carry, p=p, position=position):
                far_chunks[position + at] = p * per_chunks + at
                far_marks[position + at] = wanted
                return carry

            lax.fori_loop(0, here, put, 0)
            position = position + here
        return pad(far_chunks, position)

    far_mixed = list_blocks(1, counters[1])
    far_all = list_blocks(0, far_mixed)

    def chunk_of(chunk):
        real = jnp.minimum(chunk, total_chunks - 1)
        lo = pl.multiple_of(lax.rem(real, per_chunks) * LANES, LANES)
        held = piece[real // per_chunks, :, pl.ds(lo, LANES)]
        row = lax.broadcasted_iota(jnp.int32, (8, LANES), 0)
        blank = jnp.where(row == 3, 1.0, 0.0)
        return jnp.where((row >= 3) & (chunk == total_chunks), blank, held)

    def place_far(at, carry):
        for k in range(WIDE):
            number = at * WIDE + k
            pieces = three_pieces(source_features(chunk_of(far_chunks[number]), middle))
            lo = pl.multiple_of(number * LANES, LANES)
            for slot, which in enumerate(SOURCE_PIECES):
                weights[slot * FEATURES:(slot + 1) * FEATURES, pl.ds(lo, LANES)] = pieces[which]
        return carry

    lax.fori_loop(0, far_all // WIDE, place_far, 0)

    own = target[...]
    zero_row = jnp.zeros((1, per_block), jnp.float32)
    ways = (None, (own[4:5], own[5:6], zero_row), (own[6:7], own[7:8], own[8:9]))
    for which, way in enumerate(ways):
        pieces = three_pieces(target_features(own, middle, way))
        stacked = jnp.concatenate(
            [pieces[k].astype(jnp.float32) for k in TARGET_PIECES]
            + [jnp.zeros((LANES - DEPTH, per_block), jnp.float32)], axis=0)
        factors[which, :, :] = stacked.T.astype(jnp.bfloat16)

    shear_part[...] = jnp.zeros_like(shear_part)
    normal_part[...] = jnp.zeros_like(normal_part)

    @pl.when(near_pairs > 0)
    def spread_columns():
        turned = own.T
        for row in range(FRAME):
            columns[row, :, :] = jnp.broadcast_to(turned[:, row:row + 1], (per_block, LANES))

    def near_step(at, carry):
        work = []
        for k in range(PAIRS):
            code = near_list[at * PAIRS + k]
            chunk = lax.shift_right_logical(code, 1) // per_chunks
            held = chunk_of(chunk)
            fields = [jnp.broadcast_to(held[row:row + 1, :], (8, LANES)) for row in range(FIELDS)]
            run = lax.shift_right_logical(code, 1) & (per_chunks - 1)
            work.append(((code & 1) == 1, run, fields))
        for sub in range(LANES // 8):
            for linked, run, fields in work:
                rows = pl.ds(pl.multiple_of(run * LANES + 8 * sub, 8), 8)
                x, y, z, s2, tx, ty, nx, ny, nz = (columns[row, rows, :] for row in range(FRAME))
                fx, fy, fz = pair_sums((x, y, z, s2), fields.__getitem__)
                shear_part[rows, :] += tx * fx + ty * fy
                normal_part[rows, :] += jnp.where(linked, nx * fx + ny * fy + nz * fz, 0.0)
        return carry

    lax.fori_loop(0, near_steps, near_step, 0)

    def far_step(mixed, at, carry):
        lo = pl.multiple_of(at * WIDE * LANES, WIDE * LANES)
        sources = weights[:, pl.ds(lo, WIDE * LANES)]

        held_marks = [far_marks[at * WIDE + k] for k in range(WIDE)] if mixed else None
        for top in range(0, per_block, TALL):
            def product(which):
                return jnp.dot(factors[which, top:top + TALL, 0:DEPTH], sources,
                               preferred_element_type=jnp.float32)

            def add(part, terms, linked_only):
                total = None
                for k in range(WIDE):
                    term = terms[:, k * LANES:(k + 1) * LANES]
                    if mixed:
                        mark = held_marks[k]
                        keep = (lax.shift_right_logical(mark, top // TALL + 1) & 1) == 0
                        if linked_only:
                            keep = keep & ((mark & 1) == 1)
                        term = jnp.where(keep, term, 0.0)
                    total = term if total is None else total + term
                part[top:top + TALL, :] += total

            root = lax.rsqrt(product(0))
            inverse = root * root
            fourth = inverse * inverse
            add(shear_part, (product(1) * root) * fourth, False)
            if mixed:
                add(normal_part, (product(2) * root) * fourth, True)
        return carry

    mixed_steps, far_steps = far_mixed // WIDE, far_all // WIDE
    lax.fori_loop(0, mixed_steps, functools.partial(far_step, True), 0)
    lax.fori_loop(mixed_steps, far_steps, functools.partial(far_step, False), 0)

    ones = jnp.ones((8, LANES), jnp.bfloat16)
    dims = (((1,), (1,)), ((), ()))
    sums = []
    for at, part in enumerate((shear_part, normal_part)):
        first_sum, second_sum, third_sum = (
            lax.dot_general(ones, piece_of, dims, preferred_element_type=jnp.float32)[0:1, :]
            for piece_of in three_pieces(part[...]))
        summed = first_sum + (second_sum + third_sum)
        for other in earlier:
            summed = summed + other[at:at + 1, :]
        sums.append(summed)
    if not last:
        for at in range(2):
            sums_ref[at:at + 1, :] = sums[at]
        return
    both = jnp.concatenate([jnp.where(own[9:10, :] > 0.0, one * own[9:10, :], 0.0) for one in sums]
                           + [jnp.zeros((14, per_block), jnp.float32)], axis=0)
    pieces = jnp.concatenate(three_pieces(both), axis=0)
    step = math.gcd(per_block, 256)
    slot = lax.broadcasted_iota(jnp.int32, (per_block, 1), 0).astype(jnp.float32)
    for at in range(0, per_block, step):
        pick = jnp.where(slot == own[10:11, at:at + step], 1.0, 0.0).astype(jnp.bfloat16)
        three = jnp.dot(pieces, pick, preferred_element_type=jnp.float32)
        back = three[0:16, :] + (three[16:32, :] + three[32:48, :])
        shear_ref[:, at:at + step] = back[0:1, :]
        normal_ref[:, at:at + step] = back[1:2, :]


def body(centroid, angles, size, slip_rate, live_count, near):
    per_block = centroid.shape[1]
    count_blocks = near.shape[1]
    smem = pl.BlockSpec(memory_space=pltpu.SMEM)
    vmem = pl.BlockSpec(memory_space=pltpu.VMEM)
    source, target = pl.pallas_call(
        prep_kernel,
        out_shape=(jax.ShapeDtypeStruct((8, per_block), jnp.float32),
                   jax.ShapeDtypeStruct((16, per_block), jnp.float32)),
        in_specs=[smem] + [vmem] * 4,
        out_specs=(vmem, vmem),
        compiler_params=pltpu.CompilerParams(vmem_limit_bytes=16 * 1024 * 1024),
    )(live_count, centroid, angles, size.reshape(1, per_block), slip_rate.reshape(1, per_block))
    me = lax.axis_index("blocks").astype(jnp.int32).reshape(1)

    def stage(piece, first, earlier, last):
        held_blocks = piece.shape[0]
        total_chunks = held_blocks * per_block // LANES
        row = jax.ShapeDtypeStruct((1, per_block), jnp.float32)
        pairs = per_block * per_block * held_blocks
        return pl.pallas_call(
            functools.partial(stage_kernel, first, last),
            out_shape=(row, row) if last else jax.ShapeDtypeStruct((8, per_block), jnp.float32),
            in_specs=[smem, smem] + [vmem] * (3 + len(earlier)),
            out_specs=(vmem, vmem) if last else vmem,
            scratch_shapes=[
                pltpu.VMEM((FRAME, per_block, LANES), jnp.float32),
                pltpu.SMEM((total_chunks * (per_block // LANES) + 8,), jnp.int32),
                pltpu.SMEM((total_chunks + per_block // LANES + 2 * WIDE,), jnp.int32),
                pltpu.SMEM((total_chunks + per_block // LANES + 2 * WIDE,), jnp.int32),
                pltpu.SMEM((2,), jnp.int32),
                pltpu.VMEM((per_block, LANES), jnp.float32),
                pltpu.VMEM((per_block, LANES), jnp.float32),
                pltpu.VMEM((DEPTH, (total_chunks + 2 * WIDE) * LANES), jnp.bfloat16),
                pltpu.VMEM((3, per_block, LANES), jnp.bfloat16),
            ],
            compiler_params=pltpu.CompilerParams(vmem_limit_bytes=20 * 1024 * 1024),
            cost_estimate=pl.CostEstimate(flops=pairs * 2 * DEPTH * 4, bytes_accessed=pairs,
                                          transcendentals=pairs),
        )(me, near, source, piece, target, *earlier)

    bits = exchanges(count_blocks)
    held, fresh, first, sums = source[None], None, 0, []
    for at, bit in enumerate(bits):
        swap = [(one, one ^ bit) for one in range(count_blocks)]
        coming = lax.ppermute(held, "blocks", swap)
        if at:
            sums.append(stage(fresh, first, (), False))
            first = held.shape[0]
        if at < len(bits) - 1:
            held = jnp.concatenate([held, coming], axis=0)
        fresh = coming if at else held
    shear, normal = stage(fresh, first, sums, True)
    return shear.reshape(per_block), normal.reshape(per_block)


def solution(mesh):
    in_specs = (
        P(None, ("runs", "blocks")),
        P(None, ("runs", "blocks")),
        P(("runs", "blocks")),
        P(("runs", "blocks")),
        P(("runs", "blocks")),
        P(("runs", "blocks"), None),
    )
    out_specs = (P(("runs", "blocks")), P(("runs", "blocks")))
    return jax.shard_map(body, mesh=mesh, in_specs=in_specs, out_specs=out_specs, check_vma=False)
```

```python
import functools
import math

import jax
import jax.numpy as jnp
from jax import lax
from jax.experimental import pallas as pl
from jax.experimental.pallas import tpu as pltpu
from jax.sharding import PartitionSpec as P

coupling = 0.002
LANES = 128
FIELDS = 6
FRAME = 9
WIDE = 4
PAIRS = 2
TALL = 128
TURNS = 64
COUNT_LANE = 127
BIG = 1e15
SMALLEST = 2e-6
SPREAD_LIMIT = 1500.0
FEATURES = 16
SOURCE_PIECES = (0, 0, 1, 0, 2, 1)
TARGET_PIECES = (0, 1, 0, 2, 0, 1)
DEPTH = FEATURES * len(SOURCE_PIECES)


def exchanges(count_blocks):
    bits = [1 << at for at in range(count_blocks.bit_length() - 1)]
    return bits[:1] + bits[:0:-1]


def block_at(position, me, count_blocks):
    flipped = 0
    for at, bit in enumerate(exchanges(count_blocks)):
        flipped = flipped + ((position >> at) & 1) * bit
    return me ^ flipped


def three_pieces(value):
    first = value.astype(jnp.bfloat16)
    rest = value - first.astype(jnp.float32)
    second = rest.astype(jnp.bfloat16)
    third = (rest - second.astype(jnp.float32)).astype(jnp.bfloat16)
    return first, second, third


def ranks(key_row):
    per_block = key_row.shape[1]
    key_column = jnp.broadcast_to(key_row, (8, per_block)).T[:, 0:1]
    tile = (LANES, LANES)
    earlier = lax.broadcasted_iota(jnp.int32, tile, 0) < lax.broadcasted_iota(jnp.int32, tile, 1)

    def counted(before):
        return jnp.sum(jnp.where(before, 1.0, 0.0), axis=0, keepdims=True)

    total = jnp.zeros((1, per_block), jnp.float32)
    for top in range(0, per_block, LANES):
        other = key_column[top:top + LANES, :]
        end = top + LANES
        same = key_row[:, top:end]
        parts = [counted((other < same) | ((other == same) & earlier))]
        if top:
            parts.insert(0, counted(other < key_row[:, :top]))
        if end < per_block:
            parts.append(counted(other <= key_row[:, end:]))
        total = total + jnp.concatenate(parts, axis=1)
    return total


def prep_kernel(count_blocks, me_ref, live_ref, given, source_ref, target_ref):
    per_block = given.shape[1]
    count = live_ref[0]
    strike, dip_angle, size, slip_rate = (given[row:row + 1, :] for row in range(3, 7))
    cos_p, sin_p = jnp.cos(strike), jnp.sin(strike)
    cos_q, sin_q = jnp.cos(dip_angle), jnp.sin(dip_angle)
    lane = lax.broadcasted_iota(jnp.int32, (1, per_block), 1)
    live = lane < count
    squared = size * size
    weight = slip_rate * squared
    place = [given[k:k + 1, :] for k in range(3)]

    extent = [jnp.max(jnp.where(live, row, -BIG), axis=1, keepdims=True)
              - jnp.min(jnp.where(live, row, BIG), axis=1, keepdims=True) for row in place]
    key = jnp.where((extent[0] >= extent[1]) & (extent[0] >= extent[2]), place[0],
                    jnp.where(extent[1] >= extent[2], place[1], place[2]))
    rank = ranks(jnp.where(live, key, BIG))
    rank_column = jnp.broadcast_to(rank, (8, per_block)).T[:, 0:1]

    zero = jnp.zeros((5, per_block), jnp.float32)
    rows = jnp.concatenate(place + [squared, weight * cos_p, weight * sin_p, cos_p, sin_p,
                                    -sin_q * sin_p, sin_q * cos_p, cos_q, zero], axis=0)
    pieces = jnp.concatenate(three_pieces(rows), axis=0)
    step = math.gcd(per_block, 256)
    parts = []
    for at in range(0, per_block, step):
        wanted = jnp.minimum(lax.broadcasted_iota(jnp.int32, (1, step), 1) + at, count - 1)
        pick = jnp.where(rank_column == wanted.astype(jnp.float32), 1.0, 0.0).astype(jnp.bfloat16)
        three = jnp.dot(pieces, pick, preferred_element_type=jnp.float32)
        parts.append(three[0:16, :] + (three[16:32, :] + three[32:48, :]))
    ordered = jnp.concatenate(parts, axis=1)

    source_ref[0:4, :] = ordered[0:4, :]
    source_ref[4:6, :] = jnp.where(live, ordered[4:6, :], 0.0)
    target_ref[0:4, :] = ordered[0:4, :]
    target_ref[4:9, :] = ordered[6:11, :]
    target_ref[9:10, :] = jnp.where(live, coupling, 0.0)
    target_ref[10:11, :] = rank
    links = jnp.broadcast_to(given[7:8, 0:LANES], (8, LANES)).T[:, 0:1]
    position = lax.broadcasted_iota(jnp.int32, (1, LANES), 1)
    number = lax.broadcasted_iota(jnp.int32, (LANES, 1), 0)
    links = jnp.sum(jnp.where(number == block_at(position, me_ref[0], count_blocks), links, 0.0),
                    axis=0, keepdims=True)
    target_ref[11:16, :] = zero
    target_ref[11:12, 0:LANES] = links

    turn = lax.broadcasted_iota(jnp.int32, (TURNS, 1), 0).astype(jnp.float32) * (math.pi / TURNS)
    along = jnp.cos(turn) * ordered[0:1, :] + jnp.sin(turn) * ordered[1:2, :]
    all_rows = jnp.concatenate([along, jnp.broadcast_to(ordered[2:3, :], (8, per_block))], axis=0)
    row = lax.broadcasted_iota(jnp.int32, (TURNS + 8, LANES), 0)
    column = lax.broadcasted_iota(jnp.int32, (TURNS + 8, LANES), 1)
    for lo in range(0, per_block, LANES):
        here = all_rows[:, lo:lo + LANES]
        used = live[:, lo:lo + LANES]
        for at, ends in ((6, jnp.min(jnp.where(used, here, BIG), axis=1, keepdims=True)),
                         (7, jnp.max(jnp.where(used, here, -BIG), axis=1, keepdims=True))):
            line = jnp.sum(jnp.where(row == column, ends, 0.0), axis=0, keepdims=True)
            line = jnp.where(column[0:1, :] == COUNT_LANE, count.astype(jnp.float32), line)
            source_ref[at:at + 1, lo:lo + LANES] = line


def pair_sums(columns, field):
    x, y, z, s2 = columns
    rx = x - field(0)
    ry = y - field(1)
    rz = z - field(2)
    d2 = (rx * rx + ry * ry) + (rz * rz + (s2 + field(3)))
    root = lax.rsqrt(d2)
    inverse = root * root
    cube = inverse * root
    ux, uy = field(4), field(5)
    bent = (cube * inverse) * (ux * rx + uy * ry)
    bent = 3.0 * bent
    return cube * ux - bent * rx, cube * uy - bent * ry, -bent * rz


def source_features(held, middle):
    x, y, z = (held[k:k + 1, :] - middle[k] for k in range(3))
    ux, uy = held[4:5, :], held[5:6, :]
    s = x * x + y * y + z * z + held[3:4, :]
    uxx, uxy, uxz, uyx, uyy, uyz = ux * x, ux * y, ux * z, uy * x, uy * y, uy * z
    along = uxx + uyy
    along3 = 3.0 * along
    return jnp.concatenate([
        jnp.ones_like(x), s, x, y, z, ux, uy, uxx, uxy, uxz, uyx, uyy, uyz,
        s * ux - along3 * x, s * uy - along3 * y, z * along], axis=0)


def target_features(held, middle, direction):
    x, y, z = (held[k:k + 1, :] - middle[k] for k in range(3))
    r = x * x + y * y + z * z + held[3:4, :]
    zero, one = jnp.zeros_like(x), jnp.ones_like(x)
    if direction is None:
        return jnp.concatenate([r, one, -2.0 * x, -2.0 * y, -2.0 * z] + [zero] * 11, axis=0)
    a, b, c = direction
    t3 = 3.0 * (a * x + b * y + c * z)
    return jnp.concatenate([
        zero, zero, zero, zero, zero, r * a - t3 * x, r * b - t3 * y,
        a * x + t3, 3.0 * b * x - 2.0 * a * y, 3.0 * c * x - 2.0 * a * z,
        3.0 * a * y - 2.0 * b * x, b * y + t3, 3.0 * c * y - 2.0 * b * z,
        a, b, -3.0 * c], axis=0)


def stage_kernel(first, last, source, piece, target, *rest):
    (columns, near_list, far_chunks, far_marks, counters, shear_part, normal_part,
     weights, factors) = rest[-9:]
    if last:
        earlier, (shear_ref, normal_ref) = rest[:-11], rest[-11:-9]
    else:
        earlier, sums_ref = (), rest[-10]
    held_blocks = piece.shape[0]
    per_block = target.shape[1]
    per_chunks = per_block // LANES
    total_chunks = held_blocks * per_chunks

    def runs(ref, at):
        return jnp.concatenate([ref[at:at + 1, t * LANES:(t + 1) * LANES]
                                for t in range(per_chunks)], axis=0)

    low = jnp.concatenate([runs(piece.at[p], 6) for p in range(held_blocks)], axis=0)
    high = jnp.concatenate([runs(piece.at[p], 7) for p in range(held_blocks)], axis=0)
    own_low, own_high = runs(source, 6), runs(source, 7)
    lane = lax.broadcasted_iota(jnp.int32, (1, LANES), 1)
    center = 0.5 * (jnp.min(own_low, axis=0, keepdims=True)
                    + jnp.max(own_high, axis=0, keepdims=True))
    is_axis = (lane == 0) | (lane == TURNS // 2) | (lane == TURNS)

    def reach(low, high):
        out = jnp.maximum(jnp.abs(low - center), jnp.abs(high - center))
        return jnp.sqrt(jnp.sum(jnp.where(is_axis, out * out, 0.0), axis=1, keepdims=True))

    source_reach, own_reach = reach(low, high), reach(own_low, own_high)
    marks = jnp.zeros((total_chunks, 1), jnp.int32)
    for t in range(per_chunks):
        apart = jnp.maximum(low - own_high[t:t + 1, :], own_low[t:t + 1, :] - high)
        gap = jnp.max(jnp.where(lane <= TURNS, apart, 0.0), axis=1, keepdims=True)
        gap = jnp.maximum(gap, 0.0)
        both = source_reach + own_reach[t:t + 1, :]
        is_near = (gap * gap + SMALLEST) * SPREAD_LIMIT < both * both
        marks = marks + jnp.where(is_near, 1 << t, 0)
    middle = [center[0:1, k:k + 1] for k in (0, TURNS // 2, TURNS)]
    blocks = []
    for p in range(held_blocks):
        top = p * per_chunks
        held = marks[top:top + per_chunks, :]
        count = low[top, COUNT_LANE].astype(jnp.int32)
        blocks.append((held, jnp.max(held), (count + LANES - 1) // LANES,
                       target[11, first + p].astype(jnp.int32)))

    def pad(chunks, position):
        rest = lax.rem(WIDE - lax.rem(position, WIDE), WIDE)

        def put(at, carry):
            chunks[position + at] = total_chunks
            far_marks[position + at] = 0
            return carry

        lax.fori_loop(0, rest, put, 0)
        return position + rest

    counters[0] = 0
    counters[1] = 0
    for p, (held, any_near, chunk_count, linked) in enumerate(blocks):
        @pl.when(any_near > 0)
        def near_block(p=p, held=held, chunk_count=chunk_count, linked=linked):
            pairs, position = counters[0], counters[1]
            for t in range(per_chunks):
                chunk = p * per_chunks + t
                mark = jnp.where(t < chunk_count, held[t, 0], 0)
                far_chunks[position + t] = chunk
                far_marks[position + t] = mark * 2 + linked
                for run in range(per_chunks):
                    near_list[pairs] = (chunk * per_chunks + run) * 2 + linked
                    pairs = pairs + (lax.shift_right_logical(mark, run) & 1)
            counters[0] = pairs
            counters[1] = position + chunk_count

    near_pairs = counters[0]
    for spare in range(PAIRS - 1):
        near_list[near_pairs + spare] = total_chunks * per_chunks * 2
    near_steps = (near_pairs + PAIRS - 1) // PAIRS

    def list_blocks(wanted, start):
        position = start
        for p, (_, any_near, chunk_count, linked) in enumerate(blocks):
            here = jnp.where((any_near == 0) & (linked == wanted), chunk_count, 0)

            def put(at, carry, p=p, position=position):
                far_chunks[position + at] = p * per_chunks + at
                far_marks[position + at] = wanted
                return carry

            lax.fori_loop(0, here, put, 0)
            position = position + here
        return pad(far_chunks, position)

    far_mixed = list_blocks(1, counters[1])
    far_all = list_blocks(0, far_mixed)

    def chunk_of(chunk):
        real = jnp.minimum(chunk, total_chunks - 1)
        lo = pl.multiple_of(lax.rem(real, per_chunks) * LANES, LANES)
        held = piece[real // per_chunks, :, pl.ds(lo, LANES)]
        row = lax.broadcasted_iota(jnp.int32, (8, LANES), 0)
        blank = jnp.where(row == 3, 1.0, 0.0)
        return jnp.where((row >= 3) & (chunk == total_chunks), blank, held)

    def place_far(at, carry):
        for k in range(WIDE):
            number = at * WIDE + k
            pieces = three_pieces(source_features(chunk_of(far_chunks[number]), middle))
            lo = pl.multiple_of(number * LANES, LANES)
            for slot, which in enumerate(SOURCE_PIECES):
                weights[slot * FEATURES:(slot + 1) * FEATURES, pl.ds(lo, LANES)] = pieces[which]
        return carry

    lax.fori_loop(0, far_all // WIDE, place_far, 0)

    own = target[...]
    zero_row = jnp.zeros((1, per_block), jnp.float32)
    ways = (None, (own[4:5], own[5:6], zero_row), (own[6:7], own[7:8], own[8:9]))
    for which, way in enumerate(ways):
        pieces = three_pieces(target_features(own, middle, way))
        stacked = jnp.concatenate(
            [pieces[k].astype(jnp.float32) for k in TARGET_PIECES]
            + [jnp.zeros((LANES - DEPTH, per_block), jnp.float32)], axis=0)
        factors[which, :, :] = stacked.T.astype(jnp.bfloat16)

    shear_part[...] = jnp.zeros_like(shear_part)
    normal_part[...] = jnp.zeros_like(normal_part)

    @pl.when(near_pairs > 0)
    def spread_columns():
        turned = own.T
        for row in range(FRAME):
            columns[row, :, :] = jnp.broadcast_to(turned[:, row:row + 1], (per_block, LANES))

    def near_step(at, carry):
        work = []
        for k in range(PAIRS):
            code = near_list[at * PAIRS + k]
            chunk = lax.shift_right_logical(code, 1) // per_chunks
            held = chunk_of(chunk)
            fields = [jnp.broadcast_to(held[row:row + 1, :], (8, LANES)) for row in range(FIELDS)]
            run = lax.shift_right_logical(code, 1) & (per_chunks - 1)
            work.append(((code & 1) == 1, run, fields))
        for sub in range(LANES // 8):
            for linked, run, fields in work:
                rows = pl.ds(pl.multiple_of(run * LANES + 8 * sub, 8), 8)
                x, y, z, s2, tx, ty, nx, ny, nz = (columns[row, rows, :] for row in range(FRAME))
                fx, fy, fz = pair_sums((x, y, z, s2), fields.__getitem__)
                shear_part[rows, :] += tx * fx + ty * fy
                normal_part[rows, :] += jnp.where(linked, nx * fx + ny * fy + nz * fz, 0.0)
        return carry

    lax.fori_loop(0, near_steps, near_step, 0)

    def far_step(mixed, at, carry):
        lo = pl.multiple_of(at * WIDE * LANES, WIDE * LANES)
        sources = weights[:, pl.ds(lo, WIDE * LANES)]

        held_marks = [far_marks[at * WIDE + k] for k in range(WIDE)] if mixed else None
        for top in range(0, per_block, TALL):
            def product(which):
                return jnp.dot(factors[which, top:top + TALL, 0:DEPTH], sources,
                               preferred_element_type=jnp.float32)

            def add(part, terms, linked_only):
                total = None
                for k in range(WIDE):
                    term = terms[:, k * LANES:(k + 1) * LANES]
                    if mixed:
                        mark = held_marks[k]
                        keep = (lax.shift_right_logical(mark, top // TALL + 1) & 1) == 0
                        if linked_only:
                            keep = keep & ((mark & 1) == 1)
                        term = jnp.where(keep, term, 0.0)
                    total = term if total is None else total + term
                part[top:top + TALL, :] += total

            root = lax.rsqrt(product(0))
            inverse = root * root
            fourth = inverse * inverse
            add(shear_part, (product(1) * root) * fourth, False)
            if mixed:
                add(normal_part, (product(2) * root) * fourth, True)
        return carry

    mixed_steps, far_steps = far_mixed // WIDE, far_all // WIDE
    lax.fori_loop(0, mixed_steps, functools.partial(far_step, True), 0)
    lax.fori_loop(mixed_steps, far_steps, functools.partial(far_step, False), 0)

    ones = jnp.ones((8, LANES), jnp.bfloat16)
    dims = (((1,), (1,)), ((), ()))
    sums = []
    for at, part in enumerate((shear_part, normal_part)):
        first_sum, second_sum, third_sum = (
            lax.dot_general(ones, piece_of, dims, preferred_element_type=jnp.float32)[0:1, :]
            for piece_of in three_pieces(part[...]))
        summed = first_sum + (second_sum + third_sum)
        for other in earlier:
            summed = summed + other[at:at + 1, :]
        sums.append(summed)
    if not last:
        for at in range(2):
            sums_ref[at:at + 1, :] = sums[at]
        return
    both = jnp.concatenate([jnp.where(own[9:10, :] > 0.0, one * own[9:10, :], 0.0) for one in sums]
                           + [jnp.zeros((14, per_block), jnp.float32)], axis=0)
    pieces = jnp.concatenate(three_pieces(both), axis=0)
    step = math.gcd(per_block, 256)
    slot = lax.broadcasted_iota(jnp.int32, (per_block, 1), 0).astype(jnp.float32)
    for at in range(0, per_block, step):
        pick = jnp.where(slot == own[10:11, at:at + step], 1.0, 0.0).astype(jnp.bfloat16)
        three = jnp.dot(pieces, pick, preferred_element_type=jnp.float32)
        back = three[0:16, :] + (three[16:32, :] + three[32:48, :])
        shear_ref[:, at:at + step] = back[0:1, :]
        normal_ref[:, at:at + step] = back[1:2, :]


def body(centroid, angles, size, slip_rate, live_count, near):
    per_block = centroid.shape[1]
    count_blocks = near.shape[1]
    smem = pl.BlockSpec(memory_space=pltpu.SMEM)
    vmem = pl.BlockSpec(memory_space=pltpu.VMEM)
    me = lax.axis_index("blocks").astype(jnp.int32).reshape(1)
    links = jnp.pad(near.astype(jnp.float32), ((0, 0), (0, per_block - count_blocks)))
    given = jnp.concatenate([centroid, angles, size[None], slip_rate[None], links], axis=0)
    source, target = pl.pallas_call(
        functools.partial(prep_kernel, count_blocks),
        out_shape=(jax.ShapeDtypeStruct((8, per_block), jnp.float32),
                   jax.ShapeDtypeStruct((16, per_block), jnp.float32)),
        in_specs=[smem, smem, vmem],
        out_specs=(vmem, vmem),
        compiler_params=pltpu.CompilerParams(vmem_limit_bytes=16 * 1024 * 1024),
    )(me, live_count, given)

    def stage(piece, first, earlier, last):
        held_blocks = piece.shape[0]
        total_chunks = held_blocks * per_block // LANES
        row = jax.ShapeDtypeStruct((1, per_block), jnp.float32)
        pairs = per_block * per_block * held_blocks
        return pl.pallas_call(
            functools.partial(stage_kernel, first, last),
            out_shape=(row, row) if last else jax.ShapeDtypeStruct((8, per_block), jnp.float32),
            in_specs=[vmem] * (3 + len(earlier)),
            out_specs=(vmem, vmem) if last else vmem,
            scratch_shapes=[
                pltpu.VMEM((FRAME, per_block, LANES), jnp.float32),
                pltpu.SMEM((total_chunks * (per_block // LANES) + 8,), jnp.int32),
                pltpu.SMEM((total_chunks + per_block // LANES + 2 * WIDE,), jnp.int32),
                pltpu.SMEM((total_chunks + per_block // LANES + 2 * WIDE,), jnp.int32),
                pltpu.SMEM((2,), jnp.int32),
                pltpu.VMEM((per_block, LANES), jnp.float32),
                pltpu.VMEM((per_block, LANES), jnp.float32),
                pltpu.VMEM((DEPTH, (total_chunks + 2 * WIDE) * LANES), jnp.bfloat16),
                pltpu.VMEM((3, per_block, LANES), jnp.bfloat16),
            ],
            compiler_params=pltpu.CompilerParams(vmem_limit_bytes=20 * 1024 * 1024),
            cost_estimate=pl.CostEstimate(flops=pairs * 2 * DEPTH * 4, bytes_accessed=pairs,
                                          transcendentals=pairs),
        )(source, piece, target, *earlier)

    def exchange(held, bit):
        return lax.ppermute(held, "blocks", [(one, one ^ bit) for one in range(count_blocks)])

    bits = exchanges(count_blocks)
    rounds = [[bits[1], bits[2], bits[1] | bits[2]]] + [[bit] for bit in bits[3:]]
    held = jnp.concatenate([source[None], exchange(source[None], bits[0])], axis=0)
    fresh, first, sums = held, 0, []
    for offsets in rounds:
        coming = [exchange(held, bit) for bit in offsets]
        sums.append(stage(fresh, first, (), False))
        first = held.shape[0]
        fresh = jnp.concatenate(coming, axis=0) if len(coming) > 1 else coming[0]
        held = jnp.concatenate([held, fresh], axis=0)
    shear, normal = stage(fresh, first, sums, True)
    return shear.reshape(per_block), normal.reshape(per_block)


def solution(mesh):
    in_specs = (
        P(None, ("runs", "blocks")),
        P(None, ("runs", "blocks")),
        P(("runs", "blocks")),
        P(("runs", "blocks")),
        P(("runs", "blocks")),
        P(("runs", "blocks"), None),
    )
    out_specs = (P(("runs", "blocks")), P(("runs", "blocks")))
    return jax.shard_map(body, mesh=mesh, in_specs=in_specs, out_specs=out_specs, check_vma=False)
```

```python
import functools
import math

import jax
import jax.numpy as jnp
from jax import lax
from jax.experimental import pallas as pl
from jax.experimental.pallas import tpu as pltpu
from jax.sharding import PartitionSpec as P

coupling = 0.002
LANES = 128
FIELDS = 6
FRAME = 9
WIDE = 4
PAIRS = 2
TALL = 128
TURNS = 64
COUNT_LANE = 127
BIG = 1e15
SMALLEST = 2e-6
SPREAD_LIMIT = 1500.0
FEATURES = 16
SOURCE_PIECES = (0, 0, 1, 0, 2, 1)
TARGET_PIECES = (0, 1, 0, 2, 0, 1)
DEPTH = FEATURES * len(SOURCE_PIECES)


def exchanges(count_blocks):
    bits = [1 << at for at in range(count_blocks.bit_length() - 1)]
    return bits[:1] + bits[:0:-1]


def block_at(position, me, count_blocks):
    flipped = 0
    for at, bit in enumerate(exchanges(count_blocks)):
        flipped = flipped + ((position >> at) & 1) * bit
    return me ^ flipped


def three_pieces(value):
    first = value.astype(jnp.bfloat16)
    rest = value - first.astype(jnp.float32)
    second = rest.astype(jnp.bfloat16)
    third = (rest - second.astype(jnp.float32)).astype(jnp.bfloat16)
    return first, second, third


def ranks(key_row):
    per_block = key_row.shape[1]
    key_column = jnp.broadcast_to(key_row, (8, per_block)).T[:, 0:1]
    tile = (LANES, LANES)
    earlier = lax.broadcasted_iota(jnp.int32, tile, 0) < lax.broadcasted_iota(jnp.int32, tile, 1)

    def counted(before):
        return jnp.sum(jnp.where(before, 1.0, 0.0), axis=0, keepdims=True)

    total = jnp.zeros((1, per_block), jnp.float32)
    for top in range(0, per_block, LANES):
        other = key_column[top:top + LANES, :]
        end = top + LANES
        same = key_row[:, top:end]
        parts = [counted((other < same) | ((other == same) & earlier))]
        if top:
            parts.insert(0, counted(other < key_row[:, :top]))
        if end < per_block:
            parts.append(counted(other <= key_row[:, end:]))
        total = total + jnp.concatenate(parts, axis=1)
    return total


def prep_kernel(count_blocks, me_ref, given, source_ref, target_ref):
    per_block = given.shape[1]
    count = given[7:8, per_block - 1:per_block].astype(jnp.int32)
    strike, dip_angle, size, slip_rate = (given[row:row + 1, :] for row in range(3, 7))
    cos_p, sin_p = jnp.cos(strike), jnp.sin(strike)
    cos_q, sin_q = jnp.cos(dip_angle), jnp.sin(dip_angle)
    lane = lax.broadcasted_iota(jnp.int32, (1, per_block), 1)
    live = lane < count
    squared = size * size
    weight = slip_rate * squared
    place = [given[k:k + 1, :] for k in range(3)]

    extent = [jnp.max(jnp.where(live, row, -BIG), axis=1, keepdims=True)
              - jnp.min(jnp.where(live, row, BIG), axis=1, keepdims=True) for row in place]
    key = jnp.where((extent[0] >= extent[1]) & (extent[0] >= extent[2]), place[0],
                    jnp.where(extent[1] >= extent[2], place[1], place[2]))
    rank = ranks(jnp.where(live, key, BIG))
    rank_column = jnp.broadcast_to(rank, (8, per_block)).T[:, 0:1]

    zero = jnp.zeros((5, per_block), jnp.float32)
    rows = jnp.concatenate(place + [squared, weight * cos_p, weight * sin_p, cos_p, sin_p,
                                    -sin_q * sin_p, sin_q * cos_p, cos_q, zero], axis=0)
    pieces = jnp.concatenate(three_pieces(rows), axis=0)
    step = math.gcd(per_block, 256)
    parts = []
    for at in range(0, per_block, step):
        wanted = jnp.minimum(lax.broadcasted_iota(jnp.int32, (1, step), 1) + at, count - 1)
        pick = jnp.where(rank_column == wanted.astype(jnp.float32), 1.0, 0.0).astype(jnp.bfloat16)
        three = jnp.dot(pieces, pick, preferred_element_type=jnp.float32)
        parts.append(three[0:16, :] + (three[16:32, :] + three[32:48, :]))
    ordered = jnp.concatenate(parts, axis=1)

    source_ref[0:4, :] = ordered[0:4, :]
    source_ref[4:6, :] = jnp.where(live, ordered[4:6, :], 0.0)
    target_ref[0:4, :] = ordered[0:4, :]
    target_ref[4:9, :] = ordered[6:11, :]
    target_ref[9:10, :] = jnp.where(live, coupling, 0.0)
    target_ref[10:11, :] = rank
    links = jnp.broadcast_to(given[7:8, 0:LANES], (8, LANES)).T[:, 0:1]
    position = lax.broadcasted_iota(jnp.int32, (1, LANES), 1)
    number = lax.broadcasted_iota(jnp.int32, (LANES, 1), 0)
    links = jnp.sum(jnp.where(number == block_at(position, me_ref[0], count_blocks), links, 0.0),
                    axis=0, keepdims=True)
    target_ref[11:16, :] = zero
    target_ref[11:12, 0:LANES] = links

    turn = lax.broadcasted_iota(jnp.int32, (TURNS, 1), 0).astype(jnp.float32) * (math.pi / TURNS)
    along = jnp.cos(turn) * ordered[0:1, :] + jnp.sin(turn) * ordered[1:2, :]
    all_rows = jnp.concatenate([along, jnp.broadcast_to(ordered[2:3, :], (8, per_block))], axis=0)
    row = lax.broadcasted_iota(jnp.int32, (TURNS + 8, LANES), 0)
    column = lax.broadcasted_iota(jnp.int32, (TURNS + 8, LANES), 1)
    for lo in range(0, per_block, LANES):
        here = all_rows[:, lo:lo + LANES]
        used = live[:, lo:lo + LANES]
        for at, ends in ((6, jnp.min(jnp.where(used, here, BIG), axis=1, keepdims=True)),
                         (7, jnp.max(jnp.where(used, here, -BIG), axis=1, keepdims=True))):
            line = jnp.sum(jnp.where(row == column, ends, 0.0), axis=0, keepdims=True)
            line = jnp.where(column[0:1, :] == COUNT_LANE, count.astype(jnp.float32), line)
            source_ref[at:at + 1, lo:lo + LANES] = line


def pair_sums(columns, field):
    x, y, z, s2 = columns
    rx = x - field(0)
    ry = y - field(1)
    rz = z - field(2)
    d2 = (rx * rx + ry * ry) + (rz * rz + (s2 + field(3)))
    root = lax.rsqrt(d2)
    inverse = root * root
    cube = inverse * root
    ux, uy = field(4), field(5)
    bent = (cube * inverse) * (ux * rx + uy * ry)
    bent = 3.0 * bent
    return cube * ux - bent * rx, cube * uy - bent * ry, -bent * rz


def source_features(held, middle):
    x, y, z = (held[k:k + 1, :] - middle[k] for k in range(3))
    ux, uy = held[4:5, :], held[5:6, :]
    s = x * x + y * y + z * z + held[3:4, :]
    uxx, uxy, uxz, uyx, uyy, uyz = ux * x, ux * y, ux * z, uy * x, uy * y, uy * z
    along = uxx + uyy
    along3 = 3.0 * along
    return jnp.concatenate([
        jnp.ones_like(x), s, x, y, z, ux, uy, uxx, uxy, uxz, uyx, uyy, uyz,
        s * ux - along3 * x, s * uy - along3 * y, z * along], axis=0)


def target_features(held, middle, direction):
    x, y, z = (held[k:k + 1, :] - middle[k] for k in range(3))
    r = x * x + y * y + z * z + held[3:4, :]
    zero, one = jnp.zeros_like(x), jnp.ones_like(x)
    if direction is None:
        return jnp.concatenate([r, one, -2.0 * x, -2.0 * y, -2.0 * z] + [zero] * 11, axis=0)
    a, b, c = direction
    t3 = 3.0 * (a * x + b * y + c * z)
    return jnp.concatenate([
        zero, zero, zero, zero, zero, r * a - t3 * x, r * b - t3 * y,
        a * x + t3, 3.0 * b * x - 2.0 * a * y, 3.0 * c * x - 2.0 * a * z,
        3.0 * a * y - 2.0 * b * x, b * y + t3, 3.0 * c * y - 2.0 * b * z,
        a, b, -3.0 * c], axis=0)


def stage_kernel(first, last, source, piece, target, *rest):
    (columns, near_list, far_chunks, far_marks, counters, shear_part, normal_part,
     weights, factors) = rest[-9:]
    if last:
        earlier, (shear_ref, normal_ref) = rest[:-11], rest[-11:-9]
    else:
        earlier, sums_ref = (), rest[-10]
    held_blocks = piece.shape[0]
    per_block = target.shape[1]
    per_chunks = per_block // LANES
    total_chunks = held_blocks * per_chunks

    def runs(ref, at):
        return jnp.concatenate([ref[at:at + 1, t * LANES:(t + 1) * LANES]
                                for t in range(per_chunks)], axis=0)

    low = jnp.concatenate([runs(piece.at[p], 6) for p in range(held_blocks)], axis=0)
    high = jnp.concatenate([runs(piece.at[p], 7) for p in range(held_blocks)], axis=0)
    own_low, own_high = runs(source, 6), runs(source, 7)
    lane = lax.broadcasted_iota(jnp.int32, (1, LANES), 1)
    center = 0.5 * (jnp.min(own_low, axis=0, keepdims=True)
                    + jnp.max(own_high, axis=0, keepdims=True))
    is_axis = (lane == 0) | (lane == TURNS // 2) | (lane == TURNS)

    def reach(low, high):
        out = jnp.maximum(jnp.abs(low - center), jnp.abs(high - center))
        return jnp.sqrt(jnp.sum(jnp.where(is_axis, out * out, 0.0), axis=1, keepdims=True))

    source_reach, own_reach = reach(low, high), reach(own_low, own_high)
    marks = jnp.zeros((total_chunks, 1), jnp.int32)
    for t in range(per_chunks):
        apart = jnp.maximum(low - own_high[t:t + 1, :], own_low[t:t + 1, :] - high)
        gap = jnp.max(jnp.where(lane <= TURNS, apart, 0.0), axis=1, keepdims=True)
        gap = jnp.maximum(gap, 0.0)
        both = source_reach + own_reach[t:t + 1, :]
        is_near = (gap * gap + SMALLEST) * SPREAD_LIMIT < both * both
        marks = marks + jnp.where(is_near, 1 << t, 0)
    middle = [center[0:1, k:k + 1] for k in (0, TURNS // 2, TURNS)]
    blocks = []
    for p in range(held_blocks):
        top = p * per_chunks
        held = marks[top:top + per_chunks, :]
        count = low[top, COUNT_LANE].astype(jnp.int32)
        blocks.append((held, jnp.max(held), (count + LANES - 1) // LANES,
                       target[11, first + p].astype(jnp.int32)))

    def pad(chunks, position):
        rest = lax.rem(WIDE - lax.rem(position, WIDE), WIDE)

        def put(at, carry):
            chunks[position + at] = total_chunks
            far_marks[position + at] = 0
            return carry

        lax.fori_loop(0, rest, put, 0)
        return position + rest

    counters[0] = 0
    counters[1] = 0
    def list_near(wanted):
        for p, (held, any_near, chunk_count, linked) in enumerate(blocks):
            @pl.when((any_near > 0) & (linked == wanted))
            def near_block(p=p, held=held, chunk_count=chunk_count):
                pairs, position = counters[0], counters[1]
                for t in range(per_chunks):
                    chunk = p * per_chunks + t
                    mark = jnp.where(t < chunk_count, held[t, 0], 0)
                    far_chunks[position + t] = chunk
                    far_marks[position + t] = mark * 2 + wanted
                    for run in range(per_chunks):
                        near_list[pairs] = (chunk * per_chunks + run) * 2 + wanted
                        pairs = pairs + (lax.shift_right_logical(mark, run) & 1)
                counters[0] = pairs
                counters[1] = position + chunk_count

    def list_blocks(wanted, start):
        position = start
        for p, (_, any_near, chunk_count, linked) in enumerate(blocks):
            here = jnp.where((any_near == 0) & (linked == wanted), chunk_count, 0)

            def put(at, carry, p=p, position=position):
                far_chunks[position + at] = p * per_chunks + at
                far_marks[position + at] = wanted
                return carry

            lax.fori_loop(0, here, put, 0)
            position = position + here
        return position

    list_near(1)
    far_linked = list_blocks(1, counters[1])
    counters[1] = far_linked
    list_near(0)
    far_mixed = pad(far_chunks, counters[1])
    far_all = pad(far_chunks, list_blocks(0, far_mixed))
    near_pairs = counters[0]
    for spare in range(PAIRS - 1):
        near_list[near_pairs + spare] = total_chunks * per_chunks * 2
    near_steps = (near_pairs + PAIRS - 1) // PAIRS

    def chunk_of(chunk):
        real = jnp.minimum(chunk, total_chunks - 1)
        lo = pl.multiple_of(lax.rem(real, per_chunks) * LANES, LANES)
        held = piece[real // per_chunks, :, pl.ds(lo, LANES)]
        row = lax.broadcasted_iota(jnp.int32, (8, LANES), 0)
        blank = jnp.where(row == 3, 1.0, 0.0)
        return jnp.where((row >= 3) & (chunk == total_chunks), blank, held)

    def place_far(at, carry):
        for k in range(WIDE):
            number = at * WIDE + k
            pieces = three_pieces(source_features(chunk_of(far_chunks[number]), middle))
            lo = pl.multiple_of(number * LANES, LANES)
            for slot, which in enumerate(SOURCE_PIECES):
                weights[slot * FEATURES:(slot + 1) * FEATURES, pl.ds(lo, LANES)] = pieces[which]
        return carry

    lax.fori_loop(0, far_all // WIDE, place_far, 0)

    own = target[...]
    zero_row = jnp.zeros((1, per_block), jnp.float32)
    ways = (None, (own[4:5], own[5:6], zero_row), (own[6:7], own[7:8], own[8:9]))
    for which, way in enumerate(ways):
        pieces = three_pieces(target_features(own, middle, way))
        stacked = jnp.concatenate(
            [pieces[k].astype(jnp.float32) for k in TARGET_PIECES]
            + [jnp.zeros((LANES - DEPTH, per_block), jnp.float32)], axis=0)
        factors[which, :, :] = stacked.T.astype(jnp.bfloat16)

    shear_part[...] = jnp.zeros_like(shear_part)
    normal_part[...] = jnp.zeros_like(normal_part)

    @pl.when(near_pairs > 0)
    def spread_columns():
        turned = own.T
        for row in range(FRAME):
            columns[row, :, :] = jnp.broadcast_to(turned[:, row:row + 1], (per_block, LANES))

    def near_step(at, carry):
        work = []
        for k in range(PAIRS):
            code = near_list[at * PAIRS + k]
            chunk = lax.shift_right_logical(code, 1) // per_chunks
            held = chunk_of(chunk)
            fields = [jnp.broadcast_to(held[row:row + 1, :], (8, LANES)) for row in range(FIELDS)]
            run = lax.shift_right_logical(code, 1) & (per_chunks - 1)
            work.append(((code & 1) == 1, run, fields))
        for sub in range(LANES // 8):
            for linked, run, fields in work:
                rows = pl.ds(pl.multiple_of(run * LANES + 8 * sub, 8), 8)
                x, y, z, s2, tx, ty, nx, ny, nz = (columns[row, rows, :] for row in range(FRAME))
                fx, fy, fz = pair_sums((x, y, z, s2), fields.__getitem__)
                shear_part[rows, :] += tx * fx + ty * fy
                normal_part[rows, :] += jnp.where(linked, nx * fx + ny * fy + nz * fz, 0.0)
        return carry

    lax.fori_loop(0, near_steps, near_step, 0)

    def far_step(mixed, with_normal, at, carry):
        lo = pl.multiple_of(at * WIDE * LANES, WIDE * LANES)
        sources = weights[:, pl.ds(lo, WIDE * LANES)]

        held_marks = [far_marks[at * WIDE + k] for k in range(WIDE)] if mixed else None
        for top in range(0, per_block, TALL):
            def product(which):
                return jnp.dot(factors[which, top:top + TALL, 0:DEPTH], sources,
                               preferred_element_type=jnp.float32)

            def add(part, terms, linked_only):
                total = None
                for k in range(WIDE):
                    term = terms[:, k * LANES:(k + 1) * LANES]
                    if mixed:
                        mark = held_marks[k]
                        keep = (lax.shift_right_logical(mark, top // TALL + 1) & 1) == 0
                        if linked_only:
                            keep = keep & ((mark & 1) == 1)
                        term = jnp.where(keep, term, 0.0)
                    total = term if total is None else total + term
                part[top:top + TALL, :] += total

            root = lax.rsqrt(product(0))
            inverse = root * root
            fourth = inverse * inverse
            add(shear_part, (product(1) * root) * fourth, False)
            if with_normal:
                add(normal_part, (product(2) * root) * fourth, True)
        return carry

    ends = (0, (far_linked + WIDE - 1) // WIDE, far_mixed // WIDE, far_all // WIDE)
    for kind, way in enumerate(((True, True), (True, False), (False, False))):
        lax.fori_loop(ends[kind], ends[kind + 1], functools.partial(far_step, *way), 0)

    ones = jnp.ones((8, LANES), jnp.bfloat16)
    dims = (((1,), (1,)), ((), ()))
    sums = []
    for at, part in enumerate((shear_part, normal_part)):
        first_sum, second_sum, third_sum = (
            lax.dot_general(ones, piece_of, dims, preferred_element_type=jnp.float32)[0:1, :]
            for piece_of in three_pieces(part[...]))
        summed = first_sum + (second_sum + third_sum)
        for other in earlier:
            summed = summed + other[at:at + 1, :]
        sums.append(summed)
    if not last:
        for at in range(2):
            sums_ref[at:at + 1, :] = sums[at]
        return
    both = jnp.concatenate([jnp.where(own[9:10, :] > 0.0, one * own[9:10, :], 0.0) for one in sums]
                           + [jnp.zeros((14, per_block), jnp.float32)], axis=0)
    pieces = jnp.concatenate(three_pieces(both), axis=0)
    step = math.gcd(per_block, 256)
    slot = lax.broadcasted_iota(jnp.int32, (per_block, 1), 0).astype(jnp.float32)
    for at in range(0, per_block, step):
        pick = jnp.where(slot == own[10:11, at:at + step], 1.0, 0.0).astype(jnp.bfloat16)
        three = jnp.dot(pieces, pick, preferred_element_type=jnp.float32)
        back = three[0:16, :] + (three[16:32, :] + three[32:48, :])
        shear_ref[:, at:at + step] = back[0:1, :]
        normal_ref[:, at:at + step] = back[1:2, :]


def body(centroid, angles, size, slip_rate, live_count, near):
    per_block = centroid.shape[1]
    count_blocks = near.shape[1]
    smem = pl.BlockSpec(memory_space=pltpu.SMEM)
    vmem = pl.BlockSpec(memory_space=pltpu.VMEM)
    me = lax.axis_index("blocks").astype(jnp.int32).reshape(1)
    gap = jnp.zeros((1, per_block - count_blocks - 1), jnp.int32)
    links = jnp.concatenate([near, gap, live_count[None]], axis=1).astype(jnp.float32)
    given = jnp.concatenate([centroid, angles, size[None], slip_rate[None], links], axis=0)
    source, target = pl.pallas_call(
        functools.partial(prep_kernel, count_blocks),
        out_shape=(jax.ShapeDtypeStruct((8, per_block), jnp.float32),
                   jax.ShapeDtypeStruct((16, per_block), jnp.float32)),
        in_specs=[smem, vmem],
        out_specs=(vmem, vmem),
        compiler_params=pltpu.CompilerParams(vmem_limit_bytes=16 * 1024 * 1024),
    )(me, given)

    def stage(piece, first, earlier, last):
        held_blocks = piece.shape[0]
        total_chunks = held_blocks * per_block // LANES
        row = jax.ShapeDtypeStruct((1, per_block), jnp.float32)
        pairs = per_block * per_block * held_blocks
        return pl.pallas_call(
            functools.partial(stage_kernel, first, last),
            out_shape=(row, row) if last else jax.ShapeDtypeStruct((8, per_block), jnp.float32),
            in_specs=[vmem] * (3 + len(earlier)),
            out_specs=(vmem, vmem) if last else vmem,
            scratch_shapes=[
                pltpu.VMEM((FRAME, per_block, LANES), jnp.float32),
                pltpu.SMEM((total_chunks * (per_block // LANES) + 8,), jnp.int32),
                pltpu.SMEM((total_chunks + per_block // LANES + 2 * WIDE,), jnp.int32),
                pltpu.SMEM((total_chunks + per_block // LANES + 2 * WIDE,), jnp.int32),
                pltpu.SMEM((2,), jnp.int32),
                pltpu.VMEM((per_block, LANES), jnp.float32),
                pltpu.VMEM((per_block, LANES), jnp.float32),
                pltpu.VMEM((DEPTH, (total_chunks + 2 * WIDE) * LANES), jnp.bfloat16),
                pltpu.VMEM((3, per_block, LANES), jnp.bfloat16),
            ],
            compiler_params=pltpu.CompilerParams(vmem_limit_bytes=20 * 1024 * 1024),
            cost_estimate=pl.CostEstimate(flops=pairs * 2 * DEPTH * 4, bytes_accessed=pairs,
                                          transcendentals=pairs),
        )(source, piece, target, *earlier)

    def exchange(held, bit):
        return lax.ppermute(held, "blocks", [(one, one ^ bit) for one in range(count_blocks)])

    bits = exchanges(count_blocks)
    rounds = [[bits[1], bits[2], bits[1] | bits[2]]] + [[bit] for bit in bits[3:]]
    held = jnp.concatenate([source[None], exchange(source[None], bits[0])], axis=0)
    fresh, first, sums = held, 0, []
    for offsets in rounds:
        coming = [exchange(held, bit) for bit in offsets]
        sums.append(stage(fresh, first, (), False))
        first = held.shape[0]
        fresh = jnp.concatenate(coming, axis=0) if len(coming) > 1 else coming[0]
        held = jnp.concatenate([held, fresh], axis=0)
    shear, normal = stage(fresh, first, sums, True)
    return shear.reshape(per_block), normal.reshape(per_block)


def solution(mesh):
    in_specs = (
        P(None, ("runs", "blocks")),
        P(None, ("runs", "blocks")),
        P(("runs", "blocks")),
        P(("runs", "blocks")),
        P(("runs", "blocks")),
        P(("runs", "blocks"), None),
    )
    out_specs = (P(("runs", "blocks")), P(("runs", "blocks")))
    return jax.shard_map(body, mesh=mesh, in_specs=in_specs, out_specs=out_specs, check_vma=False)
```

```python
import functools
import math

import jax
import jax.numpy as jnp
from jax import lax
from jax.experimental import pallas as pl
from jax.experimental.pallas import tpu as pltpu
from jax.sharding import PartitionSpec as P

coupling = 0.002
LANES = 128
FIELDS = 6
FRAME = 9
WIDE = 4
PAIRS = 2
TALL = 128
TURNS = 64
COUNT_LANE = 127
BIG = 1e15
SMALLEST = 2e-6
SPREAD_LIMIT = 1500.0
FEATURES = 16
SOURCE_PIECES = (0, 0, 1, 0, 2, 1)
TARGET_PIECES = (0, 1, 0, 2, 0, 1)
DEPTH = FEATURES * len(SOURCE_PIECES)


def exchanges(count_blocks):
    bits = [1 << at for at in range(count_blocks.bit_length() - 1)]
    return bits[:1] + bits[:0:-1]


def block_at(position, me, count_blocks):
    flipped = 0
    for at, bit in enumerate(exchanges(count_blocks)):
        flipped = flipped + ((position >> at) & 1) * bit
    return me ^ flipped


def three_pieces(value):
    first = value.astype(jnp.bfloat16)
    rest = value - first.astype(jnp.float32)
    second = rest.astype(jnp.bfloat16)
    third = (rest - second.astype(jnp.float32)).astype(jnp.bfloat16)
    return first, second, third


def ranks(key_row):
    per_block = key_row.shape[1]
    key_column = jnp.broadcast_to(key_row, (8, per_block)).T[:, 0:1]
    tile = (LANES, LANES)
    earlier = lax.broadcasted_iota(jnp.int32, tile, 0) < lax.broadcasted_iota(jnp.int32, tile, 1)

    def counted(before):
        return jnp.sum(jnp.where(before, 1.0, 0.0), axis=0, keepdims=True)

    total = jnp.zeros((1, per_block), jnp.float32)
    for top in range(0, per_block, LANES):
        other = key_column[top:top + LANES, :]
        end = top + LANES
        same = key_row[:, top:end]
        parts = [counted((other < same) | ((other == same) & earlier))]
        if top:
            parts.insert(0, counted(other < key_row[:, :top]))
        if end < per_block:
            parts.append(counted(other <= key_row[:, end:]))
        total = total + jnp.concatenate(parts, axis=1)
    return total


def prep_kernel(count_blocks, me_ref, given, source_ref, target_ref):
    per_block = given.shape[1]
    count = given[7:8, per_block - 1:per_block].astype(jnp.int32)
    strike, dip_angle, size, slip_rate = (given[row:row + 1, :] for row in range(3, 7))
    cos_p, sin_p = jnp.cos(strike), jnp.sin(strike)
    cos_q, sin_q = jnp.cos(dip_angle), jnp.sin(dip_angle)
    lane = lax.broadcasted_iota(jnp.int32, (1, per_block), 1)
    live = lane < count
    squared = size * size
    weight = slip_rate * squared
    place = [given[k:k + 1, :] for k in range(3)]

    extent = [jnp.max(jnp.where(live, row, -BIG), axis=1, keepdims=True)
              - jnp.min(jnp.where(live, row, BIG), axis=1, keepdims=True) for row in place]
    key = jnp.where((extent[0] >= extent[1]) & (extent[0] >= extent[2]), place[0],
                    jnp.where(extent[1] >= extent[2], place[1], place[2]))
    rank = ranks(jnp.where(live, key, BIG))
    rank_column = jnp.broadcast_to(rank, (8, per_block)).T[:, 0:1]

    zero = jnp.zeros((5, per_block), jnp.float32)
    rows = jnp.concatenate(place + [squared, weight * cos_p, weight * sin_p, cos_p, sin_p,
                                    -sin_q * sin_p, sin_q * cos_p, cos_q, zero], axis=0)
    pieces = jnp.concatenate(three_pieces(rows), axis=0)
    step = math.gcd(per_block, 256)
    parts = []
    for at in range(0, per_block, step):
        wanted = jnp.minimum(lax.broadcasted_iota(jnp.int32, (1, step), 1) + at, count - 1)
        pick = jnp.where(rank_column == wanted.astype(jnp.float32), 1.0, 0.0).astype(jnp.bfloat16)
        three = jnp.dot(pieces, pick, preferred_element_type=jnp.float32)
        parts.append(three[0:16, :] + (three[16:32, :] + three[32:48, :]))
    ordered = jnp.concatenate(parts, axis=1)

    source_ref[0:4, :] = ordered[0:4, :]
    source_ref[4:6, :] = jnp.where(live, ordered[4:6, :], 0.0)
    target_ref[0:4, :] = ordered[0:4, :]
    target_ref[4:9, :] = ordered[6:11, :]
    target_ref[9:10, :] = jnp.where(live, coupling, 0.0)
    target_ref[10:11, :] = rank
    links = jnp.broadcast_to(given[7:8, 0:LANES], (8, LANES)).T[:, 0:1]
    position = lax.broadcasted_iota(jnp.int32, (1, LANES), 1)
    number = lax.broadcasted_iota(jnp.int32, (LANES, 1), 0)
    links = jnp.sum(jnp.where(number == block_at(position, me_ref[0], count_blocks), links, 0.0),
                    axis=0, keepdims=True)
    target_ref[11:16, :] = zero
    target_ref[11:12, 0:LANES] = links

    turn = lax.broadcasted_iota(jnp.int32, (TURNS, 1), 0).astype(jnp.float32) * (math.pi / TURNS)
    along = jnp.cos(turn) * ordered[0:1, :] + jnp.sin(turn) * ordered[1:2, :]
    all_rows = jnp.concatenate([along, jnp.broadcast_to(ordered[2:3, :], (8, per_block))], axis=0)
    row = lax.broadcasted_iota(jnp.int32, (TURNS + 8, LANES), 0)
    column = lax.broadcasted_iota(jnp.int32, (TURNS + 8, LANES), 1)
    for lo in range(0, per_block, LANES):
        here = all_rows[:, lo:lo + LANES]
        used = live[:, lo:lo + LANES]
        for at, ends in ((6, jnp.min(jnp.where(used, here, BIG), axis=1, keepdims=True)),
                         (7, jnp.max(jnp.where(used, here, -BIG), axis=1, keepdims=True))):
            line = jnp.sum(jnp.where(row == column, ends, 0.0), axis=0, keepdims=True)
            line = jnp.where(column[0:1, :] == COUNT_LANE, count.astype(jnp.float32), line)
            source_ref[at:at + 1, lo:lo + LANES] = line


def pair_sums(columns, field):
    x, y, z, s2 = columns
    rx = x - field(0)
    ry = y - field(1)
    rz = z - field(2)
    d2 = (rx * rx + ry * ry) + (rz * rz + (s2 + field(3)))
    root = lax.rsqrt(d2)
    inverse = root * root
    cube = inverse * root
    ux, uy = field(4), field(5)
    bent = (cube * inverse) * (ux * rx + uy * ry)
    bent = 3.0 * bent
    return cube * ux - bent * rx, cube * uy - bent * ry, -bent * rz


def source_features(held, middle):
    x, y, z = (held[k:k + 1, :] - middle[k] for k in range(3))
    ux, uy = held[4:5, :], held[5:6, :]
    s = x * x + y * y + z * z + held[3:4, :]
    uxx, uxy, uxz, uyx, uyy, uyz = ux * x, ux * y, ux * z, uy * x, uy * y, uy * z
    along = uxx + uyy
    along3 = 3.0 * along
    return jnp.concatenate([
        jnp.ones_like(x), s, x, y, z, ux, uy, uxx, uxy, uxz, uyx, uyy, uyz,
        s * ux - along3 * x, s * uy - along3 * y, z * along], axis=0)


def target_features(held, middle, direction):
    x, y, z = (held[k:k + 1, :] - middle[k] for k in range(3))
    r = x * x + y * y + z * z + held[3:4, :]
    zero, one = jnp.zeros_like(x), jnp.ones_like(x)
    if direction is None:
        return jnp.concatenate([r, one, -2.0 * x, -2.0 * y, -2.0 * z] + [zero] * 11, axis=0)
    a, b, c = direction
    t3 = 3.0 * (a * x + b * y + c * z)
    return jnp.concatenate([
        zero, zero, zero, zero, zero, r * a - t3 * x, r * b - t3 * y,
        a * x + t3, 3.0 * b * x - 2.0 * a * y, 3.0 * c * x - 2.0 * a * z,
        3.0 * a * y - 2.0 * b * x, b * y + t3, 3.0 * c * y - 2.0 * b * z,
        a, b, -3.0 * c], axis=0)


def stage_kernel(first, last, source, piece, target, *rest):
    if last:
        rest, (shear_part, normal_part) = rest[:-2], rest[-2:]
    (columns, near_list, far_chunks, far_marks, counters, weights, factors) = rest[-7:]
    earlier, outs = rest[:-9], rest[-9:-7]
    if last:
        shear_ref, normal_ref = outs
    else:
        shear_part, normal_part = outs
    held_blocks = piece.shape[0]
    per_block = target.shape[1]
    per_chunks = per_block // LANES
    total_chunks = held_blocks * per_chunks

    def runs(ref, at):
        return jnp.concatenate([ref[at:at + 1, t * LANES:(t + 1) * LANES]
                                for t in range(per_chunks)], axis=0)

    low = jnp.concatenate([runs(piece.at[p], 6) for p in range(held_blocks)], axis=0)
    high = jnp.concatenate([runs(piece.at[p], 7) for p in range(held_blocks)], axis=0)
    own_low, own_high = runs(source, 6), runs(source, 7)
    lane = lax.broadcasted_iota(jnp.int32, (1, LANES), 1)
    center = 0.5 * (jnp.min(own_low, axis=0, keepdims=True)
                    + jnp.max(own_high, axis=0, keepdims=True))
    is_axis = (lane == 0) | (lane == TURNS // 2) | (lane == TURNS)

    def reach(low, high):
        out = jnp.maximum(jnp.abs(low - center), jnp.abs(high - center))
        return jnp.sqrt(jnp.sum(jnp.where(is_axis, out * out, 0.0), axis=1, keepdims=True))

    source_reach, own_reach = reach(low, high), reach(own_low, own_high)
    marks = jnp.zeros((total_chunks, 1), jnp.int32)
    for t in range(per_chunks):
        apart = jnp.maximum(low - own_high[t:t + 1, :], own_low[t:t + 1, :] - high)
        gap = jnp.max(jnp.where(lane <= TURNS, apart, 0.0), axis=1, keepdims=True)
        gap = jnp.maximum(gap, 0.0)
        both = source_reach + own_reach[t:t + 1, :]
        is_near = (gap * gap + SMALLEST) * SPREAD_LIMIT < both * both
        marks = marks + jnp.where(is_near, 1 << t, 0)
    middle = [center[0:1, k:k + 1] for k in (0, TURNS // 2, TURNS)]
    blocks = []
    for p in range(held_blocks):
        top = p * per_chunks
        held = marks[top:top + per_chunks, :]
        count = low[top, COUNT_LANE].astype(jnp.int32)
        blocks.append((held, jnp.max(held), (count + LANES - 1) // LANES,
                       target[11, first + p].astype(jnp.int32)))

    def pad(chunks, position):
        rest = lax.rem(WIDE - lax.rem(position, WIDE), WIDE)

        def put(at, carry):
            chunks[position + at] = total_chunks
            far_marks[position + at] = 0
            return carry

        lax.fori_loop(0, rest, put, 0)
        return position + rest

    counters[0] = 0
    counters[1] = 0
    def list_near(wanted):
        for p, (held, any_near, chunk_count, linked) in enumerate(blocks):
            @pl.when((any_near > 0) & (linked == wanted))
            def near_block(p=p, held=held, chunk_count=chunk_count):
                pairs, position = counters[0], counters[1]
                for t in range(per_chunks):
                    chunk = p * per_chunks + t
                    mark = jnp.where(t < chunk_count, held[t, 0], 0)
                    far_chunks[position + t] = chunk
                    far_marks[position + t] = mark * 2 + wanted
                    for run in range(per_chunks):
                        near_list[pairs] = (chunk * per_chunks + run) * 2 + wanted
                        pairs = pairs + (lax.shift_right_logical(mark, run) & 1)
                counters[0] = pairs
                counters[1] = position + chunk_count

    def list_blocks(wanted, start):
        position = start
        for p, (_, any_near, chunk_count, linked) in enumerate(blocks):
            here = jnp.where((any_near == 0) & (linked == wanted), chunk_count, 0)

            def put(at, carry, p=p, position=position):
                far_chunks[position + at] = p * per_chunks + at
                far_marks[position + at] = wanted
                return carry

            lax.fori_loop(0, here, put, 0)
            position = position + here
        return position

    list_near(1)
    far_linked = list_blocks(1, counters[1])
    counters[1] = far_linked
    list_near(0)
    far_mixed = pad(far_chunks, counters[1])
    far_all = pad(far_chunks, list_blocks(0, far_mixed))
    near_pairs = counters[0]
    for spare in range(PAIRS - 1):
        near_list[near_pairs + spare] = total_chunks * per_chunks * 2
    near_steps = (near_pairs + PAIRS - 1) // PAIRS

    def chunk_of(chunk):
        real = jnp.minimum(chunk, total_chunks - 1)
        lo = pl.multiple_of(lax.rem(real, per_chunks) * LANES, LANES)
        held = piece[real // per_chunks, :, pl.ds(lo, LANES)]
        row = lax.broadcasted_iota(jnp.int32, (8, LANES), 0)
        blank = jnp.where(row == 3, 1.0, 0.0)
        return jnp.where((row >= 3) & (chunk == total_chunks), blank, held)

    def place_far(at, carry):
        for k in range(WIDE):
            number = at * WIDE + k
            pieces = three_pieces(source_features(chunk_of(far_chunks[number]), middle))
            lo = pl.multiple_of(number * LANES, LANES)
            for slot, which in enumerate(SOURCE_PIECES):
                weights[slot * FEATURES:(slot + 1) * FEATURES, pl.ds(lo, LANES)] = pieces[which]
        return carry

    lax.fori_loop(0, far_all // WIDE, place_far, 0)

    own = target[...]
    zero_row = jnp.zeros((1, per_block), jnp.float32)
    ways = (None, (own[4:5], own[5:6], zero_row), (own[6:7], own[7:8], own[8:9]))
    for which, way in enumerate(ways):
        pieces = three_pieces(target_features(own, middle, way))
        stacked = jnp.concatenate(
            [pieces[k].astype(jnp.float32) for k in TARGET_PIECES]
            + [jnp.zeros((LANES - DEPTH, per_block), jnp.float32)], axis=0)
        factors[which, :, :] = stacked.T.astype(jnp.bfloat16)

    for at, part in enumerate((shear_part, normal_part)):
        part[...] = earlier[at][...] if earlier else jnp.zeros_like(part)

    @pl.when(near_pairs > 0)
    def spread_columns():
        turned = own.T
        for row in range(FRAME):
            columns[row, :, :] = jnp.broadcast_to(turned[:, row:row + 1], (per_block, LANES))

    def near_step(at, carry):
        work = []
        for k in range(PAIRS):
            code = near_list[at * PAIRS + k]
            chunk = lax.shift_right_logical(code, 1) // per_chunks
            held = chunk_of(chunk)
            fields = [jnp.broadcast_to(held[row:row + 1, :], (8, LANES)) for row in range(FIELDS)]
            run = lax.shift_right_logical(code, 1) & (per_chunks - 1)
            work.append(((code & 1) == 1, run, fields))
        for sub in range(LANES // 8):
            for linked, run, fields in work:
                rows = pl.ds(pl.multiple_of(run * LANES + 8 * sub, 8), 8)
                x, y, z, s2, tx, ty, nx, ny, nz = (columns[row, rows, :] for row in range(FRAME))
                fx, fy, fz = pair_sums((x, y, z, s2), fields.__getitem__)
                shear_part[rows, :] += tx * fx + ty * fy
                normal_part[rows, :] += jnp.where(linked, nx * fx + ny * fy + nz * fz, 0.0)
        return carry

    lax.fori_loop(0, near_steps, near_step, 0)

    def far_step(mixed, with_normal, at, carry):
        lo = pl.multiple_of(at * WIDE * LANES, WIDE * LANES)
        sources = weights[:, pl.ds(lo, WIDE * LANES)]

        held_marks = [far_marks[at * WIDE + k] for k in range(WIDE)] if mixed else None
        for top in range(0, per_block, TALL):
            def product(which):
                return jnp.dot(factors[which, top:top + TALL, 0:DEPTH], sources,
                               preferred_element_type=jnp.float32)

            def add(part, terms, linked_only):
                total = None
                for k in range(WIDE):
                    term = terms[:, k * LANES:(k + 1) * LANES]
                    if mixed:
                        mark = held_marks[k]
                        keep = (lax.shift_right_logical(mark, top // TALL + 1) & 1) == 0
                        if linked_only:
                            keep = keep & ((mark & 1) == 1)
                        term = jnp.where(keep, term, 0.0)
                    total = term if total is None else total + term
                part[top:top + TALL, :] += total

            root = lax.rsqrt(product(0))
            inverse = root * root
            fourth = inverse * inverse
            add(shear_part, (product(1) * root) * fourth, False)
            if with_normal:
                add(normal_part, (product(2) * root) * fourth, True)
        return carry

    ends = (0, (far_linked + WIDE - 1) // WIDE, far_mixed // WIDE, far_all // WIDE)
    for kind, way in enumerate(((True, True), (True, False), (False, False))):
        lax.fori_loop(ends[kind], ends[kind + 1], functools.partial(far_step, *way), 0)

    if not last:
        return
    ones = jnp.ones((8, LANES), jnp.bfloat16)
    dims = (((1,), (1,)), ((), ()))
    sums = []
    for part in (shear_part, normal_part):
        first_sum, second_sum, third_sum = (
            lax.dot_general(ones, piece_of, dims, preferred_element_type=jnp.float32)[0:1, :]
            for piece_of in three_pieces(part[...]))
        sums.append(first_sum + (second_sum + third_sum))
    both = jnp.concatenate([jnp.where(own[9:10, :] > 0.0, one * own[9:10, :], 0.0) for one in sums]
                           + [jnp.zeros((14, per_block), jnp.float32)], axis=0)
    pieces = jnp.concatenate(three_pieces(both), axis=0)
    step = math.gcd(per_block, 256)
    slot = lax.broadcasted_iota(jnp.int32, (per_block, 1), 0).astype(jnp.float32)
    for at in range(0, per_block, step):
        pick = jnp.where(slot == own[10:11, at:at + step], 1.0, 0.0).astype(jnp.bfloat16)
        three = jnp.dot(pieces, pick, preferred_element_type=jnp.float32)
        back = three[0:16, :] + (three[16:32, :] + three[32:48, :])
        shear_ref[:, at:at + step] = back[0:1, :]
        normal_ref[:, at:at + step] = back[1:2, :]


def body(centroid, angles, size, slip_rate, live_count, near):
    per_block = centroid.shape[1]
    count_blocks = near.shape[1]
    smem = pl.BlockSpec(memory_space=pltpu.SMEM)
    vmem = pl.BlockSpec(memory_space=pltpu.VMEM)
    me = lax.axis_index("blocks").astype(jnp.int32).reshape(1)
    gap = jnp.zeros((1, per_block - count_blocks - 1), jnp.int32)
    links = jnp.concatenate([near, gap, live_count[None]], axis=1).astype(jnp.float32)
    given = jnp.concatenate([centroid, angles, size[None], slip_rate[None], links], axis=0)
    source, target = pl.pallas_call(
        functools.partial(prep_kernel, count_blocks),
        out_shape=(jax.ShapeDtypeStruct((8, per_block), jnp.float32),
                   jax.ShapeDtypeStruct((16, per_block), jnp.float32)),
        in_specs=[smem, vmem],
        out_specs=(vmem, vmem),
        compiler_params=pltpu.CompilerParams(vmem_limit_bytes=16 * 1024 * 1024),
    )(me, given)

    def stage(piece, first, earlier, last):
        held_blocks = piece.shape[0]
        total_chunks = held_blocks * per_block // LANES
        row = jax.ShapeDtypeStruct((1, per_block), jnp.float32)
        lanes = jax.ShapeDtypeStruct((per_block, LANES), jnp.float32)
        pairs = per_block * per_block * held_blocks
        return pl.pallas_call(
            functools.partial(stage_kernel, first, last),
            out_shape=(row, row) if last else (lanes, lanes),
            in_specs=[vmem] * (3 + len(earlier)),
            out_specs=(vmem, vmem),
            scratch_shapes=[
                pltpu.VMEM((FRAME, per_block, LANES), jnp.float32),
                pltpu.SMEM((total_chunks * (per_block // LANES) + 8,), jnp.int32),
                pltpu.SMEM((total_chunks + per_block // LANES + 2 * WIDE,), jnp.int32),
                pltpu.SMEM((total_chunks + per_block // LANES + 2 * WIDE,), jnp.int32),
                pltpu.SMEM((2,), jnp.int32),
                pltpu.VMEM((DEPTH, (total_chunks + 2 * WIDE) * LANES), jnp.bfloat16),
                pltpu.VMEM((3, per_block, LANES), jnp.bfloat16),
            ] + [pltpu.VMEM((per_block, LANES), jnp.float32)] * (2 if last else 0),
            compiler_params=pltpu.CompilerParams(vmem_limit_bytes=20 * 1024 * 1024),
            cost_estimate=pl.CostEstimate(flops=pairs * 2 * DEPTH * 4, bytes_accessed=pairs,
                                          transcendentals=pairs),
        )(source, piece, target, *earlier)

    def exchange(held, bit):
        return lax.ppermute(held, "blocks", [(one, one ^ bit) for one in range(count_blocks)])

    bits = exchanges(count_blocks)
    rounds = [[bits[1], bits[2], bits[1] | bits[2]]] + [[bit] for bit in bits[3:]]
    held = jnp.concatenate([source[None], exchange(source[None], bits[0])], axis=0)
    fresh, first, sums = held, 0, ()
    for offsets in rounds:
        coming = [exchange(held, bit) for bit in offsets]
        sums = stage(fresh, first, sums, False)
        first = held.shape[0]
        fresh = jnp.concatenate(coming, axis=0) if len(coming) > 1 else coming[0]
        held = jnp.concatenate([held, fresh], axis=0)
    shear, normal = stage(fresh, first, sums, True)
    return shear.reshape(per_block), normal.reshape(per_block)


def solution(mesh):
    in_specs = (
        P(None, ("runs", "blocks")),
        P(None, ("runs", "blocks")),
        P(("runs", "blocks")),
        P(("runs", "blocks")),
        P(("runs", "blocks")),
        P(("runs", "blocks"), None),
    )
    out_specs = (P(("runs", "blocks")), P(("runs", "blocks")))
    return jax.shard_map(body, mesh=mesh, in_specs=in_specs, out_specs=out_specs, check_vma=False)
```

```python
import functools
import math

import jax
import jax.numpy as jnp
from jax import lax
from jax.experimental import pallas as pl
from jax.experimental.pallas import tpu as pltpu
from jax.sharding import PartitionSpec as P

coupling = 0.002
LANES = 128
FIELDS = 6
FRAME = 9
WIDE = 4
PAIRS = 2
TALL = 128
TURNS = 64
COUNT_LANE = 127
BIG = 1e15
SMALLEST = 2e-6
SPREAD_LIMIT = 1500.0
FEATURES = 16
SOURCE_PIECES = (0, 0, 1, 0, 2, 1)
TARGET_PIECES = (0, 1, 0, 2, 0, 1)
DEPTH = FEATURES * len(SOURCE_PIECES)


def exchanges(count_blocks):
    bits = [1 << at for at in range(count_blocks.bit_length() - 1)]
    return bits[:1] + bits[:0:-1]


def block_at(position, me, count_blocks):
    flipped = 0
    for at, bit in enumerate(exchanges(count_blocks)):
        flipped = flipped + ((position >> at) & 1) * bit
    return me ^ flipped


def three_pieces(value):
    first = value.astype(jnp.bfloat16)
    rest = value - first.astype(jnp.float32)
    second = rest.astype(jnp.bfloat16)
    third = (rest - second.astype(jnp.float32)).astype(jnp.bfloat16)
    return first, second, third


def ranks(key_row):
    per_block = key_row.shape[1]
    key_column = jnp.broadcast_to(key_row, (8, per_block)).T[:, 0:1]
    tile = (LANES, LANES)
    earlier = lax.broadcasted_iota(jnp.int32, tile, 0) < lax.broadcasted_iota(jnp.int32, tile, 1)

    def counted(before):
        return jnp.sum(jnp.where(before, 1.0, 0.0), axis=0, keepdims=True)

    total = jnp.zeros((1, per_block), jnp.float32)
    for top in range(0, per_block, LANES):
        other = key_column[top:top + LANES, :]
        end = top + LANES
        same = key_row[:, top:end]
        parts = [counted((other < same) | ((other == same) & earlier))]
        if top:
            parts.insert(0, counted(other < key_row[:, :top]))
        if end < per_block:
            parts.append(counted(other <= key_row[:, end:]))
        total = total + jnp.concatenate(parts, axis=1)
    return total


def prep_kernel(count_blocks, me_ref, given, source_ref, target_ref):
    per_block = given.shape[1]
    count = given[7:8, per_block - 1:per_block].astype(jnp.int32)
    strike, dip_angle, size, slip_rate = (given[row:row + 1, :] for row in range(3, 7))
    cos_p, sin_p = jnp.cos(strike), jnp.sin(strike)
    cos_q, sin_q = jnp.cos(dip_angle), jnp.sin(dip_angle)
    lane = lax.broadcasted_iota(jnp.int32, (1, per_block), 1)
    live = lane < count
    squared = size * size
    weight = slip_rate * squared
    place = [given[k:k + 1, :] for k in range(3)]

    extent = [jnp.max(jnp.where(live, row, -BIG), axis=1, keepdims=True)
              - jnp.min(jnp.where(live, row, BIG), axis=1, keepdims=True) for row in place]
    key = jnp.where((extent[0] >= extent[1]) & (extent[0] >= extent[2]), place[0],
                    jnp.where(extent[1] >= extent[2], place[1], place[2]))
    rank = ranks(jnp.where(live, key, BIG))
    rank_column = jnp.broadcast_to(rank, (8, per_block)).T[:, 0:1]

    zero = jnp.zeros((5, per_block), jnp.float32)
    rows = jnp.concatenate(place + [squared, weight * cos_p, weight * sin_p, cos_p, sin_p,
                                    -sin_q * sin_p, sin_q * cos_p, cos_q, zero], axis=0)
    pieces = jnp.concatenate(three_pieces(rows), axis=0)
    step = math.gcd(per_block, 256)
    parts = []
    for at in range(0, per_block, step):
        wanted = jnp.minimum(lax.broadcasted_iota(jnp.int32, (1, step), 1) + at, count - 1)
        pick = jnp.where(rank_column == wanted.astype(jnp.float32), 1.0, 0.0).astype(jnp.bfloat16)
        three = jnp.dot(pieces, pick, preferred_element_type=jnp.float32)
        parts.append(three[0:16, :] + (three[16:32, :] + three[32:48, :]))
    ordered = jnp.concatenate(parts, axis=1)

    source_ref[0:4, :] = ordered[0:4, :]
    source_ref[4:6, :] = jnp.where(live, ordered[4:6, :], 0.0)
    target_ref[0:4, :] = ordered[0:4, :]
    target_ref[4:9, :] = ordered[6:11, :]
    target_ref[9:10, :] = jnp.where(live, coupling, 0.0)
    target_ref[10:11, :] = rank
    links = jnp.broadcast_to(given[7:8, 0:LANES], (8, LANES)).T[:, 0:1]
    position = lax.broadcasted_iota(jnp.int32, (1, LANES), 1)
    number = lax.broadcasted_iota(jnp.int32, (LANES, 1), 0)
    links = jnp.sum(jnp.where(number == block_at(position, me_ref[0], count_blocks), links, 0.0),
                    axis=0, keepdims=True)
    target_ref[11:16, :] = zero
    target_ref[11:12, 0:LANES] = links

    turn = lax.broadcasted_iota(jnp.int32, (TURNS, 1), 0).astype(jnp.float32) * (math.pi / TURNS)
    along = jnp.cos(turn) * ordered[0:1, :] + jnp.sin(turn) * ordered[1:2, :]
    all_rows = jnp.concatenate([along, jnp.broadcast_to(ordered[2:3, :], (8, per_block))], axis=0)
    row = lax.broadcasted_iota(jnp.int32, (TURNS + 8, LANES), 0)
    column = lax.broadcasted_iota(jnp.int32, (TURNS + 8, LANES), 1)
    for lo in range(0, per_block, LANES):
        here = all_rows[:, lo:lo + LANES]
        used = live[:, lo:lo + LANES]
        for at, ends in ((6, jnp.min(jnp.where(used, here, BIG), axis=1, keepdims=True)),
                         (7, jnp.max(jnp.where(used, here, -BIG), axis=1, keepdims=True))):
            line = jnp.sum(jnp.where(row == column, ends, 0.0), axis=0, keepdims=True)
            line = jnp.where(column[0:1, :] == COUNT_LANE, count.astype(jnp.float32), line)
            source_ref[at:at + 1, lo:lo + LANES] = line


def pair_sums(columns, field):
    x, y, z, s2 = columns
    rx = x - field(0)
    ry = y - field(1)
    rz = z - field(2)
    d2 = (rx * rx + ry * ry) + (rz * rz + (s2 + field(3)))
    root = lax.rsqrt(d2)
    inverse = root * root
    cube = inverse * root
    ux, uy = field(4), field(5)
    bent = (cube * inverse) * (ux * rx + uy * ry)
    bent = 3.0 * bent
    return cube * ux - bent * rx, cube * uy - bent * ry, -bent * rz


def source_features(held, middle):
    x, y, z = (held[k:k + 1, :] - middle[k] for k in range(3))
    ux, uy = held[4:5, :], held[5:6, :]
    s = x * x + y * y + z * z + held[3:4, :]
    uxx, uxy, uxz, uyx, uyy, uyz = ux * x, ux * y, ux * z, uy * x, uy * y, uy * z
    along = uxx + uyy
    along3 = 3.0 * along
    return jnp.concatenate([
        jnp.ones_like(x), s, x, y, z, ux, uy, uxx, uxy, uxz, uyx, uyy, uyz,
        s * ux - along3 * x, s * uy - along3 * y, z * along], axis=0)


def target_features(held, middle, direction):
    x, y, z = (held[k:k + 1, :] - middle[k] for k in range(3))
    r = x * x + y * y + z * z + held[3:4, :]
    zero, one = jnp.zeros_like(x), jnp.ones_like(x)
    if direction is None:
        return jnp.concatenate([r, one, -2.0 * x, -2.0 * y, -2.0 * z] + [zero] * 11, axis=0)
    a, b, c = direction
    t3 = 3.0 * (a * x + b * y + c * z)
    return jnp.concatenate([
        zero, zero, zero, zero, zero, r * a - t3 * x, r * b - t3 * y,
        a * x + t3, 3.0 * b * x - 2.0 * a * y, 3.0 * c * x - 2.0 * a * z,
        3.0 * a * y - 2.0 * b * x, b * y + t3, 3.0 * c * y - 2.0 * b * z,
        a, b, -3.0 * c], axis=0)


def stage_kernel(first, last, source, piece, target, *rest):
    if last:
        rest, (shear_part, normal_part) = rest[:-2], rest[-2:]
    (columns, near_list, far_chunks, far_marks, counters, weights) = rest[-6:]
    rest = rest[:-6]
    starts = not rest[3:]
    if starts:
        earlier, (shear_part, normal_part, factors) = (), rest
    else:
        earlier, factors, outs = rest[:2], rest[2], rest[3:]
        if last:
            shear_ref, normal_ref = outs
        else:
            shear_part, normal_part = outs
    held_blocks = piece.shape[0]
    per_block = target.shape[1]
    per_chunks = per_block // LANES
    total_chunks = held_blocks * per_chunks

    def runs(ref, at):
        return jnp.concatenate([ref[at:at + 1, t * LANES:(t + 1) * LANES]
                                for t in range(per_chunks)], axis=0)

    low = jnp.concatenate([runs(piece.at[p], 6) for p in range(held_blocks)], axis=0)
    high = jnp.concatenate([runs(piece.at[p], 7) for p in range(held_blocks)], axis=0)
    own_low, own_high = runs(source, 6), runs(source, 7)
    lane = lax.broadcasted_iota(jnp.int32, (1, LANES), 1)
    center = 0.5 * (jnp.min(own_low, axis=0, keepdims=True)
                    + jnp.max(own_high, axis=0, keepdims=True))
    is_axis = (lane == 0) | (lane == TURNS // 2) | (lane == TURNS)

    def reach(low, high):
        out = jnp.maximum(jnp.abs(low - center), jnp.abs(high - center))
        return jnp.sqrt(jnp.sum(jnp.where(is_axis, out * out, 0.0), axis=1, keepdims=True))

    source_reach, own_reach = reach(low, high), reach(own_low, own_high)
    marks = jnp.zeros((total_chunks, 1), jnp.int32)
    for t in range(per_chunks):
        apart = jnp.maximum(low - own_high[t:t + 1, :], own_low[t:t + 1, :] - high)
        gap = jnp.max(jnp.where(lane <= TURNS, apart, 0.0), axis=1, keepdims=True)
        gap = jnp.maximum(gap, 0.0)
        both = source_reach + own_reach[t:t + 1, :]
        is_near = (gap * gap + SMALLEST) * SPREAD_LIMIT < both * both
        marks = marks + jnp.where(is_near, 1 << t, 0)
    middle = [center[0:1, k:k + 1] for k in (0, TURNS // 2, TURNS)]
    blocks = []
    for p in range(held_blocks):
        top = p * per_chunks
        held = marks[top:top + per_chunks, :]
        count = low[top, COUNT_LANE].astype(jnp.int32)
        blocks.append((held, jnp.max(held), (count + LANES - 1) // LANES,
                       target[11, first + p].astype(jnp.int32)))

    def pad(chunks, position):
        rest = lax.rem(WIDE - lax.rem(position, WIDE), WIDE)

        def put(at, carry):
            chunks[position + at] = total_chunks
            far_marks[position + at] = 0
            return carry

        lax.fori_loop(0, rest, put, 0)
        return position + rest

    counters[0] = 0
    counters[1] = 0
    def list_near(wanted):
        for p, (held, any_near, chunk_count, linked) in enumerate(blocks):
            @pl.when((any_near > 0) & (linked == wanted))
            def near_block(p=p, held=held, chunk_count=chunk_count):
                pairs, position = counters[0], counters[1]
                for t in range(per_chunks):
                    chunk = p * per_chunks + t
                    mark = jnp.where(t < chunk_count, held[t, 0], 0)
                    far_chunks[position + t] = chunk
                    far_marks[position + t] = mark * 2 + wanted
                    for run in range(per_chunks):
                        near_list[pairs] = (chunk * per_chunks + run) * 2 + wanted
                        pairs = pairs + (lax.shift_right_logical(mark, run) & 1)
                counters[0] = pairs
                counters[1] = position + chunk_count

    def list_blocks(wanted, start):
        position = start
        for p, (_, any_near, chunk_count, linked) in enumerate(blocks):
            here = jnp.where((any_near == 0) & (linked == wanted), chunk_count, 0)

            def put(at, carry, p=p, position=position):
                far_chunks[position + at] = p * per_chunks + at
                far_marks[position + at] = wanted
                return carry

            lax.fori_loop(0, here, put, 0)
            position = position + here
        return position

    list_near(1)
    far_linked = list_blocks(1, counters[1])
    counters[1] = far_linked
    list_near(0)
    far_mixed = pad(far_chunks, counters[1])
    far_all = pad(far_chunks, list_blocks(0, far_mixed))
    near_pairs = counters[0]
    for spare in range(PAIRS - 1):
        near_list[near_pairs + spare] = total_chunks * per_chunks * 2
    near_steps = (near_pairs + PAIRS - 1) // PAIRS

    def chunk_of(chunk):
        real = jnp.minimum(chunk, total_chunks - 1)
        lo = pl.multiple_of(lax.rem(real, per_chunks) * LANES, LANES)
        held = piece[real // per_chunks, :, pl.ds(lo, LANES)]
        row = lax.broadcasted_iota(jnp.int32, (8, LANES), 0)
        blank = jnp.where(row == 3, 1.0, 0.0)
        return jnp.where((row >= 3) & (chunk == total_chunks), blank, held)

    def place_far(at, carry):
        for k in range(WIDE):
            number = at * WIDE + k
            pieces = three_pieces(source_features(chunk_of(far_chunks[number]), middle))
            lo = pl.multiple_of(number * LANES, LANES)
            for slot, which in enumerate(SOURCE_PIECES):
                weights[slot * FEATURES:(slot + 1) * FEATURES, pl.ds(lo, LANES)] = pieces[which]
        return carry

    lax.fori_loop(0, far_all // WIDE, place_far, 0)

    own = target[...]
    if starts:
        zero_row = jnp.zeros((1, per_block), jnp.float32)
        ways = (None, (own[4:5], own[5:6], zero_row), (own[6:7], own[7:8], own[8:9]))
        for which, way in enumerate(ways):
            pieces = three_pieces(target_features(own, middle, way))
            stacked = jnp.concatenate(
                [pieces[k].astype(jnp.float32) for k in TARGET_PIECES]
                + [jnp.zeros((LANES - DEPTH, per_block), jnp.float32)], axis=0)
            factors[which, :, :] = stacked.T.astype(jnp.bfloat16)

    for at, part in enumerate((shear_part, normal_part)):
        part[...] = earlier[at][...] if earlier else jnp.zeros_like(part)

    @pl.when(near_pairs > 0)
    def spread_columns():
        turned = own.T
        for row in range(FRAME):
            columns[row, :, :] = jnp.broadcast_to(turned[:, row:row + 1], (per_block, LANES))

    def near_step(at, carry):
        work = []
        for k in range(PAIRS):
            code = near_list[at * PAIRS + k]
            chunk = lax.shift_right_logical(code, 1) // per_chunks
            held = chunk_of(chunk)
            fields = [jnp.broadcast_to(held[row:row + 1, :], (8, LANES)) for row in range(FIELDS)]
            run = lax.shift_right_logical(code, 1) & (per_chunks - 1)
            work.append(((code & 1) == 1, run, fields))
        for sub in range(LANES // 8):
            for linked, run, fields in work:
                rows = pl.ds(pl.multiple_of(run * LANES + 8 * sub, 8), 8)
                x, y, z, s2, tx, ty, nx, ny, nz = (columns[row, rows, :] for row in range(FRAME))
                fx, fy, fz = pair_sums((x, y, z, s2), fields.__getitem__)
                shear_part[rows, :] += tx * fx + ty * fy
                normal_part[rows, :] += jnp.where(linked, nx * fx + ny * fy + nz * fz, 0.0)
        return carry

    lax.fori_loop(0, near_steps, near_step, 0)

    def far_step(mixed, with_normal, at, carry):
        lo = pl.multiple_of(at * WIDE * LANES, WIDE * LANES)
        sources = weights[:, pl.ds(lo, WIDE * LANES)]

        held_marks = [far_marks[at * WIDE + k] for k in range(WIDE)] if mixed else None
        for top in range(0, per_block, TALL):
            def product(which):
                return jnp.dot(factors[which, top:top + TALL, 0:DEPTH], sources,
                               preferred_element_type=jnp.float32)

            def add(part, terms, linked_only):
                total = None
                for k in range(WIDE):
                    term = terms[:, k * LANES:(k + 1) * LANES]
                    if mixed:
                        mark = held_marks[k]
                        keep = (lax.shift_right_logical(mark, top // TALL + 1) & 1) == 0
                        if linked_only:
                            keep = keep & ((mark & 1) == 1)
                        term = jnp.where(keep, term, 0.0)
                    total = term if total is None else total + term
                part[top:top + TALL, :] += total

            root = lax.rsqrt(product(0))
            inverse = root * root
            fourth = inverse * inverse
            add(shear_part, (product(1) * root) * fourth, False)
            if with_normal:
                add(normal_part, (product(2) * root) * fourth, True)
        return carry

    ends = (0, (far_linked + WIDE - 1) // WIDE, far_mixed // WIDE, far_all // WIDE)
    for kind, way in enumerate(((True, True), (True, False), (False, False))):
        lax.fori_loop(ends[kind], ends[kind + 1], functools.partial(far_step, *way), 0)

    if not last:
        return
    ones = jnp.ones((8, LANES), jnp.bfloat16)
    dims = (((1,), (1,)), ((), ()))
    sums = []
    for part in (shear_part, normal_part):
        first_sum, second_sum, third_sum = (
            lax.dot_general(ones, piece_of, dims, preferred_element_type=jnp.float32)[0:1, :]
            for piece_of in three_pieces(part[...]))
        sums.append(first_sum + (second_sum + third_sum))
    both = jnp.concatenate([jnp.where(own[9:10, :] > 0.0, one * own[9:10, :], 0.0) for one in sums]
                           + [jnp.zeros((14, per_block), jnp.float32)], axis=0)
    pieces = jnp.concatenate(three_pieces(both), axis=0)
    step = math.gcd(per_block, 256)
    slot = lax.broadcasted_iota(jnp.int32, (per_block, 1), 0).astype(jnp.float32)
    for at in range(0, per_block, step):
        pick = jnp.where(slot == own[10:11, at:at + step], 1.0, 0.0).astype(jnp.bfloat16)
        three = jnp.dot(pieces, pick, preferred_element_type=jnp.float32)
        back = three[0:16, :] + (three[16:32, :] + three[32:48, :])
        shear_ref[:, at:at + step] = back[0:1, :]
        normal_ref[:, at:at + step] = back[1:2, :]


def body(centroid, angles, size, slip_rate, live_count, near):
    per_block = centroid.shape[1]
    count_blocks = near.shape[1]
    smem = pl.BlockSpec(memory_space=pltpu.SMEM)
    vmem = pl.BlockSpec(memory_space=pltpu.VMEM)
    me = lax.axis_index("blocks").astype(jnp.int32).reshape(1)
    gap = jnp.zeros((1, per_block - count_blocks - 1), jnp.int32)
    links = jnp.concatenate([near, gap, live_count[None]], axis=1).astype(jnp.float32)
    given = jnp.concatenate([centroid, angles, size[None], slip_rate[None], links], axis=0)
    source, target = pl.pallas_call(
        functools.partial(prep_kernel, count_blocks),
        out_shape=(jax.ShapeDtypeStruct((8, per_block), jnp.float32),
                   jax.ShapeDtypeStruct((16, per_block), jnp.float32)),
        in_specs=[smem, vmem],
        out_specs=(vmem, vmem),
        compiler_params=pltpu.CompilerParams(vmem_limit_bytes=16 * 1024 * 1024),
    )(me, given)

    def stage(piece, first, earlier, last):
        held_blocks = piece.shape[0]
        total_chunks = held_blocks * per_block // LANES
        row = jax.ShapeDtypeStruct((1, per_block), jnp.float32)
        lanes = jax.ShapeDtypeStruct((per_block, LANES), jnp.float32)
        pieces = jax.ShapeDtypeStruct((3, per_block, LANES), jnp.bfloat16)
        pairs = per_block * per_block * held_blocks
        return pl.pallas_call(
            functools.partial(stage_kernel, first, last),
            out_shape=(row, row) if last else (lanes, lanes) if earlier else (lanes, lanes, pieces),
            in_specs=[vmem] * (3 + len(earlier)),
            out_specs=(vmem,) * (2 if earlier else 3),
            scratch_shapes=[
                pltpu.VMEM((FRAME, per_block, LANES), jnp.float32),
                pltpu.SMEM((total_chunks * (per_block // LANES) + 8,), jnp.int32),
                pltpu.SMEM((total_chunks + per_block // LANES + 2 * WIDE,), jnp.int32),
                pltpu.SMEM((total_chunks + per_block // LANES + 2 * WIDE,), jnp.int32),
                pltpu.SMEM((2,), jnp.int32),
                pltpu.VMEM((DEPTH, (total_chunks + 2 * WIDE) * LANES), jnp.bfloat16),
            ] + [pltpu.VMEM((per_block, LANES), jnp.float32)] * (2 if last else 0),
            compiler_params=pltpu.CompilerParams(vmem_limit_bytes=20 * 1024 * 1024),
            cost_estimate=pl.CostEstimate(flops=pairs * 2 * DEPTH * 4, bytes_accessed=pairs,
                                          transcendentals=pairs),
        )(source, piece, target, *earlier)

    def exchange(held, bit):
        return lax.ppermute(held, "blocks", [(one, one ^ bit) for one in range(count_blocks)])

    bits = exchanges(count_blocks)
    rounds = [[bits[1], bits[2], bits[1] | bits[2]]] + [[bit] for bit in bits[3:]]
    held = jnp.concatenate([source[None], exchange(source[None], bits[0])], axis=0)
    fresh, first, sums = held, 0, ()
    for offsets in rounds:
        coming = [exchange(held, bit) for bit in offsets]
        made = stage(fresh, first, sums, False)
        sums = made if not sums else (*made, sums[2])
        first = held.shape[0]
        fresh = jnp.concatenate(coming, axis=0) if len(coming) > 1 else coming[0]
        held = jnp.concatenate([held, fresh], axis=0)
    shear, normal = stage(fresh, first, sums, True)
    return shear.reshape(per_block), normal.reshape(per_block)


def solution(mesh):
    in_specs = (
        P(None, ("runs", "blocks")),
        P(None, ("runs", "blocks")),
        P(("runs", "blocks")),
        P(("runs", "blocks")),
        P(("runs", "blocks")),
        P(("runs", "blocks"), None),
    )
    out_specs = (P(("runs", "blocks")), P(("runs", "blocks")))
    return jax.shard_map(body, mesh=mesh, in_specs=in_specs, out_specs=out_specs, check_vma=False)
```

```python
import functools
import math

import jax
import jax.numpy as jnp
from jax import lax
from jax.experimental import pallas as pl
from jax.experimental.pallas import tpu as pltpu
from jax.sharding import PartitionSpec as P

coupling = 0.002
LANES = 128
FIELDS = 6
FRAME = 9
WIDE = 4
PAIRS = 2
TALL = 128
TURNS = 32
COUNT_LANE = 127
BIG = 1e15
SMALLEST = 2e-6
SPREAD_LIMIT = 1500.0
FEATURES = 16
SOURCE_PIECES = (0, 0, 1, 0, 2, 1)
TARGET_PIECES = (0, 1, 0, 2, 0, 1)
DEPTH = FEATURES * len(SOURCE_PIECES)


def exchanges(count_blocks):
    bits = [1 << at for at in range(count_blocks.bit_length() - 1)]
    return bits[:1] + bits[:0:-1]


def block_at(position, me, count_blocks):
    flipped = 0
    for at, bit in enumerate(exchanges(count_blocks)):
        flipped = flipped + ((position >> at) & 1) * bit
    return me ^ flipped


def three_pieces(value):
    first = value.astype(jnp.bfloat16)
    rest = value - first.astype(jnp.float32)
    second = rest.astype(jnp.bfloat16)
    third = (rest - second.astype(jnp.float32)).astype(jnp.bfloat16)
    return first, second, third


def ranks(key_row):
    per_block = key_row.shape[1]
    key_column = jnp.broadcast_to(key_row, (8, per_block)).T[:, 0:1]
    tile = (LANES, LANES)
    earlier = lax.broadcasted_iota(jnp.int32, tile, 0) < lax.broadcasted_iota(jnp.int32, tile, 1)

    def counted(before):
        return jnp.sum(jnp.where(before, 1.0, 0.0), axis=0, keepdims=True)

    total = jnp.zeros((1, per_block), jnp.float32)
    for top in range(0, per_block, LANES):
        other = key_column[top:top + LANES, :]
        end = top + LANES
        same = key_row[:, top:end]
        parts = [counted((other < same) | ((other == same) & earlier))]
        if top:
            parts.insert(0, counted(other < key_row[:, :top]))
        if end < per_block:
            parts.append(counted(other <= key_row[:, end:]))
        total = total + jnp.concatenate(parts, axis=1)
    return total


def prep_kernel(count_blocks, me_ref, given, source_ref, target_ref):
    per_block = given.shape[1]
    count = given[7:8, per_block - 1:per_block].astype(jnp.int32)
    strike, dip_angle, size, slip_rate = (given[row:row + 1, :] for row in range(3, 7))
    cos_p, sin_p = jnp.cos(strike), jnp.sin(strike)
    cos_q, sin_q = jnp.cos(dip_angle), jnp.sin(dip_angle)
    lane = lax.broadcasted_iota(jnp.int32, (1, per_block), 1)
    live = lane < count
    squared = size * size
    weight = slip_rate * squared
    place = [given[k:k + 1, :] for k in range(3)]

    extent = [jnp.max(jnp.where(live, row, -BIG), axis=1, keepdims=True)
              - jnp.min(jnp.where(live, row, BIG), axis=1, keepdims=True) for row in place]
    key = jnp.where((extent[0] >= extent[1]) & (extent[0] >= extent[2]), place[0],
                    jnp.where(extent[1] >= extent[2], place[1], place[2]))
    rank = ranks(jnp.where(live, key, BIG))
    rank_column = jnp.broadcast_to(rank, (8, per_block)).T[:, 0:1]

    zero = jnp.zeros((5, per_block), jnp.float32)
    rows = jnp.concatenate(place + [squared, weight * cos_p, weight * sin_p, cos_p, sin_p,
                                    -sin_q * sin_p, sin_q * cos_p, cos_q, zero], axis=0)
    pieces = jnp.concatenate(three_pieces(rows), axis=0)
    step = math.gcd(per_block, 256)
    parts = []
    for at in range(0, per_block, step):
        wanted = jnp.minimum(lax.broadcasted_iota(jnp.int32, (1, step), 1) + at, count - 1)
        pick = jnp.where(rank_column == wanted.astype(jnp.float32), 1.0, 0.0).astype(jnp.bfloat16)
        three = jnp.dot(pieces, pick, preferred_element_type=jnp.float32)
        parts.append(three[0:16, :] + (three[16:32, :] + three[32:48, :]))
    ordered = jnp.concatenate(parts, axis=1)

    source_ref[0:4, :] = ordered[0:4, :]
    source_ref[4:6, :] = jnp.where(live, ordered[4:6, :], 0.0)
    target_ref[0:4, :] = ordered[0:4, :]
    target_ref[4:9, :] = ordered[6:11, :]
    target_ref[9:10, :] = jnp.where(live, coupling, 0.0)
    target_ref[10:11, :] = rank
    links = jnp.broadcast_to(given[7:8, 0:LANES], (8, LANES)).T[:, 0:1]
    position = lax.broadcasted_iota(jnp.int32, (1, LANES), 1)
    number = lax.broadcasted_iota(jnp.int32, (LANES, 1), 0)
    links = jnp.sum(jnp.where(number == block_at(position, me_ref[0], count_blocks), links, 0.0),
                    axis=0, keepdims=True)
    target_ref[11:16, :] = zero
    target_ref[11:12, 0:LANES] = links

    turn = lax.broadcasted_iota(jnp.int32, (TURNS, 1), 0).astype(jnp.float32) * (math.pi / TURNS)
    along = jnp.cos(turn) * ordered[0:1, :] + jnp.sin(turn) * ordered[1:2, :]
    all_rows = jnp.concatenate([along, jnp.broadcast_to(ordered[2:3, :], (8, per_block))], axis=0)
    row = lax.broadcasted_iota(jnp.int32, (TURNS + 8, LANES), 0)
    column = lax.broadcasted_iota(jnp.int32, (TURNS + 8, LANES), 1)
    for lo in range(0, per_block, LANES):
        here = all_rows[:, lo:lo + LANES]
        used = live[:, lo:lo + LANES]
        for at, ends in ((6, jnp.min(jnp.where(used, here, BIG), axis=1, keepdims=True)),
                         (7, jnp.max(jnp.where(used, here, -BIG), axis=1, keepdims=True))):
            line = jnp.sum(jnp.where(row == column, ends, 0.0), axis=0, keepdims=True)
            line = jnp.where(column[0:1, :] == COUNT_LANE, count.astype(jnp.float32), line)
            source_ref[at:at + 1, lo:lo + LANES] = line


def pair_sums(columns, field):
    x, y, z, s2 = columns
    rx = x - field(0)
    ry = y - field(1)
    rz = z - field(2)
    d2 = (rx * rx + ry * ry) + (rz * rz + (s2 + field(3)))
    root = lax.rsqrt(d2)
    inverse = root * root
    cube = inverse * root
    ux, uy = field(4), field(5)
    bent = (cube * inverse) * (ux * rx + uy * ry)
    bent = 3.0 * bent
    return cube * ux - bent * rx, cube * uy - bent * ry, -bent * rz


def source_features(held, middle):
    x, y, z = (held[k:k + 1, :] - middle[k] for k in range(3))
    ux, uy = held[4:5, :], held[5:6, :]
    s = x * x + y * y + z * z + held[3:4, :]
    uxx, uxy, uxz, uyx, uyy, uyz = ux * x, ux * y, ux * z, uy * x, uy * y, uy * z
    along = uxx + uyy
    along3 = 3.0 * along
    return jnp.concatenate([
        jnp.ones_like(x), s, x, y, z, ux, uy, uxx, uxy, uxz, uyx, uyy, uyz,
        s * ux - along3 * x, s * uy - along3 * y, z * along], axis=0)


def target_features(held, middle, direction):
    x, y, z = (held[k:k + 1, :] - middle[k] for k in range(3))
    r = x * x + y * y + z * z + held[3:4, :]
    zero, one = jnp.zeros_like(x), jnp.ones_like(x)
    if direction is None:
        return jnp.concatenate([r, one, -2.0 * x, -2.0 * y, -2.0 * z] + [zero] * 11, axis=0)
    a, b, c = direction
    t3 = 3.0 * (a * x + b * y + c * z)
    return jnp.concatenate([
        zero, zero, zero, zero, zero, r * a - t3 * x, r * b - t3 * y,
        a * x + t3, 3.0 * b * x - 2.0 * a * y, 3.0 * c * x - 2.0 * a * z,
        3.0 * a * y - 2.0 * b * x, b * y + t3, 3.0 * c * y - 2.0 * b * z,
        a, b, -3.0 * c], axis=0)


def stage_kernel(first, last, source, piece, target, *rest):
    if last:
        rest, (shear_part, normal_part) = rest[:-2], rest[-2:]
    (columns, near_list, far_chunks, far_marks, counters, weights) = rest[-6:]
    rest = rest[:-6]
    starts = not rest[3:]
    if starts:
        earlier, (shear_part, normal_part, factors) = (), rest
    else:
        earlier, factors, outs = rest[:2], rest[2], rest[3:]
        if last:
            shear_ref, normal_ref = outs
        else:
            shear_part, normal_part = outs
    held_blocks = piece.shape[0]
    per_block = target.shape[1]
    per_chunks = per_block // LANES
    total_chunks = held_blocks * per_chunks

    def runs(ref, at):
        return jnp.concatenate([ref[at:at + 1, t * LANES:(t + 1) * LANES]
                                for t in range(per_chunks)], axis=0)

    low = jnp.concatenate([runs(piece.at[p], 6) for p in range(held_blocks)], axis=0)
    high = jnp.concatenate([runs(piece.at[p], 7) for p in range(held_blocks)], axis=0)
    own_low, own_high = runs(source, 6), runs(source, 7)
    lane = lax.broadcasted_iota(jnp.int32, (1, LANES), 1)
    center = 0.5 * (jnp.min(own_low, axis=0, keepdims=True)
                    + jnp.max(own_high, axis=0, keepdims=True))
    is_axis = (lane == 0) | (lane == TURNS // 2) | (lane == TURNS)

    def reach(low, high):
        out = jnp.maximum(jnp.abs(low - center), jnp.abs(high - center))
        return jnp.sqrt(jnp.sum(jnp.where(is_axis, out * out, 0.0), axis=1, keepdims=True))

    source_reach, own_reach = reach(low, high), reach(own_low, own_high)
    marks = jnp.zeros((total_chunks, 1), jnp.int32)
    for t in range(per_chunks):
        apart = jnp.maximum(low - own_high[t:t + 1, :], own_low[t:t + 1, :] - high)
        gap = jnp.max(jnp.where(lane <= TURNS, apart, 0.0), axis=1, keepdims=True)
        gap = jnp.maximum(gap, 0.0)
        both = source_reach + own_reach[t:t + 1, :]
        is_near = (gap * gap + SMALLEST) * SPREAD_LIMIT < both * both
        marks = marks + jnp.where(is_near, 1 << t, 0)
    middle = [center[0:1, k:k + 1] for k in (0, TURNS // 2, TURNS)]
    blocks = []
    for p in range(held_blocks):
        top = p * per_chunks
        held = marks[top:top + per_chunks, :]
        count = low[top, COUNT_LANE].astype(jnp.int32)
        blocks.append((held, jnp.max(held), (count + LANES - 1) // LANES,
                       target[11, first + p].astype(jnp.int32)))

    def pad(chunks, position):
        rest = lax.rem(WIDE - lax.rem(position, WIDE), WIDE)

        def put(at, carry):
            chunks[position + at] = total_chunks
            far_marks[position + at] = 0
            return carry

        lax.fori_loop(0, rest, put, 0)
        return position + rest

    counters[0] = 0
    counters[1] = 0
    def list_near(wanted):
        for p, (held, any_near, chunk_count, linked) in enumerate(blocks):
            @pl.when((any_near > 0) & (linked == wanted))
            def near_block(p=p, held=held, chunk_count=chunk_count):
                pairs, position = counters[0], counters[1]
                for t in range(per_chunks):
                    chunk = p * per_chunks + t
                    mark = jnp.where(t < chunk_count, held[t, 0], 0)
                    far_chunks[position + t] = chunk
                    far_marks[position + t] = mark * 2 + wanted
                    for run in range(per_chunks):
                        near_list[pairs] = (chunk * per_chunks + run) * 2 + wanted
                        pairs = pairs + (lax.shift_right_logical(mark, run) & 1)
                counters[0] = pairs
                counters[1] = position + chunk_count

    def list_blocks(wanted, start):
        position = start
        for p, (_, any_near, chunk_count, linked) in enumerate(blocks):
            here = jnp.where((any_near == 0) & (linked == wanted), chunk_count, 0)

            def put(at, carry, p=p, position=position):
                far_chunks[position + at] = p * per_chunks + at
                far_marks[position + at] = wanted
                return carry

            lax.fori_loop(0, here, put, 0)
            position = position + here
        return position

    list_near(1)
    far_linked = list_blocks(1, counters[1])
    counters[1] = far_linked
    list_near(0)
    far_mixed = pad(far_chunks, counters[1])
    far_all = pad(far_chunks, list_blocks(0, far_mixed))
    near_pairs = counters[0]
    for spare in range(PAIRS - 1):
        near_list[near_pairs + spare] = total_chunks * per_chunks * 2
    near_steps = (near_pairs + PAIRS - 1) // PAIRS

    def chunk_of(chunk):
        real = jnp.minimum(chunk, total_chunks - 1)
        lo = pl.multiple_of(lax.rem(real, per_chunks) * LANES, LANES)
        held = piece[real // per_chunks, :, pl.ds(lo, LANES)]
        row = lax.broadcasted_iota(jnp.int32, (8, LANES), 0)
        blank = jnp.where(row == 3, 1.0, 0.0)
        return jnp.where((row >= 3) & (chunk == total_chunks), blank, held)

    def place_far(at, carry):
        for k in range(WIDE):
            number = at * WIDE + k
            pieces = three_pieces(source_features(chunk_of(far_chunks[number]), middle))
            lo = pl.multiple_of(number * LANES, LANES)
            for slot, which in enumerate(SOURCE_PIECES):
                weights[slot * FEATURES:(slot + 1) * FEATURES, pl.ds(lo, LANES)] = pieces[which]
        return carry

    lax.fori_loop(0, far_all // WIDE, place_far, 0)

    own = target[...]
    if starts:
        zero_row = jnp.zeros((1, per_block), jnp.float32)
        ways = (None, (own[4:5], own[5:6], zero_row), (own[6:7], own[7:8], own[8:9]))
        for which, way in enumerate(ways):
            pieces = three_pieces(target_features(own, middle, way))
            stacked = jnp.concatenate(
                [pieces[k].astype(jnp.float32) for k in TARGET_PIECES]
                + [jnp.zeros((LANES - DEPTH, per_block), jnp.float32)], axis=0)
            factors[which, :, :] = stacked.T.astype(jnp.bfloat16)

    for at, part in enumerate((shear_part, normal_part)):
        part[...] = earlier[at][...] if earlier else jnp.zeros_like(part)

    @pl.when(near_pairs > 0)
    def spread_columns():
        turned = own.T
        for row in range(FRAME):
            columns[row, :, :] = jnp.broadcast_to(turned[:, row:row + 1], (per_block, LANES))

    def near_step(at, carry):
        work = []
        for k in range(PAIRS):
            code = near_list[at * PAIRS + k]
            chunk = lax.shift_right_logical(code, 1) // per_chunks
            held = chunk_of(chunk)
            fields = [jnp.broadcast_to(held[row:row + 1, :], (8, LANES)) for row in range(FIELDS)]
            run = lax.shift_right_logical(code, 1) & (per_chunks - 1)
            work.append(((code & 1) == 1, run, fields))
        for sub in range(LANES // 8):
            for linked, run, fields in work:
                rows = pl.ds(pl.multiple_of(run * LANES + 8 * sub, 8), 8)
                x, y, z, s2, tx, ty, nx, ny, nz = (columns[row, rows, :] for row in range(FRAME))
                fx, fy, fz = pair_sums((x, y, z, s2), fields.__getitem__)
                shear_part[rows, :] += tx * fx + ty * fy
                normal_part[rows, :] += jnp.where(linked, nx * fx + ny * fy + nz * fz, 0.0)
        return carry

    lax.fori_loop(0, near_steps, near_step, 0)

    def far_step(mixed, with_normal, at, carry):
        lo = pl.multiple_of(at * WIDE * LANES, WIDE * LANES)
        sources = weights[:, pl.ds(lo, WIDE * LANES)]

        held_marks = [far_marks[at * WIDE + k] for k in range(WIDE)] if mixed else None
        for top in range(0, per_block, TALL):
            def product(which):
                return jnp.dot(factors[which, top:top + TALL, 0:DEPTH], sources,
                               preferred_element_type=jnp.float32)

            def add(part, terms, linked_only):
                total = None
                for k in range(WIDE):
                    term = terms[:, k * LANES:(k + 1) * LANES]
                    if mixed:
                        mark = held_marks[k]
                        keep = (lax.shift_right_logical(mark, top // TALL + 1) & 1) == 0
                        if linked_only:
                            keep = keep & ((mark & 1) == 1)
                        term = jnp.where(keep, term, 0.0)
                    total = term if total is None else total + term
                part[top:top + TALL, :] += total

            root = lax.rsqrt(product(0))
            inverse = root * root
            fourth = inverse * inverse
            add(shear_part, (product(1) * root) * fourth, False)
            if with_normal:
                add(normal_part, (product(2) * root) * fourth, True)
        return carry

    ends = (0, (far_linked + WIDE - 1) // WIDE, far_mixed // WIDE, far_all // WIDE)
    for kind, way in enumerate(((True, True), (True, False), (False, False))):
        lax.fori_loop(ends[kind], ends[kind + 1], functools.partial(far_step, *way), 0)

    if not last:
        return
    ones = jnp.ones((8, LANES), jnp.bfloat16)
    dims = (((1,), (1,)), ((), ()))
    sums = []
    for part in (shear_part, normal_part):
        first_sum, second_sum, third_sum = (
            lax.dot_general(ones, piece_of, dims, preferred_element_type=jnp.float32)[0:1, :]
            for piece_of in three_pieces(part[...]))
        sums.append(first_sum + (second_sum + third_sum))
    both = jnp.concatenate([jnp.where(own[9:10, :] > 0.0, one * own[9:10, :], 0.0) for one in sums]
                           + [jnp.zeros((14, per_block), jnp.float32)], axis=0)
    pieces = jnp.concatenate(three_pieces(both), axis=0)
    step = math.gcd(per_block, 256)
    slot = lax.broadcasted_iota(jnp.int32, (per_block, 1), 0).astype(jnp.float32)
    for at in range(0, per_block, step):
        pick = jnp.where(slot == own[10:11, at:at + step], 1.0, 0.0).astype(jnp.bfloat16)
        three = jnp.dot(pieces, pick, preferred_element_type=jnp.float32)
        back = three[0:16, :] + (three[16:32, :] + three[32:48, :])
        shear_ref[:, at:at + step] = back[0:1, :]
        normal_ref[:, at:at + step] = back[1:2, :]


def body(centroid, angles, size, slip_rate, live_count, near):
    per_block = centroid.shape[1]
    count_blocks = near.shape[1]
    smem = pl.BlockSpec(memory_space=pltpu.SMEM)
    vmem = pl.BlockSpec(memory_space=pltpu.VMEM)
    me = lax.axis_index("blocks").astype(jnp.int32).reshape(1)
    gap = jnp.zeros((1, per_block - count_blocks - 1), jnp.int32)
    links = jnp.concatenate([near, gap, live_count[None]], axis=1).astype(jnp.float32)
    given = jnp.concatenate([centroid, angles, size[None], slip_rate[None], links], axis=0)
    source, target = pl.pallas_call(
        functools.partial(prep_kernel, count_blocks),
        out_shape=(jax.ShapeDtypeStruct((8, per_block), jnp.float32),
                   jax.ShapeDtypeStruct((16, per_block), jnp.float32)),
        in_specs=[smem, vmem],
        out_specs=(vmem, vmem),
        compiler_params=pltpu.CompilerParams(vmem_limit_bytes=16 * 1024 * 1024),
    )(me, given)

    def stage(piece, first, earlier, last):
        held_blocks = piece.shape[0]
        total_chunks = held_blocks * per_block // LANES
        row = jax.ShapeDtypeStruct((1, per_block), jnp.float32)
        lanes = jax.ShapeDtypeStruct((per_block, LANES), jnp.float32)
        pieces = jax.ShapeDtypeStruct((3, per_block, LANES), jnp.bfloat16)
        pairs = per_block * per_block * held_blocks
        return pl.pallas_call(
            functools.partial(stage_kernel, first, last),
            out_shape=(row, row) if last else (lanes, lanes) if earlier else (lanes, lanes, pieces),
            in_specs=[vmem] * (3 + len(earlier)),
            out_specs=(vmem,) * (2 if earlier else 3),
            scratch_shapes=[
                pltpu.VMEM((FRAME, per_block, LANES), jnp.float32),
                pltpu.SMEM((total_chunks * (per_block // LANES) + 8,), jnp.int32),
                pltpu.SMEM((total_chunks + per_block // LANES + 2 * WIDE,), jnp.int32),
                pltpu.SMEM((total_chunks + per_block // LANES + 2 * WIDE,), jnp.int32),
                pltpu.SMEM((2,), jnp.int32),
                pltpu.VMEM((DEPTH, (total_chunks + 2 * WIDE) * LANES), jnp.bfloat16),
            ] + [pltpu.VMEM((per_block, LANES), jnp.float32)] * (2 if last else 0),
            compiler_params=pltpu.CompilerParams(vmem_limit_bytes=20 * 1024 * 1024),
            cost_estimate=pl.CostEstimate(flops=pairs * 2 * DEPTH * 4, bytes_accessed=pairs,
                                          transcendentals=pairs),
        )(source, piece, target, *earlier)

    def exchange(held, bit):
        return lax.ppermute(held, "blocks", [(one, one ^ bit) for one in range(count_blocks)])

    bits = exchanges(count_blocks)
    rounds = [[bits[1], bits[2], bits[1] | bits[2]]] + [[bit] for bit in bits[3:]]
    held = jnp.concatenate([source[None], exchange(source[None], bits[0])], axis=0)
    fresh, first, sums = held, 0, ()
    for offsets in rounds:
        coming = [exchange(held, bit) for bit in offsets]
        made = stage(fresh, first, sums, False)
        sums = made if not sums else (*made, sums[2])
        first = held.shape[0]
        fresh = jnp.concatenate(coming, axis=0) if len(coming) > 1 else coming[0]
        held = jnp.concatenate([held, fresh], axis=0)
    shear, normal = stage(fresh, first, sums, True)
    return shear.reshape(per_block), normal.reshape(per_block)


def solution(mesh):
    in_specs = (
        P(None, ("runs", "blocks")),
        P(None, ("runs", "blocks")),
        P(("runs", "blocks")),
        P(("runs", "blocks")),
        P(("runs", "blocks")),
        P(("runs", "blocks"), None),
    )
    out_specs = (P(("runs", "blocks")), P(("runs", "blocks")))
    return jax.shard_map(body, mesh=mesh, in_specs=in_specs, out_specs=out_specs, check_vma=False)
```
